32 devices in a mesh: pts: 8 (over z, y), fsdp: 4 (over x, core).
Axes of the slice: x: 2, y: 2, z: 4, core: 2. Of those that a mesh axis runs over, the one named last changes fastest.
Arguments:
- points: bfloat16 [65536, 256], P(('pts', 'fsdp')), may hold values from -6 to 6
- cotangent: bfloat16 [65536, 256], P(('pts', 'fsdp')), may hold values from -6 to 6
- surface_count: int32 [32, 16], P(('pts', 'fsdp')), may hold values from 8 to 16, as said below
- volume_count: int32 [32, 16], P(('pts', 'fsdp')), may hold values from 28 to 112, as said below
- attn_weight: float32 [3, 256, 256], P(None, 'fsdp')
- attn_first: float32 [3, 256, 256], P(None, 'fsdp'), may hold values from -0.015625 to 0.015625
- attn_second: float32 [3, 256, 256], P(None, 'fsdp'), may hold values from 6.879623e-07 to 5.5036985e-06
- attn_average: float32 [3, 256, 256], P(None, 'fsdp'), may hold values from -1 to 1
- mlp_weight: float32 [2, 256, 1024], P(None, 'fsdp')
- mlp_first: float32 [2, 256, 1024], P(None, 'fsdp'), may hold values from -0.015625 to 0.015625
- mlp_second: float32 [2, 256, 1024], P(None, 'fsdp'), may hold values from 6.879623e-07 to 5.5036985e-06
- mlp_average: float32 [2, 256, 1024], P(None, 'fsdp'), may hold values from -1 to 1
- small_weight: float32 [32, 160], replicated
- small_first: float32 [32, 160], replicated, may hold values from -0.015625 to 0.015625
- small_second: float32 [32, 160], replicated, may hold values from 6.879623e-07 to 5.5036985e-06
- small_average: float32 [32, 160], replicated, may hold values from -2.5 to 2.5
- vector_params: float32 [3, 256], replicated
- vector_first: float32 [3, 256], replicated, may hold values from -0.015625 to 0.015625
- vector_second: float32 [3, 256], replicated, may hold values from 6.879623e-07 to 5.5036985e-06
- vector_average: float32 [3, 256], replicated, may hold values from 0.5 to 1.5
Outputs:
- mixed: bfloat16 [65536, 256], P(('pts', 'fsdp'))
- points_grad: float32 [65536, 256], P(('pts', 'fsdp'))
- grad_norm: float32 [], replicated
- attn_new: float32 [3, 256, 256], P(None, 'fsdp')
- attn_first_new: float32 [3, 256, 256], P(None, 'fsdp')
- attn_second_new: float32 [3, 256, 256], P(None, 'fsdp')
- attn_average_new: float32 [3, 256, 256], P(None, 'fsdp')
- attn_copy: bfloat16 [3, 256, 256], P(None, 'fsdp')
- mlp_new: float32 [2, 256, 1024], P(None, 'fsdp')
- mlp_first_new: float32 [2, 256, 1024], P(None, 'fsdp')
- mlp_second_new: float32 [2, 256, 1024], P(None, 'fsdp')
- mlp_average_new: float32 [2, 256, 1024], P(None, 'fsdp')
- mlp_copy: bfloat16 [2, 256, 1024], P(None, 'fsdp')
- small_new: float32 [32, 160], replicated
- small_first_new: float32 [32, 160], replicated
- small_second_new: float32 [32, 160], replicated
- small_average_new: float32 [32, 160], replicated
- small_copy: bfloat16 [32, 160], replicated
- vector_new: float32 [3, 256], replicated
- vector_first_new: float32 [3, 256], replicated
- vector_second_new: float32 [3, 256], replicated
- vector_average_new: float32 [3, 256], replicated
- vector_copy: bfloat16 [3, 256], replicated
The draws below stay inside these ranges and needn't reach their ends.
Inputs may be any that keep to these rules, and one draw needn't show every extreme that they name: `surface_count`: some device holds 16 surface points of every item. `volume_count`: some device holds 112 volume points of every item.
All inputs are finite; a program needn't handle non-finite values.
Results may differ from the reference program's by a relative error of at most 0.02.
Values may be sent and summed in bfloat16 or wider, within the bound.
A program may use at most 256 MiB of HBM per device.

```python
import math
import jax
import jax.numpy as jnp
from jax import lax

C = 256
H = 8
DH = 32
G = 64
FF = 1024
TOK_DEV = 2048
ITEMS = 16
STEP = 5
TOKENS = 65536
SURF_MAX = 16
VOL_MAX = 112
PARAMS = 726784
DEVICES = 32


def draw_surface_count(key, part):
    key = jax.random.fold_in(key, 11)
    lowest = max(1, SURF_MAX // 2)
    counts = jax.random.randint(key, (DEVICES, ITEMS), lowest, SURF_MAX + 1)
    chosen = jax.random.randint(jax.random.fold_in(key, 5), (), 0, DEVICES)
    device_rows = jnp.arange(DEVICES)[:, None]
    return jnp.where(device_rows == chosen, SURF_MAX, counts).astype(jnp.int32)


def draw_volume_count(key, part):
    key = jax.random.fold_in(key, 13)
    lowest = VOL_MAX // 4
    counts = jax.random.randint(key, (DEVICES, ITEMS), lowest, VOL_MAX + 1)
    chosen = jax.random.randint(jax.random.fold_in(key, 7), (), 0, DEVICES)
    device_rows = jnp.arange(DEVICES)[:, None]
    return jnp.where(device_rows == chosen, VOL_MAX, counts).astype(jnp.int32)


def draw_attn_weight(key, part):
    key = jax.random.fold_in(key, 21)
    base = jax.random.normal(key, (3, C, C), jnp.float32)
    factor = jnp.where(jnp.arange(3) == 2, 3.0, 1.0).astype(jnp.float32)[:, None, None]
    return base * factor * C ** (-0.5)


def draw_mlp_weight(key, part):
    key = jax.random.fold_in(key, 23)
    base = jax.random.normal(key, (2, C, FF), jnp.float32)
    factor = jnp.where(jnp.arange(2) == 0, C ** (-0.5), FF ** (-0.5)).astype(jnp.float32)[:, None, None]
    return base * factor


def draw_small_weight(key, part):
    key = jax.random.fold_in(key, 29)
    base = jax.random.normal(key, (DH, G + 3 * DH), jnp.float32)
    columns = jnp.arange(G + 3 * DH)
    factor = jnp.where(columns < G, 2.0, jnp.where(columns < G + 2 * DH, 6.0, 4.0)).astype(jnp.float32)
    return base * factor[None, :] * DH ** (-0.5)


def draw_vector_params(key, part):
    key = jax.random.fold_in(key, 31)
    ramp = 0.6 + 1.2 * jnp.arange(C).astype(jnp.float32) / (C - 1)
    jitter = jax.random.uniform(key, (2, C), jnp.float32, 0.8, 1.2)
    embed = 0.5 * jax.random.normal(jax.random.fold_in(key, 3), (1, C), jnp.float32)
    return jnp.concatenate([ramp[None, :] * jitter, embed], axis=0)


def levels(key, extent, cuts, smallest, largest):
    level, own = 1.0, jax.random.fold_in(key, 6)
    for dim, parts in cuts:
        draws = jnp.exp(jax.random.uniform(jax.random.fold_in(own, dim), (parts,), jnp.float32, smallest / len(cuts), largest / len(cuts)))
        level = level * jnp.repeat(draws, extent[dim] // parts).reshape([-1 if axis == dim else 1 for axis in range(len(extent))])
    return level


def gaussian(own_key, extent, deviation, limit, pieces=(), kind=jnp.bfloat16):
    factor_of = levels(own_key, extent, pieces, -0.22, 0.18) if pieces else 1.0
    drawn = jax.random.normal(own_key, extent, jnp.float32) * deviation * factor_of
    return jnp.minimum(jnp.maximum(drawn, -limit), limit).astype(kind)


def setup_inputs(seed: int = 0) -> dict:
    key_list = jax.random.split(jax.random.key(seed), 21)
    points = gaussian(key_list[0], (TOKENS, C), 1.0, 6.0, ((0, 32),))
    cotangent = gaussian(key_list[1], (TOKENS, C), 1.0, 6.0, ((0, 32),))
    surface_count = draw_surface_count(jax.random.fold_in(key_list[20], 71), 0)
    volume_count = draw_volume_count(jax.random.fold_in(key_list[20], 71), 0)
    attn_weight = draw_attn_weight(jax.random.fold_in(key_list[20], 71), 0)
    attn_first = gaussian(key_list[5], (3, C, C), (PARAMS ** -0.5), 0.015625, ((1, 4),), jnp.float32)
    attn_second = jnp.clip(jnp.exp(math.log(5.503698503162013e-06) - 2.0794415 * jax.random.uniform(key_list[6], (3, C, C), jnp.float32) ** levels(key_list[6], (3, C, C), ((1, 4),), -0.2, 0.2)), 6.879623128952517e-07, 5.503698503162013e-06)
    attn_average = gaussian(key_list[7], (3, C, C), (C ** -0.5), 1.0, ((1, 4),), jnp.float32)
    mlp_weight = draw_mlp_weight(jax.random.fold_in(key_list[20], 71), 0)
    mlp_first = gaussian(key_list[9], (2, C, FF), (PARAMS ** -0.5), 0.015625, ((1, 4),), jnp.float32)
    mlp_second = jnp.clip(jnp.exp(math.log(5.503698503162013e-06) - 2.0794415 * jax.random.uniform(key_list[10], (2, C, FF), jnp.float32) ** levels(key_list[10], (2, C, FF), ((1, 4),), -0.2, 0.2)), 6.879623128952517e-07, 5.503698503162013e-06)
    mlp_average = gaussian(key_list[11], (2, C, FF), (C ** -0.5), 1.0, ((1, 4),), jnp.float32)
    small_weight = draw_small_weight(jax.random.fold_in(key_list[20], 71), 0)
    small_first = gaussian(key_list[13], (DH, G + 3 * DH), (PARAMS ** -0.5), 0.015625, (), jnp.float32)
    small_second = jnp.clip(jnp.exp(jax.random.uniform(key_list[14], (DH, G + 3 * DH), jnp.float32, math.log(6.879623128952517e-07), math.log(5.503698503162013e-06))), 6.879623128952517e-07, 5.503698503162013e-06)
    small_average = gaussian(key_list[15], (DH, G + 3 * DH), (DH ** -0.5), 2.5, (), jnp.float32)
    vector_params = draw_vector_params(jax.random.fold_in(key_list[20], 71), 0)
    vector_first = gaussian(key_list[17], (3, C), (PARAMS ** -0.5), 0.015625, (), jnp.float32)
    vector_second = jnp.clip(jnp.exp(jax.random.uniform(key_list[18], (3, C), jnp.float32, math.log(6.879623128952517e-07), math.log(5.503698503162013e-06))), 6.879623128952517e-07, 5.503698503162013e-06)
    vector_average = jnp.clip(1.0 + 0.1 * jax.random.normal(key_list[19], (3, C), jnp.float32), 0.5, 1.5)
    return {"points": points, "cotangent": cotangent, "surface_count": surface_count, "volume_count": volume_count, "attn_weight": attn_weight, "attn_first": attn_first, "attn_second": attn_second, "attn_average": attn_average, "mlp_weight": mlp_weight, "mlp_first": mlp_first, "mlp_second": mlp_second, "mlp_average": mlp_average, "small_weight": small_weight, "small_first": small_first, "small_second": small_second, "small_average": small_average, "vector_params": vector_params, "vector_first": vector_first, "vector_second": vector_second, "vector_average": vector_average}


HIGH = lax.Precision.HIGHEST
NORM_EPS = 1e-05
SLICE_EPS = 1e-05
CLIP = 1.0
BETA_ONE = 0.5
BETA_TWO = 0.5
ADAM_EPS = 1e-08
DECAY = 0.01
EMA_RATE = 0.6
RATE_ATTN = 0.04
RATE_MLP = 0.03
RATE_SMALL = 0.4
RATE_VECTOR = 0.3

@jax.custom_vjp
def low(v):
    return lax.optimization_barrier(v.astype(jnp.bfloat16)).astype(jnp.float32)

@jax.custom_vjp
def low_back(v):
    return v

def low_keep(v):
    return (low(v), None)

def low_pass(kept, grad):
    return (grad,)

def back_keep(v):
    return (v, None)

def back_low(kept, grad):
    return (low(grad),)
low.defvjp(low_keep, low_pass)
low_back.defvjp(back_keep, back_low)

def layout(surface_count, volume_count, rows):
    counted = surface_count + volume_count
    ends = jnp.cumsum(counted, axis=1).astype(jnp.int32)
    starts = (ends - counted).astype(jnp.int32)
    position = jnp.arange(rows, dtype=jnp.int32)[None, :, None]
    inside = (position >= starts[:, None, :]) & (position < ends[:, None, :])
    surface_end = (starts + surface_count).astype(jnp.int32)[:, None, :]
    onehot = inside.astype(jnp.float32)
    surface = lax.optimization_barrier(jnp.sum((inside & (position < surface_end)).astype(jnp.float32), axis=2))
    return (onehot, surface)

def layer_norm(field, gain):
    row_mean = lax.optimization_barrier(jnp.mean(field, axis=-1, keepdims=True))
    centred = field - row_mean
    row_var = lax.optimization_barrier(jnp.mean(centred * centred, axis=-1, keepdims=True))
    return centred * lax.rsqrt(row_var + NORM_EPS) * gain

def slice_attention(sums, totals, small):
    tokens_slice = sums / (totals[..., None] + SLICE_EPS)
    queries = jnp.einsum('bhgd,de->bhge', tokens_slice, small[:, G:G + DH], precision=HIGH)
    key_rows = jnp.einsum('bhgd,de->bhge', tokens_slice, small[:, G + DH:G + 2 * DH], precision=HIGH)
    value_rows = jnp.einsum('bhgd,de->bhge', tokens_slice, small[:, G + 2 * DH:], precision=HIGH)
    scores = jnp.einsum('bhge,bhke->bhgk', queries, key_rows, precision=HIGH) / math.sqrt(DH)
    weights = jax.nn.softmax(scores, axis=-1)
    return jnp.einsum('bhgk,bhke->bhge', weights, value_rows, precision=HIGH)

def adamw(weight, first, second, average, grad, factor, rate):
    clipped = grad * factor
    first_new = BETA_ONE * first + (1.0 - BETA_ONE) * clipped
    second_new = BETA_TWO * second + (1.0 - BETA_TWO) * clipped * clipped
    first_hat = first_new / (1.0 - BETA_ONE ** STEP)
    second_hat = second_new / (1.0 - BETA_TWO ** STEP)
    new_weight = weight - rate * (first_hat / (jnp.sqrt(second_hat) + ADAM_EPS) + DECAY * weight)
    average_new = EMA_RATE * average + (1.0 - EMA_RATE) * new_weight
    return (new_weight, first_new, second_new, average_new, new_weight.astype(jnp.bfloat16))

def forward(points, attn_weight, mlp_weight, small_weight, vector_params, onehot, surface):
    devices, rows, items = onehot.shape
    width = points.shape[1]
    start = points + surface.reshape(-1, 1) * vector_params[2]
    normed = low(layer_norm(start, vector_params[0]))
    weight_x = low(attn_weight[0])
    weight_f = low(attn_weight[1])
    weight_o = low(attn_weight[2])
    weight_in = low(mlp_weight[0])
    weight_out = low(mlp_weight[1])
    weight_slice = low(small_weight[:, :G])
    mid_x = low_back(low(jnp.dot(normed, weight_x, precision=HIGH)))
    mid_f = low_back(low(jnp.dot(normed, weight_f, precision=HIGH)))
    logits = low_back(jnp.dot(mid_x.reshape(-1, DH), weight_slice, precision=HIGH))
    slice_prob = low(jax.nn.softmax(logits.reshape(-1, H, G), axis=-1)).reshape(devices, rows, H, G)
    features = mid_f.reshape(devices, rows, H, DH)

    def collect(block):
        select, probs, fields = block
        masked = select[:, :, None, None] * probs[:, None, :, :]
        return (jnp.einsum('nbhg,nhd->bhgd', masked, fields, precision=HIGH), lax.optimization_barrier(jnp.sum(masked, axis=0)))
    part_sums, part_totals = lax.map(jax.checkpoint(collect), (onehot, slice_prob, features))
    slice_sum = low_back(lax.optimization_barrier(jnp.sum(part_sums, axis=0)))
    slice_total = lax.optimization_barrier(jnp.sum(part_totals, axis=0))
    slice_out = low(slice_attention(slice_sum, slice_total, small_weight))

    def spread(block):
        select, probs = block
        masked = select[:, :, None, None] * probs[:, None, :, :]
        return jnp.einsum('nbhg,bhgd->nhd', masked, slice_out, precision=HIGH)
    spread_out = lax.map(jax.checkpoint(spread), (onehot, slice_prob))
    mixed_heads = low_back(low(spread_out.reshape(-1, width)))
    branch = low_back(jnp.dot(mixed_heads, weight_o, precision=HIGH))
    middle = start + branch

    def feed(block):
        normed_two = low(layer_norm(block, vector_params[1]))
        hidden = low_back(jnp.dot(normed_two, weight_in, precision=HIGH))
        active = low(jax.nn.gelu(hidden))
        return jnp.dot(active, weight_out.T, precision=HIGH)
    update = lax.map(jax.checkpoint(feed), middle.reshape(devices, rows, width))
    return middle + update.reshape(-1, width)

def reference(points, cotangent, surface_count, volume_count, attn_weight, attn_first, attn_second, attn_average, mlp_weight, mlp_first, mlp_second, mlp_average, small_weight, small_first, small_second, small_average, vector_params, vector_first, vector_second, vector_average):
    onehot, surface = layout(surface_count, volume_count, TOK_DEV)

    def whole(field, attn, mlp, small, vector):
        return forward(field, attn, mlp, small, vector, onehot, surface)
    result, pull = jax.vjp(whole, points.astype(jnp.float32), attn_weight, mlp_weight, small_weight, vector_params)
    grad_points, grad_attn, grad_mlp, grad_small, grad_vector = pull(cotangent.astype(jnp.float32))
    squares = jnp.sum(grad_attn * grad_attn) + jnp.sum(grad_mlp * grad_mlp) + jnp.sum(grad_small * grad_small) + jnp.sum(grad_vector * grad_vector)
    grad_norm = jnp.sqrt(squares)
    factor = jnp.minimum(1.0, CLIP / grad_norm)
    attn_state = adamw(attn_weight, attn_first, attn_second, attn_average, grad_attn, factor, RATE_ATTN)
    mlp_state = adamw(mlp_weight, mlp_first, mlp_second, mlp_average, grad_mlp, factor, RATE_MLP)
    small_state = adamw(small_weight, small_first, small_second, small_average, grad_small, factor, RATE_SMALL)
    vector_state = adamw(vector_params, vector_first, vector_second, vector_average, grad_vector, factor, RATE_VECTOR)
    return (result.astype(jnp.bfloat16), grad_points, grad_norm, attn_state[0], attn_state[1], attn_state[2], attn_state[3], attn_state[4], mlp_state[0], mlp_state[1], mlp_state[2], mlp_state[3], mlp_state[4], small_state[0], small_state[1], small_state[2], small_state[3], small_state[4], vector_state[0], vector_state[1], vector_state[2], vector_state[3], vector_state[4])
```

```python
import functools
import math

import jax
import jax.numpy as jnp
from jax import lax
from jax.experimental import pallas as pl
from jax.experimental.pallas import tpu as pltpu
from jax.sharding import PartitionSpec as P

C = 256
H = 8
DH = 32
G = 64
FF = 1024
ITEMS = 16
STEP = 5
W = 256
NORM_EPS = 1e-05
SLICE_EPS = 1e-05
CLIP = 1.0
BETA_ONE = 0.5
BETA_TWO = 0.5
ADAM_EPS = 1e-08
DECAY = 0.01
EMA_RATE = 0.6
RATE_ATTN = 0.04
RATE_MLP = 0.03
RATE_SMALL = 0.4
RATE_VECTOR = 0.3
ZO = 4
CH = 80
CB = 144
CL = 32
SM = 80
MESH = pl.DeviceIdType.MESH
HIGH = lax.Precision.HIGHEST
F32 = jnp.float32
BF = jnp.bfloat16
GELU_A = math.sqrt(2.0 / math.pi)
GELU_B = GELU_A * 0.044715


def nn(a, b, precision=None):
    return lax.dot_general(a, b, (((1,), (0,)), ((), ())), precision=precision, preferred_element_type=F32)


def nt(a, b, precision=None):
    return lax.dot_general(a, b, (((1,), (1,)), ((), ())), precision=precision, preferred_element_type=F32)


def tn(a, b, precision=None):
    return lax.dot_general(a, b, (((0,), (0,)), ((), ())), precision=precision, preferred_element_type=F32)


def iota(shape, dim):
    return lax.broadcasted_iota(jnp.int32, shape, dim)


def tile_of(i, width=W):
    return pl.ds(pl.multiple_of(i * width, width), width)


class Place:
    def __init__(self, zs):
        self.p = lax.axis_index("pts")
        self.f = lax.axis_index("fsdp")
        self.a = self.f % 2
        self.x = self.f // 2
        self.y = self.p % 2
        self.z = self.p // 2
        self.m = self.x * 2 + self.y
        self.zs = zs
        self.core = (self.p, self.f + 1 - 2 * self.a)
        self.xpeer = (self.p, (1 - self.x) * 2 + self.a)
        self.ypeer = (self.z * 2 + 1 - self.y, self.f)
        self.zown = self.z if zs == ZO else jnp.minimum(self.z, ZO - 1)

    def xy(self, k):
        mm = (self.m + k) % 4
        return mm, (self.z * 2 + mm % 2, (mm // 2) * 2 + self.a)

    def xy_other(self, k):
        mm = (self.m + k) % 4
        return mm, (self.z * 2 + mm % 2, (mm // 2) * 2 + 1 - self.a)

    def zl(self, k):
        zz = (self.z + k) % self.zs
        return zz, (zz * 2 + self.y, self.f)

    def barrier(self, crossed=False):
        b = pltpu.get_barrier_semaphore()
        peers = [self.core] + [self.xy(k)[1] for k in (1, 2, 3)] + [self.zl(k)[1] for k in range(1, self.zs)]
        if crossed:
            peers += [self.xy_other(k)[1] for k in (1, 2, 3)]
        for d in peers:
            pl.semaphore_signal(b, inc=1, device_id=d, device_id_type=MESH)
        pl.semaphore_wait(b, len(peers))

    def owned(self, z, fn):
        if self.zs == ZO:
            fn()
        else:
            pl.when(z < ZO)(fn)


def rcopy(src, dst, ss, rs, dev):
    return pltpu.make_async_remote_copy(
        src_ref=src, dst_ref=dst, send_sem=ss, recv_sem=rs, device_id=dev, device_id_type=MESH
    )


class Reduce:
    def __init__(self, g, src, bufs):
        self.g, self.src = g, src
        self.r1, self.s2, self.r2, self.s3, self.r3, self.sem = bufs
        self.c1, self.c2, self.c3 = {}, [], []

    @staticmethod
    def scratch(rows, zs):
        return [
            pltpu.VMEM((4, ZO, rows, 128), BF),
            pltpu.VMEM((3, ZO, rows, 128), BF),
            pltpu.VMEM((3, ZO, rows, 128), BF),
            pltpu.VMEM((ZO, rows, 128), BF),
            pltpu.VMEM((zs - 1, rows, 128), BF),
            pltpu.SemaphoreType.DMA((6, max(zs, 4))),
        ]

    def core(self, k):
        g = self.g
        mm = (g.m + k) % 4
        c = rcopy(self.src.at[1 - g.a, mm], self.r1.at[mm], self.sem.at[0, k], self.sem.at[1, k], g.core)
        c.start()
        self.c1[k] = c

    def pair(self, k):
        g = self.g
        self.c1[k].wait_recv()
        mm = (g.m + k) % 4
        return self.src[g.a, mm].astype(F32) + self.r1[mm].astype(F32)

    def square(self, k):
        g = self.g
        dev = g.xy(k)[1]
        self.s2[k - 1] = self.pair(k).astype(BF)
        c = rcopy(self.s2.at[k - 1], self.r2.at[k - 1], self.sem.at[2, k - 1], self.sem.at[3, k - 1], dev)
        c.start()
        self.c2.append(c)

    def line(self):
        g = self.g
        acc = self.pair(0)
        for k in (1, 2, 3):
            self.c2[k - 1].wait_recv()
            acc = acc + self.r2[k - 1].astype(F32)
        self.s3[...] = acc.astype(BF)
        for k in range(1, g.zs):
            zz, dev = g.zl(k)
            at = zz if g.zs == ZO else jnp.minimum(zz, ZO - 1)
            c = rcopy(self.s3.at[at], self.r3.at[k - 1], self.sem.at[4, k - 1], self.sem.at[5, k - 1], dev)
            g.owned(zz, c.start)
            self.c3.append(c)

    def result(self):
        g = self.g
        out = self.s3[g.zown].astype(F32)
        for k in range(1, g.zs):
            g.owned(g.z, self.c3[k - 1].wait_recv)
            out = out + self.r3[k - 1].astype(F32)
        return out

    def finish(self):
        g = self.g
        for c in self.c1.values():
            c.wait_send()
        for c in self.c2:
            c.wait_send()
        for k in range(1, g.zs):
            g.owned(g.zl(k)[0], self.c3[k - 1].wait_send)


class Gather:
    def __init__(self, g, out, sem):
        self.g, self.out, self.sem = g, out, sem
        self.cz, self.cxy, self.cc = [], {}, []

    @staticmethod
    def scratch(zs):
        return [pltpu.SemaphoreType.DMA((6, 4, max(zs, 4)))]

    def start(self):
        g = self.g
        own = self.out.at[g.a, g.m, g.zown]
        for k in range(1, g.zs):
            c = rcopy(own, own, self.sem.at[0, 0, k], self.sem.at[1, 0, k], g.zl(k)[1])
            g.owned(g.z, c.start)
            self.cz.append(c)
        self.fan(g.z, 0)

    def fan(self, z, k):
        g = self.g
        at = z if g.zs == ZO else jnp.minimum(z, ZO - 1)
        r = self.out.at[g.a, g.m, at]
        for j in (1, 2, 3):
            c = rcopy(r, r, self.sem.at[2, j, k], self.sem.at[3, j, k], g.xy(j)[1])
            g.owned(z, c.start)
            self.cxy[j, k] = (z, c)

    def line(self):
        g = self.g
        for k in range(1, g.zs):
            z = (g.z - k + g.zs) % g.zs
            g.owned(z, self.cz[k - 1].wait_recv)
            self.fan(z, k)

    def to_core(self, mm, i):
        r = self.out.at[self.g.a, mm]
        c = rcopy(r, r, self.sem.at[4, 0, i], self.sem.at[5, 0, i], self.g.core)
        c.start()
        self.cc.append(c)

    def square(self):
        g = self.g
        self.to_core(g.m, 0)
        for j in (1, 2, 3):
            for k in range(g.zs):
                z, c = self.cxy[j, k]
                g.owned(z, c.wait_recv)
            self.to_core((g.m - j + 4) % 4, j)

    def done(self):
        for c in self.cc:
            c.wait_recv()

    def finish(self):
        g = self.g
        for c in self.cz:
            g.owned(g.z, c.wait_send)
        for z, c in self.cxy.values():
            g.owned(z, c.wait_send)
        for c in self.cc:
            c.wait_send()


class Items:
    def __init__(self, surface, volume, bounds, rows):
        at = jnp.int32(0)
        self.starts, self.ends, self.surfs = [], [], []
        self.rows, self.bounds = rows, bounds
        for b in range(ITEMS):
            s = surface[0, b]
            self.starts.append(at)
            self.surfs.append(at + s)
            at = at + s + volume[0, b]
            self.ends.append(at)
            bounds[0, b] = self.starts[b]
            bounds[1, b] = self.ends[b]
            bounds[2, b] = jnp.minimum(lax.div(self.starts[b], jnp.int32(128)), rows // 128 - 2)

    def window(self, b):
        base = self.bounds[2, b]
        pos = iota((1, W), 1) + base * 128
        mask = (pos >= self.bounds[0, b]) & (pos < self.bounds[1, b])
        return base, mask.astype(F32).astype(BF)

    def surface(self):
        pos = iota((1, self.rows), 1)
        out = jnp.zeros((1, self.rows), F32)
        for b in range(ITEMS):
            out = out + ((pos >= self.starts[b]) & (pos < self.surfs[b])).astype(F32)
        return out

    def combine(self, t, buffers):
        first = jnp.int32(0)
        for b in range(ITEMS):
            first = first + (self.ends[b] <= t * 128).astype(jnp.int32)
        pos = iota((1, 128), 1) + t * 128
        outs = [None for _ in buffers]
        for k in range(5):
            b = jnp.minimum(first + k, ITEMS - 1)
            half = jnp.clip(t - self.bounds[2, b], 0, 1)
            low = jnp.where(first + k < ITEMS, self.bounds[0, b], self.rows)
            mask = ((pos >= low) & (pos < self.bounds[1, b])).astype(F32).astype(BF)
            for i, buf in enumerate(buffers):
                part = buf[2 * b + half] * mask
                outs[i] = part if outs[i] is None else outs[i] + part
        return outs


def pair(ref, base, rows):
    return jnp.concatenate([ref[base, rows, :], ref[base + 1, rows, :]], axis=1)


def put_pair(ref, i, rows, value):
    ref[2 * i, rows, :] = value[:, 0:128]
    ref[2 * i + 1, rows, :] = value[:, 128:256]


def column(row):
    return jnp.broadcast_to(row, (128, row.shape[1])).T


def wide(col):
    return jnp.concatenate([col, col], axis=1)


def norm_stats(v):
    mean = jnp.mean(v, axis=0, keepdims=True)
    centred = v - mean
    var = jnp.mean(centred * centred, axis=0, keepdims=True)
    scale = lax.rsqrt(var + NORM_EPS)
    return centred * scale, scale


def halves():
    lane = iota((1, 128), 1)
    return (lane < G).astype(F32).astype(BF), (lane >= G).astype(F32).astype(BF)


def spread_chunk(chunk):
    low, high = halves()
    zero = jnp.zeros((DH, 128), BF)
    one, two = chunk[0:DH], chunk[DH : 2 * DH]
    return jnp.concatenate(
        [
            jnp.concatenate([one * low, zero], axis=1),
            jnp.concatenate([one * high, zero], axis=1),
            jnp.concatenate([zero, two * low], axis=1),
            jnp.concatenate([zero, two * high], axis=1),
        ],
        axis=0,
    )


def take_chunk(full):
    low = iota((DH, 128), 1) < G
    one = jnp.where(low, full[0:DH, 0:128], full[DH : 2 * DH, 0:128])
    two = jnp.where(low, full[2 * DH : 3 * DH, 128:256], full[3 * DH : 4 * DH, 128:256])
    return one, two


def item_sums(probs, fields, mask):
    left = fields * mask
    left = jnp.concatenate([left, jnp.broadcast_to(mask, (16, W))], axis=0)
    full = nt(left, probs)
    one, two = take_chunk(full)
    return jnp.concatenate([one, two, full[128:136, 0:128], full[136:144, 128:256]], axis=0)


def slice_columns(small):
    low = small[:, 0:128].astype(BF)
    pick = (iota((H * G, 128), 0) % G == iota((H * G, 128), 1)).astype(F32).astype(BF)
    rows = nt(pick, low).astype(BF)
    place = (iota((DH, C), 1) % DH == iota((DH, C), 0)).astype(F32).astype(BF)
    full = nn(rows, place)
    keep = iota((H * G, C), 0) // G == iota((H * G, C), 1) // DH
    return jnp.where(keep, full, 0.0).astype(BF)


def same_head():
    return iota((4 * G, 4 * G), 0) // G == iota((4 * G, 4 * G), 1) // G


def first_kernel(
    zs, surface, volume, points, attn_w, mlp_w, small, vector,
    xt, normed, mid, probs, slice_out, saved, attention, wat, wml,
    bounds, surf, src, wxf, slicew, weight_sem, *sems,
):
    g = Place(zs)
    rows = points.shape[0]
    reduce = Reduce(g, src, sems[0:6])
    gather = Gather(g, slice_out, sems[6])
    own = pl.ds(pl.multiple_of(g.f * 64, 64), 64)
    other = pl.ds(pl.multiple_of(((1 - g.x) * 2 + g.a) * 64, 64), 64)
    wat[:, own, :] = attn_w[...].astype(BF)
    wml[:, own, :] = mlp_w[...].astype(BF)
    g.barrier()

    def weight(ref, at, i, dev):
        r = ref.at[:, at, :]
        return rcopy(r, r, weight_sem.at[0, i], weight_sem.at[1, i], dev)

    a_x, a_c = weight(wat, own, 0, g.xpeer), weight(wat, own, 1, g.core)
    m_x, m_c = weight(wml, own, 2, g.xpeer), weight(wml, own, 3, g.core)
    a_f, m_f = weight(wat, other, 4, g.core), weight(wml, other, 5, g.core)
    for c in (a_x, a_c, m_x, m_c):
        c.start()

    items = Items(surface, volume, bounds, rows)
    surf[...] = items.surface()
    gain = wide(column(vector[0:1, :]))
    embed = wide(column(vector[2:3, :]))

    def norm_tile(i, carry):
        at = tile_of(i)
        field = points[at, :].astype(F32).T
        xt[:, at] = field.astype(BF)
        unit, _ = norm_stats(field + embed * surf[:, at])
        normed[:, at] = (unit * gain).astype(BF)
        return carry

    lax.fori_loop(0, rows // W, norm_tile, 0)
    slicew[...] = slice_columns(small)
    a_x.wait_recv()
    a_f.start()
    a_c.wait_recv()
    a_f.wait_recv()
    wxf[0:C, :] = wat[0].astype(F32).T.astype(BF)
    wxf[C : 2 * C, :] = wat[1].astype(F32).T.astype(BF)

    def soft_tile(i, carry):
        at = tile_of(i)
        both = nn(wxf[...], normed[:, at]).astype(BF)
        put_pair(mid, i, slice(None), both)
        logits = nn(slicew[...], both[0:C]).reshape(H, G, W)
        top = jnp.max(logits, axis=1, keepdims=True)
        e = jnp.exp(logits - top)
        total = jnp.sum(e, axis=1, keepdims=True)
        put_pair(probs, i, slice(None), (e * (1.0 / total)).reshape(H * G, W).astype(BF))
        return carry

    lax.fori_loop(0, rows // W, soft_tile, 0)
    m_x.wait_recv()
    m_f.start()

    def item(half, mm, j):
        b = half * 8 + mm * 2 + j
        base, mask = items.window(b)
        for q in range(2):
            fields = pair(mid, base, slice(C + q * 128, C + q * 128 + 128))
            part = item_sums(pair(probs, base, slice(q * 256, q * 256 + 256)), fields, mask)
            src[half, mm, 2 * j + q] = part.astype(BF)

    for k in (1, 2, 3, 0):
        mm = (g.m + k) % 4
        for j in range(2):
            item(1 - g.a, mm, j)
        reduce.core(k)
    for k in (1, 2, 3, 0):
        mm = (g.m + k) % 4
        for j in range(2):
            item(g.a, mm, j)
        if k:
            reduce.square(k)
    reduce.line()
    chunk = reduce.result()

    sums = jnp.concatenate([chunk[0:DH], chunk[DH : 2 * DH]], axis=1)
    scale = jnp.concatenate([chunk[64:72], chunk[72:80]], axis=1) + SLICE_EPS
    token = sums / scale[0:1]
    maps = small[...]
    qkv = tn(maps, token, HIGH)
    query, key, value = qkv[64:96], qkv[96:128], qkv[128:160]
    scores = tn(key, query, HIGH) / math.sqrt(DH)
    scores = jnp.where(same_head(), scores, -jnp.inf)
    top = jnp.max(scores, axis=0, keepdims=True)
    e = jnp.exp(scores - top)
    weights = e / jnp.sum(e, axis=0, keepdims=True)
    out = nn(value, weights, HIGH)
    slice_out[g.a, g.m, g.zown] = jnp.concatenate([out[:, 0:128], out[:, 128:256]], axis=0).astype(BF)
    gather.start()
    saved[0:32] = token
    saved[32:128] = qkv[64:160]
    saved[128:160] = sums
    saved[160:168] = scale
    attention[...] = weights
    gather.line()
    gather.square()
    m_c.wait_recv()
    m_f.wait_recv()
    for c in (a_x, a_c, m_x, m_c, a_f, m_f):
        c.wait_send()
    gather.done()
    gather.finish()
    reduce.finish()


def second_kernel(
    zs, surface, volume, xt, probs, slice_out, saved, attention, wat, wml, small, vector, cotangent,
    mixed, d_mid, d_spread, d_slice, big, squares, small_part,
    bounds, surf, windows, spread, norm_two, active, d_hidden, cot_t, d_branch, wot, wint, woutt, gain_acc,
    src, src_big, red_big, big_sem, *sems,
):
    g = Place(zs)
    rows = cotangent.shape[0]
    reduce = Reduce(g, src, sems[0:6])
    reduce_big = Reduce(g, src_big, sems[6:12])
    gather = Gather(g, d_slice, sems[12])
    items = Items(surface, volume, bounds, rows)
    surf[...] = items.surface()
    gain = wide(column(vector[1:2, :]))
    embed = wide(column(vector[2:3, :]))
    g.barrier()

    def turned(v):
        return v.astype(F32).T.astype(BF)

    wot[...] = turned(wat[2])
    for j in range(FF // 256):
        wint[j * 256 : j * 256 + 256, :] = turned(wml[0, :, j * 256 : j * 256 + 256])
        woutt[j * 256 : j * 256 + 256, :] = turned(wml[1, :, j * 256 : j * 256 + 256])
    gain_acc[...] = jnp.zeros_like(gain_acc)

    def spread_item(b, carry):
        base, _ = items.window(b)
        for q in range(2):
            part = nn(spread_chunk(slice_out[2 * b + q]), pair(probs, base, slice(q * 256, q * 256 + 256))).astype(BF)
            windows[2 * b, q * 128 : q * 128 + 128, :] = part[:, 0:128]
            windows[2 * b + 1, q * 128 : q * 128 + 128, :] = part[:, 128:256]
        return carry

    lax.fori_loop(0, ITEMS, spread_item, 0)

    def mlp_tile(i, carry):
        at = tile_of(i)
        parts = [items.combine(2 * i + j, [windows])[0] for j in range(2)]
        sp = jnp.concatenate(parts, axis=1)
        spread[:, at] = sp
        middle = xt[:, at].astype(F32) + embed * surf[:, at] + nn(wot[...], sp)
        unit, scale = norm_stats(middle)
        two = (unit * gain).astype(BF)
        norm_two[:, at] = two
        ct = cotangent[at, :].astype(F32).T
        ctb = ct.astype(BF)
        cot_t[:, at] = ctb
        out = middle
        d_two = jnp.zeros((C, W), F32)
        for j in range(FF // 256):
            hid = pl.ds(j * 256, 256)
            x = nn(wint[hid, :], two)
            da = nn(woutt[hid, :], ctb)
            sq = x * x
            t = jnp.tanh(x * (GELU_A + GELU_B * sq))
            s = 0.5 + 0.5 * t
            act = (x * s).astype(BF)
            slope = s + (x * (s - s * s)) * (2.0 * GELU_A + 6.0 * GELU_B * sq)
            dh = (slope * da).astype(BF)
            active[hid, at] = act
            d_hidden[hid, at] = dh
            out = out + nn(wml[1, :, hid], act)
            d_two = d_two + nn(wml[0, :, hid], dh)
        mixed[at, :] = out.T.astype(BF)
        gs = d_two * unit
        gain_acc[...] += gs[:, 0:128] + gs[:, 128:256]
        du = d_two * gain
        m1 = jnp.mean(du, axis=0, keepdims=True)
        m2 = jnp.mean(du * unit, axis=0, keepdims=True)
        dm = ct + scale * (du - m1 - unit * m2)
        d_mid[:, at] = dm
        db = dm.astype(BF)
        d_branch[:, at] = db
        put_pair(d_spread, i, slice(None), nn(wat[2], db).astype(BF))
        return carry

    lax.fori_loop(0, rows // W, mlp_tile, 0)

    def item(half, mm, j):
        b = half * 8 + mm * 2 + j
        base, mask = items.window(b)
        for q in range(2):
            fields = pair(d_spread, base, slice(q * 128, q * 128 + 128))
            part = item_sums(pair(probs, base, slice(q * 256, q * 256 + 256)), fields, mask)
            src[half, mm, 2 * j + q] = part.astype(BF)

    for k in (1, 2, 3, 0):
        mm = (g.m + k) % 4
        for j in range(2):
            item(1 - g.a, mm, j)
        reduce.core(k)
    for k in (1, 2, 3, 0):
        mm = (g.m + k) % 4
        for j in range(2):
            item(g.a, mm, j)
        if k:
            reduce.square(k)

    def put(f, p, lo, value):
        src_big[f % 2, (f // 2) * 2 + p % 2, p // 2, lo : lo + value.shape[0], :] = value

    for which, (left, right) in enumerate(((norm_two, d_hidden), (cot_t, active))):
        for j in range(FF // 256):
            grad = nt(left[...], right[j * 256 : j * 256 + 256, :]).astype(BF)
            for f in range(4):
                for i in range(2):
                    put(f, 2 * j + i, which * 64, grad[f * 64 : f * 64 + 64, i * 128 : i * 128 + 128])
    grad = nt(spread[...], d_branch[...]).astype(BF)
    for f in range(4):
        for p in range(8):
            lo = f * 64 + (p % 4) * 16
            put(f, p, 128, grad[lo : lo + 16, (p // 4) * 128 : (p // 4) * 128 + 128])
    for k in (1, 2, 3, 0):
        reduce_big.core(k)

    reduce.line()
    chunk = reduce.result()
    d_out = jnp.concatenate([chunk[0:DH], chunk[DH : 2 * DH]], axis=1)
    token, query, key, value = saved[0:32], saved[32:64], saved[64:96], saved[96:128]
    sums, scale = saved[128:160], saved[160:161]
    weights = attention[...]
    d_value = nt(d_out, weights, HIGH)
    d_weights = tn(value, d_out, HIGH)
    d_scores = weights * (d_weights - jnp.sum(weights * d_weights, axis=0, keepdims=True))
    d_query = nn(key, d_scores, HIGH) / math.sqrt(DH)
    d_key = nt(query, d_scores, HIGH) / math.sqrt(DH)
    d_maps = jnp.concatenate([jnp.zeros((64, 256), F32), d_query, d_key, d_value], axis=0)
    d_token = nn(small[...], d_maps, HIGH)
    d_total = -jnp.sum(d_token * sums, axis=0, keepdims=True) / (scale * scale)
    d_sum = d_token / scale
    tot = jnp.broadcast_to(d_total, (8, 256))
    d_slice[g.a, g.m, g.zown] = jnp.concatenate(
        [d_sum[:, 0:128], d_sum[:, 128:256], tot[:, 0:128], tot[:, 128:256]], axis=0
    ).astype(BF)
    gather.start()
    grad_maps = nt(token, jnp.concatenate([d_maps, jnp.zeros((96, 256), F32)], axis=0), HIGH)
    if zs != ZO:
        grad_maps = jnp.where(g.z < ZO, grad_maps, 0.0)
    small_part[0:32, :] = grad_maps
    small_part[32:40, :] = nt(jnp.ones((8, 128), F32), gain_acc[...], HIGH)
    for k in (1, 2, 3):
        reduce_big.square(k)
    gather.line()
    gather.square()
    reduce_big.line()
    whole = reduce_big.result().astype(BF)
    red_big[...] = whole
    mine = whole.astype(F32)
    sq = jnp.sum((mine * mine).reshape(CB // 8, 8, 128), axis=0)
    squares[...] = sq if zs == ZO else jnp.where(g.z < ZO, sq, 0.0)
    big[g.zown, g.y] = whole
    part = big.at[g.zown, g.y]
    cz = []
    for k in range(1, zs):
        c = rcopy(part, part, big_sem.at[0, k], big_sem.at[1, k], g.zl(k)[1])
        g.owned(g.z, c.start)
        cz.append(c)
    cy = []

    def to_y(z, k):
        at = z if zs == ZO else jnp.minimum(z, ZO - 1)
        r = big.at[at, g.y]
        c = rcopy(r, r, big_sem.at[2, k], big_sem.at[3, k], g.ypeer)
        g.owned(z, c.start)
        cy.append((z, c))

    to_y(g.z, 0)
    for k in range(1, zs):
        z = (g.z - k + zs) % zs
        g.owned(z, cz[k - 1].wait_recv)
        to_y(z, k)
    gather.done()
    for z, c in cy:
        g.owned(z, c.wait_recv)
    gather.finish()
    reduce.finish()
    reduce_big.finish()
    for c in cz:
        g.owned(g.z, c.wait_send)
    for z, c in cy:
        g.owned(z, c.wait_send)


def adamw(state, new, sl, grad, factor, rate):
    weight, first, second, average = [r[sl] for r in state]
    clipped = grad * factor
    first_new = BETA_ONE * first + (1.0 - BETA_ONE) * clipped
    second_new = BETA_TWO * second + (1.0 - BETA_TWO) * clipped * clipped
    first_hat = first_new / (1.0 - BETA_ONE**STEP)
    second_hat = second_new / (1.0 - BETA_TWO**STEP)
    new_weight = weight - rate * (first_hat / (jnp.sqrt(second_hat) + ADAM_EPS) + DECAY * weight)
    average_new = EMA_RATE * average + (1.0 - EMA_RATE) * new_weight
    for r, v in zip(new, (new_weight, first_new, second_new, average_new, new_weight.astype(BF))):
        r[sl] = v


def third_kernel(zs, surface, volume, *refs):
    (xt, normed, mid, probs, slice_out, d_slice, d_mid, d_spread, wat, small_all, vector_all,
     big, squares, small_part) = refs[0:14]
    attn, mlp, small_s, vector_s = [refs[14 + 4 * i : 18 + 4 * i] for i in range(4)]
    points_grad, norm_out = refs[30:32]
    attn_new, mlp_new, small_new, vector_new = [refs[32 + 5 * i : 37 + 5 * i] for i in range(4)]
    (bounds, surf, windows_x, windows_f, d_both, slicet, slice_acc, gain_acc, embed_acc, src, late,
     small_src, small_sum, sr1, sr2, sr3, sqa, sqb, sem) = refs[52:71]
    sems = refs[71:]
    g = Place(zs)
    rows = xt.shape[1]
    reduce = Reduce(g, src, sems[0:6])
    items = Items(surface, volume, bounds, rows)
    surf[...] = items.surface()
    gain = wide(column(vector_all[0:1, :]))
    embed = wide(column(vector_all[2:3, :]))
    g.barrier(crossed=True)
    for r in (slice_acc, gain_acc, embed_acc):
        r[...] = jnp.zeros_like(r)
    slicet[...] = slice_columns(small_all).astype(F32).T.astype(BF)
    first_row = (iota((16, W), 0) == 0).astype(F32).astype(BF)

    def item(b, carry):
        base, mask = items.window(b)
        for q in range(2):
            four = slice(q * 128, q * 128 + 128)
            eight = slice(q * 256, q * 256 + 256)
            d_chunk = d_slice[2 * b + q]
            maps = spread_chunk(d_chunk[0:64])
            both = jnp.concatenate([spread_chunk(slice_out[2 * b + q]), maps], axis=0)
            fields = jnp.concatenate(
                [pair(d_spread, base, four), pair(mid, base, slice(C + q * 128, C + q * 128 + 128))], axis=0
            )
            tot = jnp.concatenate([d_chunk[64:72], d_chunk[72:80]], axis=1)
            tot = jnp.concatenate([tot, tot], axis=0)
            pb = pair(probs, base, eight)
            dp = (tn(both, fields) + tn(tot, first_row)).reshape(4, G, W)
            pf = pb.astype(F32).reshape(4, G, W)
            back = pf * (dp - jnp.sum(pf * dp, axis=1, keepdims=True))
            dl = back.reshape(4 * G, W).astype(BF) * mask
            dx = nn(slicet[four, eight], dl).astype(BF)
            df = nn(maps, pb).astype(BF)
            for half in range(2):
                windows_x[2 * b + half, four, :] = dx[:, half * 128 : half * 128 + 128]
                windows_f[2 * b + half, four, :] = df[:, half * 128 : half * 128 + 128]
            one, two = take_chunk(nt(pair(mid, base, four), dl))
            slice_acc[...] += one + two
        return carry

    lax.fori_loop(0, ITEMS, item, 0)

    def back_tile(i, carry):
        at = tile_of(i)
        parts = [items.combine(2 * i + j, [windows_x, windows_f]) for j in range(2)]
        dx = jnp.concatenate([parts[0][0], parts[1][0]], axis=1)
        df = jnp.concatenate([parts[0][1], parts[1][1]], axis=1)
        d_both[0:C, at] = dx
        d_both[C : 2 * C, at] = df
        d_norm = nn(wat[0], dx) + nn(wat[1], df)
        sf = surf[:, at]
        unit, scale = norm_stats(xt[:, at].astype(F32) + embed * sf)
        gs = d_norm * unit
        gain_acc[...] += gs[:, 0:128] + gs[:, 128:256]
        du = d_norm * gain
        m1 = jnp.mean(du, axis=0, keepdims=True)
        m2 = jnp.mean(du * unit, axis=0, keepdims=True)
        pg = d_mid[:, at] + scale * (du - m1 - unit * m2)
        es = pg * sf
        embed_acc[...] += es[:, 0:128] + es[:, 128:256]
        points_grad[at, :] = pg.T
        return carry

    lax.fori_loop(0, rows // W, back_tile, 0)

    grads = [nt(normed[...], d_both[i * C : i * C + C, :]).astype(BF) for i in range(2)]
    for f in range(4):
        for p in range(8):
            lo, col = f * 64 + (p % 4) * 16, (p // 4) * 128
            both = [v[lo : lo + 16, col : col + 128] for v in grads]
            src[f % 2, (f // 2) * 2 + p % 2, p // 2] = jnp.concatenate(both, axis=0)
    for k in (1, 2, 3, 0):
        reduce.core(k)

    ones = jnp.ones((8, 128), F32)
    rows_one = nt(ones, gain_acc[...], HIGH)
    rows_emb = nt(ones, embed_acc[...], HIGH)
    rows_two = small_part[32:40, :]
    fold = slice_acc[...]
    fold = jnp.where(iota((32, 128), 1) < G, fold + pltpu.roll(fold, G, 1), 0.0)
    pick = iota((8, 256), 0)
    vec = jnp.where(pick == 0, rows_one, jnp.where(pick == 1, rows_two, jnp.where(pick == 2, rows_emb, 0.0)))
    small_src[0:32] = (fold + small_part[0:32, 0:128]).astype(BF)
    small_src[32:64] = small_part[0:32, 128:256].astype(BF)
    small_src[64:80] = jnp.concatenate([vec[:, 0:128], vec[:, 128:256]], axis=0).astype(BF)
    cs = []
    c = rcopy(small_src, sr1, sem.at[0, 0], sem.at[1, 0], g.core)
    c.start()
    cs.append(c)
    for k in (1, 2, 3):
        reduce.square(k)
    c.wait_recv()
    sr2[g.m] = (small_src[...].astype(F32) + sr1[...].astype(F32)).astype(BF)
    for k in (1, 2, 3):
        c = rcopy(sr2.at[g.m], sr2.at[g.m], sem.at[0, k], sem.at[1, k], g.xy(k)[1])
        c.start()
        cs.append(c)
    reduce.line()
    for c in cs[1:4]:
        c.wait_recv()
    total = sr2[0].astype(F32)
    for m in range(1, 4):
        total = total + sr2[m].astype(F32)
    sr3[g.z] = total.astype(BF)
    for k in range(1, zs):
        c = rcopy(sr3.at[g.z], sr3.at[g.z], sem.at[2, k], sem.at[3, k], g.zl(k)[1])
        c.start()
        cs.append(c)

    whole = reduce.result().astype(BF)
    late[g.zown, g.y] = whole
    mine = whole.astype(F32)
    sq = jnp.sum((mine * mine).reshape(CL // 8, 8, 128), axis=0)
    if zs != ZO:
        sq = jnp.where(g.z < ZO, sq, 0.0)
    sqa[g.z] = sq + squares[...]
    part = late.at[g.zown, g.y]
    cz = []
    for k in range(1, zs):
        c = rcopy(part, part, sem.at[4, k], sem.at[5, k], g.zl(k)[1])
        g.owned(g.z, c.start)
        cz.append(c)
        c = rcopy(sqa.at[g.z], sqa.at[g.z], sem.at[6, k], sem.at[7, k], g.zl(k)[1])
        c.start()
        cs.append(c)
    cy = []

    def to_y(z, k):
        at = z if zs == ZO else jnp.minimum(z, ZO - 1)
        r = late.at[at, g.y]
        c = rcopy(r, r, sem.at[8, k], sem.at[9, k], g.ypeer)
        g.owned(z, c.start)
        cy.append((z, c))

    to_y(g.z, 0)
    for k in range(1, zs):
        cs[4 + zs - 2 + k].wait_recv()
    sq = sqa[0]
    for z in range(1, zs):
        sq = sq + sqa[z]
    here = g.a * 4 + g.m
    sqb[here] = sq
    for k in range(1, 8):
        dev = (g.core if k == 4 else g.xy(k)[1] if k < 4 else g.xy_other(k - 4)[1])
        c = rcopy(sqb.at[here], sqb.at[here], sem.at[10, k], sem.at[11, k], dev)
        c.start()
        cs.append(c)
    for k in range(1, zs):
        z = (g.z - k + zs) % zs
        g.owned(z, cz[k - 1].wait_recv)
        to_y(z, k)

    for k in range(1, zs):
        cs[3 + k].wait_recv()
    total = sr3[0].astype(F32)
    for z in range(1, zs):
        total = total + sr3[z].astype(F32)
    small_sum[...] = total
    for c in cs[-7:]:
        c.wait_recv()
    sq = sqb[0]
    for i in range(1, 8):
        sq = sq + sqb[i]
    norm = jnp.sqrt(jnp.sum(sq) + jnp.sum(total * total))
    norm_out[0, 0] = norm
    factor = jnp.minimum(1.0, CLIP / norm)
    everything = slice(None)
    gsmall = jnp.concatenate([total[0:32], total[32:64]], axis=1)[:, 0:160]
    adamw(small_s, small_new, (everything, everything), gsmall, factor, RATE_SMALL)
    gvec = jnp.concatenate([total[64:72], total[72:80]], axis=1)[0:3, :]
    adamw(vector_s, vector_new, (everything, everything), gvec, factor, RATE_VECTOR)
    for z in range(ZO):
        for y in range(2):
            p = z * 2 + y
            for i in range(2):
                grad = big[z, y, i * 64 : i * 64 + 64, :].astype(F32)
                adamw(mlp, mlp_new, (i, everything, slice(p * 128, p * 128 + 128)), grad, factor, RATE_MLP)
            lo, col = (p % 4) * 16, (p // 4) * 128
            grad = big[z, y, 128:144, :].astype(F32)
            adamw(attn, attn_new, (2, slice(lo, lo + 16), slice(col, col + 128)), grad, factor, RATE_ATTN)
    for z, c in cy:
        g.owned(z, c.wait_recv)
    for z in range(ZO):
        for y in range(2):
            p = z * 2 + y
            lo, col = (p % 4) * 16, (p // 4) * 128
            for i in range(2):
                grad = late[z, y, i * 16 : i * 16 + 16, :].astype(F32)
                adamw(attn, attn_new, (i, slice(lo, lo + 16), slice(col, col + 128)), grad, factor, RATE_ATTN)
    for c in cs:
        c.wait_send()
    for c in cz:
        g.owned(g.z, c.wait_send)
    for z, c in cy:
        g.owned(z, c.wait_send)
    reduce.finish()


def body(zs, points, cotangent, surface_count, volume_count, *state):
    attn, mlp, small, vector = [state[4 * i : 4 * i + 4] for i in range(4)]
    rows = points.shape[0]
    vmem = pl.BlockSpec(memory_space=pltpu.VMEM)
    smem = pl.BlockSpec(memory_space=pltpu.SMEM)
    sd = jax.ShapeDtypeStruct
    tall = pltpu.VMEM((C, rows), BF)

    def params(cid):
        return pltpu.CompilerParams(collective_id=cid, has_side_effects=True, vmem_limit_bytes=60 << 20)

    def tiles(features):
        return sd((rows // 128, features, 128), BF)

    chunks = sd((2, 4, ZO, 2 * DH, 128), BF)
    firsts = pl.pallas_call(
        functools.partial(first_kernel, zs),
        out_shape=[
            sd((C, rows), BF), sd((C, rows), BF), tiles(2 * C), tiles(H * G), chunks,
            sd((168, 256), F32), sd((256, 256), F32), sd((3, C, C), BF), sd((2, C, FF), BF),
        ],
        in_specs=[smem, smem] + [vmem] * 5,
        out_specs=[vmem] * 9,
        scratch_shapes=[
            pltpu.SMEM((3, ITEMS), jnp.int32), pltpu.VMEM((1, rows), F32), pltpu.VMEM((2, 4, ZO, CH, 128), BF),
            pltpu.VMEM((2 * C, C), BF), pltpu.VMEM((H * G, C), BF), pltpu.SemaphoreType.DMA((2, 6)),
        ] + Reduce.scratch(CH, zs) + Gather.scratch(zs),
        compiler_params=params(0),
        name="first",
    )(surface_count, volume_count, points, attn[0], mlp[0], small[0], vector[0])
    xt, normed, mid, probs, slice_out, saved, attention, wat, wml = firsts
    flat_out = slice_out.reshape(2 * ITEMS, 2 * DH, 128)

    seconds = pl.pallas_call(
        functools.partial(second_kernel, zs),
        out_shape=[
            sd((rows, C), BF), sd((C, rows), F32), tiles(C), sd((2, 4, ZO, CH, 128), BF),
            sd((ZO, 2, CB, 128), BF), sd((8, 128), F32), sd((40, 256), F32),
        ],
        in_specs=[smem, smem] + [vmem] * 10,
        out_specs=[vmem] * 7,
        scratch_shapes=[
            pltpu.SMEM((3, ITEMS), jnp.int32), pltpu.VMEM((1, rows), F32), pltpu.VMEM((2 * ITEMS, C, 128), BF),
            tall, tall, pltpu.VMEM((FF, rows), BF), pltpu.VMEM((FF, rows), BF), tall, tall,
            pltpu.VMEM((C, C), BF), pltpu.VMEM((FF, C), BF), pltpu.VMEM((FF, C), BF), pltpu.VMEM((C, 128), F32),
            pltpu.VMEM((2, 4, ZO, CH, 128), BF), pltpu.VMEM((2, 4, ZO, CB, 128), BF), pltpu.VMEM((CB, 128), BF),
            pltpu.SemaphoreType.DMA((4, max(zs, 4))),
        ] + Reduce.scratch(CH, zs) + Reduce.scratch(CB, zs) + Gather.scratch(zs),
        compiler_params=params(1),
        name="second",
    )(surface_count, volume_count, xt, probs, flat_out, saved, attention, wat, wml, small[0], vector[0], cotangent)
    mixed, d_mid, d_spread, d_slice, big, squares, small_part = seconds
    flat_d = d_slice.reshape(2 * ITEMS, CH, 128)

    def news(leaves):
        return [sd(leaves[0].shape, F32)] * 4 + [sd(leaves[0].shape, BF)]

    thirds = pl.pallas_call(
        functools.partial(third_kernel, zs),
        out_shape=[sd((rows, C), F32), sd((1, 1), F32)] + news(attn) + news(mlp) + news(small) + news(vector),
        in_specs=[smem, smem] + [vmem] * 30,
        out_specs=[vmem, smem] + [vmem] * 20,
        scratch_shapes=[
            pltpu.SMEM((3, ITEMS), jnp.int32), pltpu.VMEM((1, rows), F32), pltpu.VMEM((2 * ITEMS, C, 128), BF),
            pltpu.VMEM((2 * ITEMS, C, 128), BF), pltpu.VMEM((2 * C, rows), BF), pltpu.VMEM((C, H * G), BF),
            pltpu.VMEM((32, 128), F32), pltpu.VMEM((C, 128), F32), pltpu.VMEM((C, 128), F32),
            pltpu.VMEM((2, 4, ZO, CL, 128), BF), pltpu.VMEM((ZO, 2, CL, 128), BF),
            pltpu.VMEM((SM, 128), BF), pltpu.VMEM((SM, 128), F32), pltpu.VMEM((SM, 128), BF),
            pltpu.VMEM((4, SM, 128), BF), pltpu.VMEM((zs, SM, 128), BF),
            pltpu.VMEM((zs, 8, 128), F32), pltpu.VMEM((8, 8, 128), F32),
            pltpu.SemaphoreType.DMA((12, max(zs, 8))),
        ] + Reduce.scratch(CL, zs),
        compiler_params=params(2),
        name="third",
    )(surface_count, volume_count, xt, normed, mid, probs, flat_out, flat_d, d_mid, d_spread, wat, small[0], vector[0],
      big, squares, small_part, *attn, *mlp, *small, *vector)
    points_grad, norm = thirds[0:2]
    return (mixed, points_grad, norm.reshape(())) + tuple(thirds[2:])


def solution(mesh):
    rows = P(("pts", "fsdp"), None)
    split = P(None, "fsdp", None)
    in_specs = (rows,) * 4 + (split,) * 8 + (P(),) * 8
    out_specs = (rows, rows, P()) + (split,) * 10 + (P(),) * 10
    return jax.shard_map(
        functools.partial(body, mesh.shape["pts"] // 2),
        mesh=mesh, in_specs=in_specs, out_specs=out_specs, check_vma=False,
    )
```

```python
import functools
import math

import jax
import jax.numpy as jnp
from jax import lax
from jax.experimental import pallas as pl
from jax.experimental.pallas import tpu as pltpu
from jax.sharding import PartitionSpec as P

C = 256
H = 8
DH = 32
G = 64
FF = 1024
ITEMS = 16
STEP = 5
W = 256
T = 128
BATCH = 8
NORM_EPS = 1e-05
SLICE_EPS = 1e-05
CLIP = 1.0
BETA_ONE = 0.5
BETA_TWO = 0.5
ADAM_EPS = 1e-08
DECAY = 0.01
EMA_RATE = 0.6
RATE_ATTN = 0.04
RATE_MLP = 0.03
RATE_SMALL = 0.4
RATE_VECTOR = 0.3
ZO = 4
UN = 48
CB = 144
CL = 32
SM = 80
MESH = pl.DeviceIdType.MESH
HIGH = lax.Precision.HIGHEST
F32 = jnp.float32
BF = jnp.bfloat16
GELU_A = math.sqrt(2.0 / math.pi)
GELU_B = GELU_A * 0.044715


def nn(a, b, precision=None):
    return lax.dot_general(a, b, (((1,), (0,)), ((), ())), precision=precision, preferred_element_type=F32)


def nt(a, b, precision=None):
    return lax.dot_general(a, b, (((1,), (1,)), ((), ())), precision=precision, preferred_element_type=F32)


def tn(a, b, precision=None):
    return lax.dot_general(a, b, (((0,), (0,)), ((), ())), precision=precision, preferred_element_type=F32)


def iota(shape, dim):
    return lax.broadcasted_iota(jnp.int32, shape, dim)


def tile_of(i, width=W):
    return pl.ds(pl.multiple_of(i * width, width), width)


class Place:
    def __init__(self, zs):
        self.p = lax.axis_index("pts")
        self.f = lax.axis_index("fsdp")
        self.a = self.f % 2
        self.x = self.f // 2
        self.y = self.p % 2
        self.z = self.p // 2
        self.m = self.x * 2 + self.y
        self.zs = zs
        self.core = (self.p, self.f + 1 - 2 * self.a)
        self.xpeer = (self.p, (1 - self.x) * 2 + self.a)
        self.ypeer = (self.z * 2 + 1 - self.y, self.f)
        self.zown = self.z if zs == ZO else jnp.minimum(self.z, ZO - 1)

    def xy(self, k):
        mm = (self.m + k) % 4
        return mm, (self.z * 2 + mm % 2, (mm // 2) * 2 + self.a)

    def xy_other(self, k):
        mm = (self.m + k) % 4
        return mm, (self.z * 2 + mm % 2, (mm // 2) * 2 + 1 - self.a)

    def zl(self, k):
        zz = (self.z + k) % self.zs
        return zz, (zz * 2 + self.y, self.f)

    def barrier(self, crossed=False):
        b = pltpu.get_barrier_semaphore()
        peers = [self.core] + [self.xy(k)[1] for k in (1, 2, 3)] + [self.zl(k)[1] for k in range(1, self.zs)]
        if crossed:
            peers += [self.xy_other(k)[1] for k in (1, 2, 3)]
        for d in peers:
            pl.semaphore_signal(b, inc=1, device_id=d, device_id_type=MESH)
        pl.semaphore_wait(b, len(peers))

    def owned(self, z, fn):
        if self.zs == ZO:
            fn()
        else:
            pl.when(z < ZO)(fn)


def rcopy(src, dst, ss, rs, dev):
    return pltpu.make_async_remote_copy(
        src_ref=src, dst_ref=dst, send_sem=ss, recv_sem=rs, device_id=dev, device_id_type=MESH
    )


class Reduce:
    def __init__(self, g, src, bufs):
        self.g, self.src = g, src
        self.r1, self.s2, self.r2, self.s3, self.r3, self.sem = bufs
        self.c1, self.c2, self.c3 = {}, [], []

    @staticmethod
    def scratch(rows, zs):
        return [
            pltpu.VMEM((4, ZO, rows, 128), BF),
            pltpu.VMEM((3, ZO, rows, 128), BF),
            pltpu.VMEM((3, ZO, rows, 128), BF),
            pltpu.VMEM((ZO, rows, 128), BF),
            pltpu.VMEM((zs - 1, rows, 128), BF),
            pltpu.SemaphoreType.DMA((6, max(zs, 4))),
        ]

    def core(self, k):
        g = self.g
        mm = (g.m + k) % 4
        c = rcopy(self.src.at[1 - g.a, mm], self.r1.at[mm], self.sem.at[0, k], self.sem.at[1, k], g.core)
        c.start()
        self.c1[k] = c

    def pair(self, k):
        g = self.g
        self.c1[k].wait_recv()
        mm = (g.m + k) % 4
        return self.src[g.a, mm].astype(F32) + self.r1[mm].astype(F32)

    def square(self, k):
        g = self.g
        dev = g.xy(k)[1]
        self.s2[k - 1] = self.pair(k).astype(BF)
        c = rcopy(self.s2.at[k - 1], self.r2.at[k - 1], self.sem.at[2, k - 1], self.sem.at[3, k - 1], dev)
        c.start()
        self.c2.append(c)

    def line(self):
        g = self.g
        acc = self.pair(0)
        for k in (1, 2, 3):
            self.c2[k - 1].wait_recv()
            acc = acc + self.r2[k - 1].astype(F32)
        self.s3[...] = acc.astype(BF)
        for k in range(1, g.zs):
            zz, dev = g.zl(k)
            at = zz if g.zs == ZO else jnp.minimum(zz, ZO - 1)
            c = rcopy(self.s3.at[at], self.r3.at[k - 1], self.sem.at[4, k - 1], self.sem.at[5, k - 1], dev)
            g.owned(zz, c.start)
            self.c3.append(c)

    def result(self):
        g = self.g
        out = self.s3[g.zown].astype(F32)
        for k in range(1, g.zs):
            g.owned(g.z, self.c3[k - 1].wait_recv)
            out = out + self.r3[k - 1].astype(F32)
        return out

    def finish(self):
        g = self.g
        for c in self.c1.values():
            c.wait_send()
        for c in self.c2:
            c.wait_send()
        for k in range(1, g.zs):
            g.owned(g.zl(k)[0], self.c3[k - 1].wait_send)


class Gather:
    def __init__(self, g, out, sem):
        self.g, self.out, self.sem = g, out, sem
        self.cz, self.cxy, self.cc = [], [], []

    @staticmethod
    def scratch(zs):
        return [pltpu.SemaphoreType.DMA((6, max(zs, 4)))]

    def start(self):
        g = self.g
        own = self.out.at[g.a, g.m, g.zown]
        for k in range(1, g.zs):
            c = rcopy(own, own, self.sem.at[0, k], self.sem.at[1, k], g.zl(k)[1])
            g.owned(g.z, c.start)
            self.cz.append(c)

    def line(self):
        g = self.g
        for k in range(1, g.zs):
            g.owned((g.z - k + g.zs) % g.zs, self.cz[k - 1].wait_recv)
        r = self.out.at[g.a, g.m]
        for j in (1, 2, 3):
            c = rcopy(r, r, self.sem.at[2, j], self.sem.at[3, j], g.xy(j)[1])
            c.start()
            self.cxy.append(c)
        self.to_core(g.m, 0)

    def to_core(self, mm, i):
        r = self.out.at[self.g.a, mm]
        c = rcopy(r, r, self.sem.at[4, i], self.sem.at[5, i], self.g.core)
        c.start()
        self.cc.append(c)

    def square(self):
        g = self.g
        for j in (1, 2, 3):
            self.cxy[j - 1].wait_recv()
            self.to_core((g.m - j + 4) % 4, j)

    def done(self):
        for c in self.cc:
            c.wait_recv()

    def finish(self):
        g = self.g
        for c in self.cz:
            g.owned(g.z, c.wait_send)
        for c in self.cxy + self.cc:
            c.wait_send()


def counts(surface, volume):
    at = jnp.int32(0)
    starts, surfs, sizes = [], [], []
    for b in range(ITEMS):
        starts.append(at)
        surfs.append(surface[0, b])
        sizes.append(surface[0, b] + volume[0, b])
        at = at + sizes[b]
    return starts, surfs, sizes, at


def column(row):
    return jnp.broadcast_to(row, (128, row.shape[1])).T


def wide(col):
    return jnp.concatenate([col, col], axis=1)


def norm_stats(v):
    mean = jnp.mean(v, axis=0, keepdims=True)
    centred = v - mean
    var = jnp.mean(centred * centred, axis=0, keepdims=True)
    scale = lax.rsqrt(var + NORM_EPS)
    return centred * scale, scale


def halves():
    lane = iota((1, 128), 1)
    return (lane < G).astype(F32).astype(BF), (lane >= G).astype(F32).astype(BF)


def spread_units(one, two):
    low, high = halves()
    zero = jnp.zeros((DH, 128), BF)
    return jnp.concatenate(
        [
            jnp.concatenate([one * low, zero], axis=1),
            jnp.concatenate([one * high, zero], axis=1),
            jnp.concatenate([zero, two * low], axis=1),
            jnp.concatenate([zero, two * high], axis=1),
        ],
        axis=0,
    )


def take_units(full):
    low = iota((DH, 128), 1) < G
    one = jnp.where(low, full[0:DH, 0:128], full[DH : 2 * DH, 0:128])
    two = jnp.where(low, full[2 * DH : 3 * DH, 128:256], full[3 * DH : 4 * DH, 128:256])
    return one, two


def item_units(fields, probs):
    left = jnp.concatenate([fields, jnp.ones((16, T), BF)], axis=0)
    full = nt(left, probs)
    one, two = take_units(full)
    one = jnp.concatenate([one, full[128:144, 0:128]], axis=0)
    two = jnp.concatenate([two, full[128:144, 128:256]], axis=0)
    return one.astype(BF), two.astype(BF)


def slice_columns(small):
    low = small[:, 0:128].astype(BF)
    pick = (iota((H * G, 128), 0) % G == iota((H * G, 128), 1)).astype(F32).astype(BF)
    rows = nt(pick, low).astype(BF)
    place = (iota((DH, C), 1) % DH == iota((DH, C), 0)).astype(F32).astype(BF)
    full = nn(rows, place)
    keep = iota((H * G, C), 0) // G == iota((H * G, C), 1) // DH
    return jnp.where(keep, full, 0.0).astype(BF)


def same_head():
    return iota((2 * G, 2 * G), 0) // G == iota((2 * G, 2 * G), 1) // G


def main_kernel(
    zs, surface, volume, points, cotangent, attn_w, mlp_w, small, vector,
    mixed, points_grad, big, late, small_sum, norm_out,
    bounds, surf, keep, xt, cot_t, normed, mid, probs, spread, norm_two, active, d_hidden, d_branch, d_spread, d_mid,
    d_both, wat, wml, wxf, slicew, slicet, wot, wint, woutt, gain_one, gain_two, embed_acc, slice_acc,
    src, src_big, src_late, slice_out, d_slice, saved, attention, maps_acc,
    small_src, sr1, sr2, sr3, sqa, sqb, weight_sem, big_sem, sem, *sems,
):
    g = Place(zs)
    rows = ITEMS * T
    red = [Reduce(g, src.at[i], sems[6 * i : 6 * i + 6]) for i in range(4)]
    red_big = Reduce(g, src_big, sems[24:30])
    red_late = Reduce(g, src_late, sems[30:36])
    gat = [Gather(g, slice_out.at[i], sems[36 + i]) for i in range(2)]
    gat += [Gather(g, d_slice.at[i], sems[38 + i]) for i in range(2)]

    own = pl.ds(pl.multiple_of(g.f * 64, 64), 64)
    other = pl.ds(pl.multiple_of(((1 - g.x) * 2 + g.a) * 64, 64), 64)
    wat[:, own, :] = attn_w[...].astype(BF)
    g.barrier(crossed=True)

    def weight(ref, at, i, dev):
        r = ref.at[:, at, :]
        return rcopy(r, r, weight_sem.at[0, i], weight_sem.at[1, i], dev)

    a_x, a_c = weight(wat, own, 0, g.xpeer), weight(wat, own, 1, g.core)
    m_x, m_c = weight(wml, own, 2, g.xpeer), weight(wml, own, 3, g.core)
    a_f, m_f = weight(wat, other, 4, g.core), weight(wml, other, 5, g.core)
    a_x.start()
    a_c.start()
    wml[:, own, :] = mlp_w[...].astype(BF)
    m_x.start()
    m_c.start()

    starts, surfs, sizes, total = counts(surface, volume)
    lane = iota((1, T), 1)
    for b in range(ITEMS):
        shift = total + b * T - starts[b] - sizes[b]
        bounds[0, b] = starts[b]
        bounds[1, b] = sizes[b]
        bounds[2, b] = shift
        bounds[3, b] = jnp.minimum(lax.div(starts[b], jnp.int32(T)), ITEMS - 2)
        bounds[4, b] = jnp.minimum(lax.div(shift, jnp.int32(T)), ITEMS - 2)
        surf[:, b * T : b * T + T] = (lane < surfs[b]).astype(F32)
        keep[:, b * T : b * T + T] = (lane < sizes[b]).astype(F32)
    gain_a = column(vector[0:1, :])
    gain_b = wide(column(vector[1:2, :]))
    embed = column(vector[2:3, :])
    embed2 = wide(embed)

    def pack_item(b, carry):
        at = tile_of(b, T)
        t, u, size = bounds[3, b], bounds[4, b], bounds[1, b]
        both = [
            jnp.concatenate([ref[i] for i in (t, t + 1, u, u + 1)], axis=0) for ref in (points, cotangent)
        ]
        to, row = iota((T, 2 * T), 0), iota((T, 2 * T), 1)
        one = (row + t * T == to + bounds[0, b]) & (to < size)
        two = (row + u * T == to + bounds[2, b]) & (to >= size)
        pick = jnp.concatenate([one.astype(F32).astype(BF), two.astype(F32).astype(BF)], axis=1)
        field = nn(pick, both[0]).T
        cot_t[:, at] = nn(pick, both[1]).T.astype(BF)
        xt[:, at] = field.astype(BF)
        unit, _ = norm_stats(field + embed * surf[:, at])
        normed[:, at] = (unit * gain_a).astype(BF)
        return carry

    lax.fori_loop(0, ITEMS, pack_item, 0)
    slicew[...] = slice_columns(small)
    for r in (gain_one, gain_two, embed_acc, slice_acc, maps_acc):
        r[...] = jnp.zeros_like(r)

    def turned(v):
        return v.astype(F32).T.astype(BF)

    a_x.wait_recv()
    a_f.start()
    a_c.wait_recv()
    a_f.wait_recv()
    wxf[0:C, :] = turned(wat[0])
    wxf[C : 2 * C, :] = turned(wat[1])

    def soft_tile(i, carry):
        at = tile_of(i)
        both = nn(wxf[...], normed[:, at]).astype(BF)
        mid[:, at] = both
        logits = nn(slicew[...], both[0:C]).reshape(H, G, W)
        top = jnp.max(logits, axis=1, keepdims=True)
        e = jnp.exp(logits - top)
        scale = keep[:, at] / jnp.sum(e, axis=1, keepdims=True)
        probs[:, at] = (e * scale).reshape(H * G, W).astype(BF)
        return carry

    def sums(r, batch, fields, off):
        for half in range(2):
            for k in (1, 2, 3, 0):
                mm = (g.m + k) % 4
                core = (1 - g.a) if half == 0 else g.a
                at = tile_of(batch * BATCH + core * 4 + mm, T)
                for q in range(2):
                    both = item_units(fields[off + q * 128 : off + q * 128 + 128, at], probs[q * 256 : q * 256 + 256, at])
                    for i in range(2):
                        r.src[core, mm, 2 * q + i] = both[i]
                if half == 0:
                    r.core(k)

    def attend(batch):
        unit = red[batch].result()
        raw, scale = unit[0:DH], unit[DH : DH + 8] + SLICE_EPS
        token = raw / scale[0:1]
        qkv = tn(small[...], token, HIGH)
        query, key, value = qkv[64:96], qkv[96:128], qkv[128:160]
        scores = tn(key, query, HIGH) / math.sqrt(DH)
        scores = jnp.where(same_head(), scores, -jnp.inf)
        top = jnp.max(scores, axis=0, keepdims=True)
        e = jnp.exp(scores - top)
        weights = e / jnp.sum(e, axis=0, keepdims=True)
        slice_out[batch, g.a, g.m, g.zown] = nn(value, weights, HIGH).astype(BF)
        gat[batch].start()
        saved[batch, 0:32] = token
        saved[batch, 32:128] = qkv[64:160]
        saved[batch, 128:160] = raw
        saved[batch, 160:168] = scale
        attention[batch] = weights

    def attend_back(batch):
        unit = red[2 + batch].result()
        d_out = unit[0:DH]
        s = saved.at[batch]
        token, query, key, value = s[0:32], s[32:64], s[64:96], s[96:128]
        raw, scale = s[128:160], s[160:161]
        weights = attention[batch]
        d_value = nt(d_out, weights, HIGH)
        d_weights = tn(value, d_out, HIGH)
        d_scores = weights * (d_weights - jnp.sum(weights * d_weights, axis=0, keepdims=True))
        d_query = nn(key, d_scores, HIGH) / math.sqrt(DH)
        d_key = nt(query, d_scores, HIGH) / math.sqrt(DH)
        d_maps = jnp.concatenate([jnp.zeros((64, T), F32), d_query, d_key, d_value], axis=0)
        d_token = nn(small[...], d_maps, HIGH)
        d_total = -jnp.sum(d_token * raw, axis=0, keepdims=True) / (scale * scale)
        tot = jnp.broadcast_to(d_total, (16, T))
        d_slice[batch, g.a, g.m, g.zown] = jnp.concatenate([d_token / scale, tot], axis=0).astype(BF)
        gat[2 + batch].start()
        part = nt(token, jnp.concatenate([d_maps, jnp.zeros((96, T), F32)], axis=0), HIGH)
        if zs != ZO:
            part = jnp.where(g.z < ZO, part, 0.0)
        maps_acc[...] += part

    lax.fori_loop(0, 4, soft_tile, 0)
    sums(red[0], 0, mid, C)
    lax.fori_loop(4, 6, soft_tile, 0)
    for k in (1, 2, 3):
        red[0].square(k)
    lax.fori_loop(6, 8, soft_tile, 0)
    sums(red[1], 1, mid, C)
    red[0].line()
    for k in (1, 2, 3):
        red[1].square(k)
    m_x.wait_recv()
    m_f.start()
    wot[...] = turned(wat[2])
    attend(0)
    red[1].line()
    slicet[...] = turned(slicew[...])
    gat[0].line()
    m_c.wait_recv()
    m_f.wait_recv()
    attend(1)
    gat[0].square()
    for j in range(FF // 256):
        wint[j * 256 : j * 256 + 256, :] = turned(wml[0, :, j * 256 : j * 256 + 256])
        woutt[j * 256 : j * 256 + 256, :] = turned(wml[1, :, j * 256 : j * 256 + 256])
    gat[1].line()
    gat[0].done()

    def spread_item(b, carry):
        at = tile_of(b, T)
        batch = b // BATCH
        core = (b % BATCH) // 4
        for q in range(2):
            units = [slice_out[batch, core, b % 4, 2 * q + i] for i in range(2)]
            part = nn(spread_units(*units), probs[q * 256 : q * 256 + 256, at])
            spread[q * 128 : q * 128 + 128, at] = part.astype(BF)
        return carry

    def mlp_tile(i, carry):
        at = tile_of(i)
        middle = xt[:, at].astype(F32) + embed2 * surf[:, at] + nn(wot[...], spread[:, at])
        unit, scale = norm_stats(middle)
        two = (unit * gain_b).astype(BF)
        norm_two[:, at] = two
        ctb = cot_t[:, at]
        out = middle
        d_two = jnp.zeros((C, W), F32)
        for j in range(FF // 256):
            hid = pl.ds(j * 256, 256)
            x = nn(wint[hid, :], two)
            da = nn(woutt[hid, :], ctb)
            sq = x * x
            t = jnp.tanh(x * (GELU_A + GELU_B * sq))
            s = 0.5 + 0.5 * t
            act = (x * s).astype(BF)
            slope = s + (x * (s - s * s)) * (2.0 * GELU_A + 6.0 * GELU_B * sq)
            dh = (slope * da).astype(BF)
            active[hid, at] = act
            d_hidden[hid, at] = dh
            out = out + nn(wml[1, :, hid], act)
            d_two = d_two + nn(wml[0, :, hid], dh)
        mixed[:, at] = out.astype(BF)
        gs = d_two * unit
        gain_two[...] += gs[:, 0:128] + gs[:, 128:256]
        du = d_two * gain_b
        m1 = jnp.mean(du, axis=0, keepdims=True)
        m2 = jnp.mean(du * unit, axis=0, keepdims=True)
        dm = ctb.astype(F32) + scale * (du - m1 - unit * m2)
        d_mid[:, at] = dm
        db = dm.astype(BF)
        d_branch[:, at] = db
        d_spread[:, at] = nn(wat[2], db).astype(BF)
        return carry

    lax.fori_loop(0, BATCH, spread_item, 0)
    lax.fori_loop(0, 2, mlp_tile, 0)
    gat[1].square()
    lax.fori_loop(2, 4, mlp_tile, 0)
    sums(red[2], 0, d_spread, 0)
    gat[1].done()
    lax.fori_loop(BATCH, ITEMS, spread_item, 0)
    lax.fori_loop(4, 5, mlp_tile, 0)
    for k in (1, 2, 3):
        red[2].square(k)
    lax.fori_loop(5, 7, mlp_tile, 0)
    red[2].line()
    lax.fori_loop(7, 8, mlp_tile, 0)
    sums(red[3], 1, d_spread, 0)
    attend_back(0)

    def put(f, p, lo, value):
        src_big[f % 2, (f // 2) * 2 + p % 2, p // 2, lo : lo + value.shape[0], :] = value

    def grad_mlp(which, left, right):
        for j in range(FF // 256):
            grad = nt(left[...], right[j * 256 : j * 256 + 256, :]).astype(BF)
            for f in range(4):
                for i in range(2):
                    put(f, 2 * j + i, which * 64, grad[f * 64 : f * 64 + 64, i * 128 : i * 128 + 128])

    grad_mlp(0, norm_two, d_hidden)
    for k in (1, 2, 3):
        red[3].square(k)
    gat[2].line()
    grad_mlp(1, cot_t, active)
    grad = nt(spread[...], d_branch[...]).astype(BF)
    for f in range(4):
        for p in range(8):
            lo = f * 64 + (p % 4) * 16
            put(f, p, 128, grad[lo : lo + 16, (p // 4) * 128 : (p // 4) * 128 + 128])
    for k in (1, 2, 3, 0):
        red_big.core(k)
    red[3].line()
    gat[2].square()
    attend_back(1)
    for k in (1, 2, 3):
        red_big.square(k)
    gat[2].done()
    first_row = (iota((16, T), 0) == 0).astype(F32).astype(BF)

    def back_item(b, carry):
        at = tile_of(b, T)
        batch = b // BATCH
        core = (b % BATCH) // 4
        for q in range(2):
            four = slice(q * 128, q * 128 + 128)
            eight = slice(q * 256, q * 256 + 256)
            outs = [slice_out[batch, core, b % 4, 2 * q + i] for i in range(2)]
            ds = [d_slice[batch, core, b % 4, 2 * q + i] for i in range(2)]
            maps = spread_units(ds[0][0:DH], ds[1][0:DH])
            both = jnp.concatenate([spread_units(*outs), maps], axis=0)
            fields = jnp.concatenate([d_spread[four, at], mid[C + q * 128 : C + q * 128 + 128, at]], axis=0)
            tot = jnp.concatenate([ds[0][DH:UN], ds[1][DH:UN]], axis=1)
            pb = probs[eight, at]
            dp = (tn(both, fields) + tn(tot, first_row)).reshape(4, G, T)
            pf = pb.astype(F32).reshape(4, G, T)
            back = pf * (dp - jnp.sum(pf * dp, axis=1, keepdims=True))
            dl = back.reshape(4 * G, T).astype(BF)
            d_both[four, at] = nn(slicet[four, eight], dl).astype(BF)
            d_both[C + q * 128 : C + q * 128 + 128, at] = nn(maps, pb).astype(BF)
            one, two = take_units(nt(mid[four, at], dl))
            slice_acc[...] += one + two
        return carry

    def back_tile(i, carry):
        at = tile_of(i)
        d_norm = nn(wat[0], d_both[0:C, at]) + nn(wat[1], d_both[C : 2 * C, at])
        sf = surf[:, at]
        unit, scale = norm_stats(xt[:, at].astype(F32) + embed2 * sf)
        gs = d_norm * unit
        gain_one[...] += gs[:, 0:128] + gs[:, 128:256]
        du = d_norm * wide(gain_a)
        m1 = jnp.mean(du, axis=0, keepdims=True)
        m2 = jnp.mean(du * unit, axis=0, keepdims=True)
        pg = d_mid[:, at] + scale * (du - m1 - unit * m2)
        es = pg * sf
        embed_acc[...] += es[:, 0:128] + es[:, 128:256]
        points_grad[:, at] = pg
        return carry

    lax.fori_loop(0, 4, back_item, 0)
    gat[3].line()
    lax.fori_loop(4, BATCH, back_item, 0)
    red_big.line()
    gat[3].square()
    lax.fori_loop(0, 4, back_tile, 0)
    gat[3].done()
    lax.fori_loop(BATCH, ITEMS, back_item, 0)

    grads = [nt(normed[...], d_both[i * C : i * C + C, :]).astype(BF) for i in range(2)]
    for f in range(4):
        for p in range(8):
            lo, col = f * 64 + (p % 4) * 16, (p // 4) * 128
            both = [v[lo : lo + 16, col : col + 128] for v in grads]
            src_late[f % 2, (f // 2) * 2 + p % 2, p // 2] = jnp.concatenate(both, axis=0)
    for k in (1, 2, 3, 0):
        red_late.core(k)
    whole = red_big.result().astype(BF)
    big[g.zown, g.y] = whole
    mine = whole.astype(F32)
    squares = jnp.sum((mine * mine).reshape(CB // 8, 8, 128), axis=0)

    def share(ref, base):
        part = ref.at[g.zown, g.y]
        cz, cy = [], []
        for k in range(1, zs):
            c = rcopy(part, part, big_sem.at[base, k], big_sem.at[base + 1, k], g.zl(k)[1])
            g.owned(g.z, c.start)
            cz.append(c)

        def to_y(z, k):
            at = z if zs == ZO else jnp.minimum(z, ZO - 1)
            r = ref.at[at, g.y]
            c = rcopy(r, r, big_sem.at[base + 2, k], big_sem.at[base + 3, k], g.ypeer)
            g.owned(z, c.start)
            cy.append((z, c))

        to_y(g.z, 0)

        def rest():
            for k in range(1, zs):
                z = (g.z - k + zs) % zs
                g.owned(z, cz[k - 1].wait_recv)
                to_y(z, k)

        def done():
            for z, c in cy:
                g.owned(z, c.wait_recv)

        def finish():
            for c in cz:
                g.owned(g.z, c.wait_send)
            for z, c in cy:
                g.owned(z, c.wait_send)

        return rest, done, finish

    big_rest, big_done, big_finish = share(big, 0)
    lax.fori_loop(4, 8, back_tile, 0)

    ones = jnp.ones((8, 128), F32)
    line = [nt(ones, r[...], HIGH) for r in (gain_one, gain_two, embed_acc)]
    fold = slice_acc[...]
    fold = jnp.where(iota((32, 128), 1) < G, fold + pltpu.roll(fold, G, 1), 0.0)
    pick = iota((8, 256), 0)
    vec = jnp.where(pick == 0, line[0], jnp.where(pick == 1, line[1], jnp.where(pick == 2, line[2], 0.0)))
    small_src[0:32] = (fold + maps_acc[:, 0:128]).astype(BF)
    small_src[32:64] = maps_acc[:, 128:256].astype(BF)
    small_src[64:80] = jnp.concatenate([vec[:, 0:128], vec[:, 128:256]], axis=0).astype(BF)
    cs = [rcopy(small_src, sr1, sem.at[0, 0], sem.at[1, 0], g.core)]
    cs[0].start()
    for k in (1, 2, 3):
        red_late.square(k)
    cs[0].wait_recv()
    sr2[g.m] = (small_src[...].astype(F32) + sr1[...].astype(F32)).astype(BF)
    for k in (1, 2, 3):
        c = rcopy(sr2.at[g.m], sr2.at[g.m], sem.at[0, k], sem.at[1, k], g.xy(k)[1])
        c.start()
        cs.append(c)
    big_rest()
    red_late.line()
    for c in cs[1:4]:
        c.wait_recv()
    total = sr2[0].astype(F32)
    for m in range(1, 4):
        total = total + sr2[m].astype(F32)
    sr3[g.z] = total.astype(BF)
    for k in range(1, zs):
        c = rcopy(sr3.at[g.z], sr3.at[g.z], sem.at[2, k], sem.at[3, k], g.zl(k)[1])
        c.start()
        cs.append(c)
    whole = red_late.result().astype(BF)
    late[g.zown, g.y] = whole
    mine = whole.astype(F32)
    squares = squares + jnp.sum((mine * mine).reshape(CL // 8, 8, 128), axis=0)
    if zs != ZO:
        squares = jnp.where(g.z < ZO, squares, 0.0)
    sqa[g.z] = squares
    late_rest, late_done, late_finish = share(late, 4)
    for k in range(1, zs):
        c = rcopy(sqa.at[g.z], sqa.at[g.z], sem.at[6, k], sem.at[7, k], g.zl(k)[1])
        c.start()
        cs.append(c)
    for k in range(1, zs):
        cs[3 + k].wait_recv()
    total = sr3[0].astype(F32)
    for z in range(1, zs):
        total = total + sr3[z].astype(F32)
    small_sum[...] = total
    late_rest()
    for k in range(1, zs):
        cs[2 + zs + k].wait_recv()
    sq = sqa[0]
    for z in range(1, zs):
        sq = sq + sqa[z]
    here = g.a * 4 + g.m
    sqb[here] = sq
    for k in range(1, 8):
        dev = g.core if k == 4 else g.xy(k)[1] if k < 4 else g.xy_other(k - 4)[1]
        c = rcopy(sqb.at[here], sqb.at[here], sem.at[10, k], sem.at[11, k], dev)
        c.start()
        cs.append(c)
    big_done()
    late_done()
    for c in cs[-7:]:
        c.wait_recv()
    sq = sqb[0]
    for i in range(1, 8):
        sq = sq + sqb[i]
    norm_out[0, 0] = jnp.sqrt(jnp.sum(sq) + jnp.sum(total * total))

    for c in cs + [a_x, a_c, m_x, m_c, a_f, m_f]:
        c.wait_send()
    big_finish()
    late_finish()
    for r in red + [red_big, red_late] + gat:
        r.finish()


def adamw(state, new, sl, grad, factor, rate):
    weight, first, second, average = [r[sl] for r in state]
    clipped = grad * factor
    first_new = BETA_ONE * first + (1.0 - BETA_ONE) * clipped
    second_new = BETA_TWO * second + (1.0 - BETA_TWO) * clipped * clipped
    first_hat = first_new / (1.0 - BETA_ONE**STEP)
    second_hat = second_new / (1.0 - BETA_TWO**STEP)
    new_weight = weight - rate * (first_hat / (jnp.sqrt(second_hat) + ADAM_EPS) + DECAY * weight)
    average_new = EMA_RATE * average + (1.0 - EMA_RATE) * new_weight
    for r, v in zip(new, (new_weight, first_new, second_new, average_new, new_weight.astype(BF))):
        r[sl] = v


def last_kernel(surface, volume, mixed_t, grad_t, big, late, small_sum, norm, *refs):
    attn, mlp, small_s, vector_s = [refs[4 * i : 4 * i + 4] for i in range(4)]
    mixed, points_grad = refs[16:18]
    attn_new, mlp_new, small_new, vector_new = [refs[18 + 5 * i : 23 + 5 * i] for i in range(4)]
    wide_mixed = refs[38]
    rows = mixed.shape[0]
    starts, _, sizes, total = counts(surface, volume)
    span = T + 8
    at = iota((span, 1), 0)
    for b in range(ITEMS):
        shift = total + b * T - starts[b] - sizes[b]
        tile = slice(b * T, b * T + T)
        zero = jnp.zeros((8, C), F32)
        for out, value in ((points_grad, grad_t[:, tile]), (wide_mixed, mixed_t[:, tile].astype(F32))):
            turned = jnp.concatenate([value.T, zero], axis=0)
            for base, low, high in ((starts[b], 0, sizes[b]), (shift, sizes[b], T)):
                first = jnp.minimum(lax.div(base, jnp.int32(8)) * 8, rows - span)
                off = base - first
                moved = pltpu.roll(turned, off, 0)
                here = pl.ds(pl.multiple_of(first, 8), span)
                out[here, :] = jnp.where((at >= low + off) & (at < high + off), moved, out[here, :])
    mixed[...] = wide_mixed[...].astype(BF)

    factor = jnp.minimum(1.0, CLIP / norm[0, 0])
    everything = slice(None)
    both = (everything, everything)
    gsmall = jnp.concatenate([small_sum[0:32, :], small_sum[32:64, :]], axis=1)[:, 0:160]
    adamw(small_s, small_new, both, gsmall, factor, RATE_SMALL)
    gvec = jnp.concatenate([small_sum[64:72, :], small_sum[72:80, :]], axis=1)[0:3, :]
    adamw(vector_s, vector_new, both, gvec, factor, RATE_VECTOR)
    for z in range(ZO):
        for y in range(2):
            p = z * 2 + y
            for i in range(2):
                grad = big[z, y, i * 64 : i * 64 + 64, :].astype(F32)
                adamw(mlp, mlp_new, (i, everything, slice(p * 128, p * 128 + 128)), grad, factor, RATE_MLP)
            lo, col = (p % 4) * 16, (p // 4) * 128
            place = (slice(lo, lo + 16), slice(col, col + 128))
            grad = big[z, y, 128:144, :].astype(F32)
            adamw(attn, attn_new, (2,) + place, grad, factor, RATE_ATTN)
            for i in range(2):
                grad = late[z, y, i * 16 : i * 16 + 16, :].astype(F32)
                adamw(attn, attn_new, (i,) + place, grad, factor, RATE_ATTN)


def body(zs, points, cotangent, surface_count, volume_count, *state):
    attn, mlp, small, vector = [state[4 * i : 4 * i + 4] for i in range(4)]
    rows = points.shape[0]
    vmem = pl.BlockSpec(memory_space=pltpu.VMEM)
    smem = pl.BlockSpec(memory_space=pltpu.SMEM)
    sd = jax.ShapeDtypeStruct

    def tall(features, dtype=BF):
        return pltpu.VMEM((features, rows), dtype)

    def units(n, depth):
        return pltpu.VMEM((n, 2, 4, ZO, depth, 128), BF)

    line = max(zs, 8)
    scratch = [
        pltpu.SMEM((5, ITEMS), jnp.int32), tall(1, F32), tall(1, F32),
        tall(C), tall(C), tall(C), tall(2 * C), tall(H * G), tall(C), tall(C), tall(FF), tall(FF), tall(C), tall(C),
        tall(C, F32), tall(2 * C),
        pltpu.VMEM((3, C, C), BF), pltpu.VMEM((2, C, FF), BF), pltpu.VMEM((2 * C, C), BF),
        pltpu.VMEM((H * G, C), BF), pltpu.VMEM((C, H * G), BF), pltpu.VMEM((C, C), BF),
        pltpu.VMEM((FF, C), BF), pltpu.VMEM((FF, C), BF),
        pltpu.VMEM((C, 128), F32), pltpu.VMEM((C, 128), F32), pltpu.VMEM((C, 128), F32), pltpu.VMEM((DH, 128), F32),
        units(4, UN), pltpu.VMEM((2, 4, ZO, CB, 128), BF), pltpu.VMEM((2, 4, ZO, CL, 128), BF),
        units(2, DH), units(2, UN), pltpu.VMEM((2, 168, 128), F32), pltpu.VMEM((2, 128, 128), F32),
        pltpu.VMEM((DH, 256), F32),
        pltpu.VMEM((SM, 128), BF), pltpu.VMEM((SM, 128), BF), pltpu.VMEM((4, SM, 128), BF), pltpu.VMEM((zs, SM, 128), BF),
        pltpu.VMEM((zs, 8, 128), F32), pltpu.VMEM((8, 8, 128), F32),
        pltpu.SemaphoreType.DMA((2, 6)), pltpu.SemaphoreType.DMA((8, line)), pltpu.SemaphoreType.DMA((12, line)),
    ]
    for depth in (UN, UN, UN, UN, CB, CL):
        scratch += Reduce.scratch(depth, zs)
    for _ in range(4):
        scratch += Gather.scratch(zs)
    mixed_t, grad_t, big, late, small_sum, norm = pl.pallas_call(
        functools.partial(main_kernel, zs),
        out_shape=[
            sd((C, rows), BF), sd((C, rows), F32), sd((ZO, 2, CB, 128), BF), sd((ZO, 2, CL, 128), BF),
            sd((SM, 128), F32), sd((1, 1), F32),
        ],
        in_specs=[smem, smem] + [vmem] * 6,
        out_specs=[vmem] * 5 + [smem],
        scratch_shapes=scratch,
        compiler_params=pltpu.CompilerParams(collective_id=0, has_side_effects=True, vmem_limit_bytes=60 << 20),
        name="main",
    )(surface_count, volume_count, points.reshape(-1, T, C), cotangent.reshape(-1, T, C), attn[0], mlp[0], small[0], vector[0])

    def news(leaves):
        return [sd(leaves[0].shape, F32)] * 4 + [sd(leaves[0].shape, BF)]

    outs = pl.pallas_call(
        last_kernel,
        out_shape=[sd((rows, C), BF), sd((rows, C), F32)] + news(attn) + news(mlp) + news(small) + news(vector),
        in_specs=[smem, smem] + [vmem] * 5 + [smem] + [vmem] * 16,
        out_specs=[vmem] * 22,
        scratch_shapes=[pltpu.VMEM((rows, C), F32)],
        compiler_params=pltpu.CompilerParams(vmem_limit_bytes=60 << 20),
        name="last",
    )(surface_count, volume_count, mixed_t, grad_t, big, late, small_sum, norm, *attn, *mlp, *small, *vector)
    return tuple(outs[0:2]) + (norm.reshape(()),) + tuple(outs[2:])


def solution(mesh):
    rows = P(("pts", "fsdp"), None)
    split = P(None, "fsdp", None)
    in_specs = (rows,) * 4 + (split,) * 8 + (P(),) * 8
    out_specs = (rows, rows, P()) + (split,) * 10 + (P(),) * 10
    return jax.shard_map(
        functools.partial(body, mesh.shape["pts"] // 2),
        mesh=mesh, in_specs=in_specs, out_specs=out_specs, check_vma=False,
    )
```

```python
import functools
import math

import jax
import jax.numpy as jnp
from jax import lax
from jax.experimental import pallas as pl
from jax.experimental.pallas import tpu as pltpu
from jax.sharding import PartitionSpec as P

C = 256
H = 8
DH = 32
G = 64
FF = 1024
ITEMS = 16
STEP = 5
W = 256
T = 128
BATCH = 8
NORM_EPS = 1e-05
SLICE_EPS = 1e-05
CLIP = 1.0
BETA_ONE = 0.5
BETA_TWO = 0.5
ADAM_EPS = 1e-08
DECAY = 0.01
EMA_RATE = 0.6
RATE_ATTN = 0.04
RATE_MLP = 0.03
RATE_SMALL = 0.4
RATE_VECTOR = 0.3
ZO = 4
UN = 48
CB = 144
CL = 32
SM = 80
MESH = pl.DeviceIdType.MESH
HIGH = lax.Precision.HIGHEST
F32 = jnp.float32
BF = jnp.bfloat16
GELU_A = math.sqrt(2.0 / math.pi)
GELU_B = GELU_A * 0.044715


def nn(a, b, precision=None):
    return lax.dot_general(a, b, (((1,), (0,)), ((), ())), precision=precision, preferred_element_type=F32)


def nt(a, b, precision=None):
    return lax.dot_general(a, b, (((1,), (1,)), ((), ())), precision=precision, preferred_element_type=F32)


def tn(a, b, precision=None):
    return lax.dot_general(a, b, (((0,), (0,)), ((), ())), precision=precision, preferred_element_type=F32)


def iota(shape, dim):
    return lax.broadcasted_iota(jnp.int32, shape, dim)


def tile_of(i, width=W):
    return pl.ds(pl.multiple_of(i * width, width), width)


class Place:
    def __init__(self, zs):
        self.p = lax.axis_index("pts")
        self.f = lax.axis_index("fsdp")
        self.a = self.f % 2
        self.x = self.f // 2
        self.y = self.p % 2
        self.z = self.p // 2
        self.m = self.x * 2 + self.y
        self.zs = zs
        self.core = (self.p, self.f + 1 - 2 * self.a)
        self.xpeer = (self.p, (1 - self.x) * 2 + self.a)
        self.ypeer = (self.z * 2 + 1 - self.y, self.f)
        self.zown = self.z if zs == ZO else jnp.minimum(self.z, ZO - 1)

    def xy(self, k):
        mm = (self.m + k) % 4
        return mm, (self.z * 2 + mm % 2, (mm // 2) * 2 + self.a)

    def xy_other(self, k):
        mm = (self.m + k) % 4
        return mm, (self.z * 2 + mm % 2, (mm // 2) * 2 + 1 - self.a)

    def chips(self):
        return [(k, j) for j in range(self.zs - 1, -1, -1) for k in (3, 2, 1, 0) if k or j]

    def chip(self, k, j):
        mm, zz = (self.m + k) % 4, (self.z + j) % self.zs
        return mm, zz, (zz * 2 + mm % 2, (mm // 2) * 2 + self.a)

    def zl(self, k):
        zz = (self.z + k) % self.zs
        return zz, (zz * 2 + self.y, self.f)

    def barrier(self):
        b = pltpu.get_barrier_semaphore()
        peers = [self.core] + [self.chip(k, j)[2] for k, j in self.chips()]
        peers += [self.xy_other(k)[1] for k in (1, 2, 3)]
        for d in peers:
            pl.semaphore_signal(b, inc=1, device_id=d, device_id_type=MESH)
        pl.semaphore_wait(b, len(peers))

    def owned(self, z, fn):
        if self.zs == ZO:
            fn()
        else:
            pl.when(z < ZO)(fn)


def rcopy(src, dst, ss, rs, dev):
    return pltpu.make_async_remote_copy(
        src_ref=src, dst_ref=dst, send_sem=ss, recv_sem=rs, device_id=dev, device_id_type=MESH
    )


class Reduce:
    def __init__(self, g, src, bufs):
        self.g, self.src = g, src
        self.r1, self.s2, self.r2, self.s3, self.r3, self.sem = bufs
        self.c1, self.c2, self.c3 = {}, [], []

    @staticmethod
    def scratch(rows, zs):
        return [
            pltpu.VMEM((4, ZO, rows, 128), BF),
            pltpu.VMEM((3, ZO, rows, 128), BF),
            pltpu.VMEM((3, ZO, rows, 128), BF),
            pltpu.VMEM((ZO, rows, 128), BF),
            pltpu.VMEM((zs - 1, rows, 128), BF),
            pltpu.SemaphoreType.DMA((6, max(zs, 4))),
        ]

    def core(self, k):
        g = self.g
        mm = (g.m + k) % 4
        c = rcopy(self.src.at[1 - g.a, mm], self.r1.at[mm], self.sem.at[0, k], self.sem.at[1, k], g.core)
        c.start()
        self.c1[k] = c

    def pair(self, k):
        g = self.g
        self.c1[k].wait_recv()
        mm = (g.m + k) % 4
        return self.src[g.a, mm].astype(F32) + self.r1[mm].astype(F32)

    def square(self, k):
        g = self.g
        dev = g.xy(k)[1]
        self.s2[k - 1] = self.pair(k).astype(BF)
        c = rcopy(self.s2.at[k - 1], self.r2.at[k - 1], self.sem.at[2, k - 1], self.sem.at[3, k - 1], dev)
        c.start()
        self.c2.append(c)

    def line(self):
        g = self.g
        acc = self.pair(0)
        for k in (1, 2, 3):
            self.c2[k - 1].wait_recv()
            acc = acc + self.r2[k - 1].astype(F32)
        self.s3[...] = acc.astype(BF)
        for k in range(1, g.zs):
            zz, dev = g.zl(k)
            at = zz if g.zs == ZO else jnp.minimum(zz, ZO - 1)
            c = rcopy(self.s3.at[at], self.r3.at[k - 1], self.sem.at[4, k - 1], self.sem.at[5, k - 1], dev)
            g.owned(zz, c.start)
            self.c3.append(c)

    def result(self):
        g = self.g
        out = self.s3[g.zown].astype(F32)
        for k in range(1, g.zs):
            g.owned(g.z, self.c3[k - 1].wait_recv)
            out = out + self.r3[k - 1].astype(F32)
        return out

    def finish(self):
        g = self.g
        for c in self.c1.values():
            c.wait_send()
        for c in self.c2:
            c.wait_send()
        for k in range(1, g.zs):
            g.owned(g.zl(k)[0], self.c3[k - 1].wait_send)


class Direct:
    def __init__(self, g, src, bufs):
        self.g, self.src = g, src
        self.r1, self.s2, self.r2, self.core_sem, self.chip_sem = bufs
        self.c1, self.c2 = {}, {}

    @staticmethod
    def scratch(rows, zs):
        return [
            pltpu.VMEM((4, ZO, rows, 128), BF),
            pltpu.VMEM((4, ZO, rows, 128), BF),
            pltpu.VMEM((4, zs, rows, 128), BF),
            pltpu.SemaphoreType.DMA((2, 4)),
            pltpu.SemaphoreType.DMA((2, 4, zs)),
        ]

    def core(self, k):
        g = self.g
        mm = (g.m + k) % 4
        c = rcopy(self.src.at[1 - g.a, mm], self.r1.at[mm], self.core_sem.at[0, k], self.core_sem.at[1, k], g.core)
        c.start()
        self.c1[k] = c

    def chips(self):
        g = self.g
        for k in (3, 2, 1, 0):
            self.c1[k].wait_recv()
            mm = (g.m + k) % 4
            self.s2[k] = (self.src[g.a, mm].astype(F32) + self.r1[mm].astype(F32)).astype(BF)
        for k, j in g.chips():
            _, zz, dev = g.chip(k, j)
            at = zz if g.zs == ZO else jnp.minimum(zz, ZO - 1)
            c = rcopy(self.s2.at[k, at], self.r2.at[k, j], self.chip_sem.at[0, k, j], self.chip_sem.at[1, k, j], dev)
            g.owned(zz, c.start)
            self.c2[k, j] = (zz, c)

    def result(self):
        g = self.g
        out = self.s2[0, g.zown].astype(F32)
        for k, j in reversed(g.chips()):
            g.owned(g.z, self.c2[k, j][1].wait_recv)
            out = out + self.r2[k, j].astype(F32)
        return out

    def finish(self):
        for c in self.c1.values():
            c.wait_send()
        for zz, c in self.c2.values():
            self.g.owned(zz, c.wait_send)


class Gather:
    def __init__(self, g, out, bufs):
        self.g, self.out = g, out
        self.chip_sem, self.core_sem = bufs
        self.cz, self.cc = {}, []

    @staticmethod
    def scratch(zs):
        return [pltpu.SemaphoreType.DMA((2, 4, zs)), pltpu.SemaphoreType.DMA((2, 4))]

    def start(self):
        g = self.g
        own = self.out.at[g.a, g.m, g.zown]
        for k, j in g.chips():
            c = rcopy(own, own, self.chip_sem.at[0, k, j], self.chip_sem.at[1, k, j], g.chip(k, j)[2])
            g.owned(g.z, c.start)
            self.cz[k, j] = c

    def to_core(self):
        g = self.g
        for k in range(4):
            for j in range(g.zs):
                if k or j:
                    g.owned((g.z - j + g.zs) % g.zs, self.cz[k, j].wait_recv)
            r = self.out.at[g.a, (g.m - k + 4) % 4]
            c = rcopy(r, r, self.core_sem.at[0, k], self.core_sem.at[1, k], g.core)
            c.start()
            self.cc.append(c)

    def done(self):
        for c in self.cc:
            c.wait_recv()

    def finish(self):
        g = self.g
        for c in self.cz.values():
            g.owned(g.z, c.wait_send)
        for c in self.cc:
            c.wait_send()


def counts(surface, volume):
    at = surface[0, 0] * 0
    starts, surfs, sizes = [], [], []
    for b in range(ITEMS):
        starts.append(at)
        surfs.append(surface[0, b])
        sizes.append(surface[0, b] + volume[0, b])
        at = at + sizes[b]
    return starts, surfs, sizes, at


def column(row):
    return jnp.broadcast_to(row, (128, row.shape[1])).T


def wide(col):
    return jnp.concatenate([col, col], axis=1)


def norm_stats(v):
    mean = jnp.mean(v, axis=0, keepdims=True)
    centred = v - mean
    var = jnp.mean(centred * centred, axis=0, keepdims=True)
    scale = lax.rsqrt(var + NORM_EPS)
    return centred * scale, scale


def halves():
    lane = iota((1, 128), 1)
    return (lane < G).astype(F32).astype(BF), (lane >= G).astype(F32).astype(BF)


def spread_unit(unit):
    low, high = halves()
    return jnp.concatenate([unit * low, unit * high], axis=0)


def take_units(full):
    low = iota((DH, 128), 1) < G
    one = jnp.where(low, full[0:DH, 0:128], full[DH : 2 * DH, 0:128])
    two = jnp.where(low, full[2 * DH : 3 * DH, 128:256], full[3 * DH : 4 * DH, 128:256])
    return one, two


def item_units(fields, probs):
    left = jnp.concatenate([fields, jnp.ones((16, T), BF)], axis=0)
    full = nt(left, probs)
    one, two = take_units(full)
    one = jnp.concatenate([one, full[128:144, 0:128]], axis=0)
    two = jnp.concatenate([two, full[128:144, 128:256]], axis=0)
    return one.astype(BF), two.astype(BF)


def slice_columns(small):
    low = small[:, 0:128].astype(BF)
    pick = (iota((H * G, 128), 0) % G == iota((H * G, 128), 1)).astype(F32).astype(BF)
    rows = nt(pick, low).astype(BF)
    place = (iota((DH, C), 1) % DH == iota((DH, C), 0)).astype(F32).astype(BF)
    full = nn(rows, place)
    keep = iota((H * G, C), 0) // G == iota((H * G, C), 1) // DH
    return jnp.where(keep, full, 0.0).astype(BF)


def same_head():
    return iota((2 * G, 2 * G), 0) // G == iota((2 * G, 2 * G), 1) // G


def main_kernel(
    zs, surface, volume, points_hbm, cot_hbm, attn_w, mlp_w, small, vector,
    mixed_hbm, grad_hbm, big, late, small_sum, norm_out, points, cotangent, mixed, points_grad, load_sem,
    bounds, surf, keep, xt, cot_t, normed, mid, probs, spread, norm_two, active, d_hidden, d_branch, d_spread, d_mid,
    d_both, d_logits, wat, wml, wxf, slicew, slicet, wot, wint, woutt, gain_one, gain_two, embed_acc,
    src, src_big, src_late, slice_out, d_slice, saved, attention, maps_acc,
    small_src, sr1, sr2, sr3, line_late, sqb, weight_sem, big_sem, y_sem, sem, *sems,
):
    g = Place(zs)
    rows = ITEMS * T
    red = [Direct(g, src.at[i], sems[5 * i : 5 * i + 5]) for i in range(4)]
    red_big = Reduce(g, src_big, sems[20:26])
    red_late = Reduce(g, src_late, sems[26:32])
    gat = [Gather(g, slice_out.at[i], sems[32 + 2 * i : 34 + 2 * i]) for i in range(2)]
    gat += [Gather(g, d_slice.at[i], sems[36 + 2 * i : 38 + 2 * i]) for i in range(2)]

    own = pl.ds(pl.multiple_of(g.f * 64, 64), 64)
    other = pl.ds(pl.multiple_of(((1 - g.x) * 2 + g.a) * 64, 64), 64)
    wat[:, own, :] = attn_w[...].astype(BF)
    load_points = pltpu.make_async_copy(points_hbm, points, load_sem.at[0])
    load_cot = pltpu.make_async_copy(cot_hbm, cotangent, load_sem.at[1])
    load_points.start()
    g.barrier()

    def weight(ref, lead, at, i, dev):
        r = ref.at[lead, at, :]
        return rcopy(r, r, weight_sem.at[0, i], weight_sem.at[1, i], dev)

    two, three, all_mlp = pl.ds(0, 2), pl.ds(2, 1), pl.ds(0, 2)
    a_x, a_c, a_f = weight(wat, two, own, 0, g.xpeer), weight(wat, two, own, 1, g.core), weight(wat, two, other, 2, g.core)
    o_x, o_c, o_f = weight(wat, three, own, 3, g.xpeer), weight(wat, three, own, 4, g.core), weight(wat, three, other, 5, g.core)
    m_x, m_c, m_f = weight(wml, all_mlp, own, 6, g.xpeer), weight(wml, all_mlp, own, 7, g.core), weight(wml, all_mlp, other, 8, g.core)
    a_x.start()
    a_c.start()
    load_cot.start()
    wml[:, own, :] = mlp_w[...].astype(BF)
    load_points.wait()

    starts, surfs, sizes, total = counts(surface, volume)
    lane = iota((1, T), 1)
    for b in range(ITEMS):
        shift = total + b * T - starts[b] - sizes[b]
        bounds[0, b] = starts[b]
        bounds[1, b] = sizes[b]
        bounds[2, b] = shift
        bounds[3, b] = jnp.minimum(lax.div(starts[b], jnp.int32(T)), ITEMS - 2)
        bounds[4, b] = jnp.minimum(lax.div(shift, jnp.int32(T)), ITEMS - 2)
        surf[:, b * T : b * T + T] = (lane < surfs[b]).astype(F32)
        keep[:, b * T : b * T + T] = (lane < sizes[b]).astype(F32)
    gain_a = column(vector[0:1, :])
    gain_b = wide(column(vector[1:2, :]))
    embed = column(vector[2:3, :])
    embed2 = wide(embed)

    def packed(ref, b):
        t, u, size = bounds[3, b], bounds[4, b], bounds[1, b]
        to, row = iota((T, 2 * T), 0), iota((T, 2 * T), 1)
        one = (row + t * T == to + bounds[0, b]) & (to < size)
        two = (row + u * T == to + bounds[2, b]) & (to >= size)
        pick = jnp.concatenate([one.astype(F32).astype(BF), two.astype(F32).astype(BF)], axis=1)
        return nn(pick, jnp.concatenate([ref[i] for i in (t, t + 1, u, u + 1)], axis=0)).T

    def pack_item(b, carry):
        at = tile_of(b, T)
        field = packed(points, b)
        xt[:, at] = field.astype(BF)
        unit, _ = norm_stats(field + embed * surf[:, at])
        normed[:, at] = (unit * gain_a).astype(BF)
        return carry

    def pack_cot(b, carry):
        cot_t[:, tile_of(b, T)] = packed(cotangent, b).astype(BF)
        return carry

    lax.fori_loop(0, ITEMS, pack_item, 0, unroll=8)
    a_x.wait_recv()
    a_f.start()
    for c in (m_x, o_x, m_c, o_c):
        c.start()
    slicew[...] = slice_columns(small)
    for r in (gain_one, gain_two, embed_acc, maps_acc):
        r[...] = jnp.zeros_like(r)

    def turned(v):
        return v.astype(F32).T.astype(BF)

    a_c.wait_recv()
    a_f.wait_recv()
    wxf[0:C, :] = turned(wat[0])
    wxf[C : 2 * C, :] = turned(wat[1])

    def soft_tile(i, carry):
        at = tile_of(i)
        both = nn(wxf[...], normed[:, at]).astype(BF)
        mid[:, at] = both
        logits = nn(slicew[...], both[0:C]).reshape(H, G, W)
        top = jnp.max(logits, axis=1, keepdims=True)
        e = jnp.exp(logits - top)
        scale = keep[:, at] / jnp.sum(e, axis=1, keepdims=True)
        probs[:, at] = (e * scale).reshape(H * G, W).astype(BF)
        return carry

    def sums(r, batch, fields, off):
        for half in range(2):
            for k in (1, 2, 3, 0):
                mm = (g.m + k) % 4
                core = (1 - g.a) if half == 0 else g.a
                at = tile_of(batch * BATCH + core * 4 + mm, T)
                for q in range(2):
                    both = item_units(fields[off + q * 128 : off + q * 128 + 128, at], probs[q * 256 : q * 256 + 256, at])
                    for i in range(2):
                        r.src[core, mm, 2 * q + i] = both[i]
                if half == 0:
                    r.core(k)

    def attend(batch):
        unit = red[batch].result()
        raw, scale = unit[0:DH], unit[DH : DH + 8] + SLICE_EPS
        token = raw / scale[0:1]
        qkv = tn(small[...], token, HIGH)
        query, key, value = qkv[64:96], qkv[96:128], qkv[128:160]
        scores = tn(key, query, HIGH) / math.sqrt(DH)
        scores = jnp.where(same_head(), scores, -jnp.inf)
        top = jnp.max(scores, axis=0, keepdims=True)
        e = jnp.exp(scores - top)
        weights = e / jnp.sum(e, axis=0, keepdims=True)
        slice_out[batch, g.a, g.m, g.zown] = nn(value, weights, HIGH).astype(BF)
        gat[batch].start()
        saved[batch, 0:32] = token
        saved[batch, 32:128] = qkv[64:160]
        saved[batch, 128:160] = raw
        saved[batch, 160:168] = scale
        attention[batch] = weights

    def attend_back(batch):
        unit = red[2 + batch].result()
        d_out = unit[0:DH]
        s = saved.at[batch]
        token, query, key, value = s[0:32], s[32:64], s[64:96], s[96:128]
        raw, scale = s[128:160], s[160:161]
        weights = attention[batch]
        d_value = nt(d_out, weights, HIGH)
        d_weights = tn(value, d_out, HIGH)
        d_scores = weights * (d_weights - jnp.sum(weights * d_weights, axis=0, keepdims=True))
        d_query = nn(key, d_scores, HIGH) / math.sqrt(DH)
        d_key = nt(query, d_scores, HIGH) / math.sqrt(DH)
        d_maps = jnp.concatenate([jnp.zeros((64, T), F32), d_query, d_key, d_value], axis=0)
        d_token = nn(small[...], d_maps, HIGH)
        d_total = -jnp.sum(d_token * raw, axis=0, keepdims=True) / (scale * scale)
        tot = jnp.broadcast_to(d_total, (16, T))
        d_slice[batch, g.a, g.m, g.zown] = jnp.concatenate([d_token / scale, tot], axis=0).astype(BF)
        gat[2 + batch].start()
        part = nt(token, jnp.concatenate([d_maps, jnp.zeros((96, T), F32)], axis=0), HIGH)
        if zs != ZO:
            part = jnp.where(g.z < ZO, part, 0.0)
        maps_acc[...] += part

    lax.fori_loop(0, 4, soft_tile, 0, unroll=2)
    sums(red[0], 0, mid, C)
    lax.fori_loop(4, 6, soft_tile, 0, unroll=2)
    red[0].chips()
    lax.fori_loop(6, 8, soft_tile, 0, unroll=2)
    sums(red[1], 1, mid, C)
    red[1].chips()
    m_x.wait_recv()
    m_f.start()
    o_x.wait_recv()
    o_f.start()
    load_cot.wait()
    slicet[...] = turned(slicew[...])
    attend(0)
    for c in (m_c, o_c, m_f, o_f):
        c.wait_recv()
    wot[...] = turned(wat[2])
    for j in range(FF // 256):
        wint[j * 256 : j * 256 + 256, :] = turned(wml[0, :, j * 256 : j * 256 + 256])
    attend(1)
    for j in range(FF // 256):
        woutt[j * 256 : j * 256 + 256, :] = turned(wml[1, :, j * 256 : j * 256 + 256])
    gat[0].to_core()
    lax.fori_loop(0, ITEMS, pack_cot, 0, unroll=4)
    gat[0].done()

    def spread_item(b, carry):
        at = tile_of(b, T)
        batch = b // BATCH
        core = (b % BATCH) // 4
        for i in range(4):
            part = nn(spread_unit(slice_out[batch, core, b % 4, i]), probs[i * 128 : i * 128 + 128, at])
            spread[i * 64 : i * 64 + 64, at] = part.astype(BF)
        return carry

    def mlp_tile(i, carry):
        at = tile_of(i)
        middle = xt[:, at].astype(F32) + embed2 * surf[:, at] + nn(wot[...], spread[:, at])
        unit, scale = norm_stats(middle)
        two = (unit * gain_b).astype(BF)
        norm_two[:, at] = two
        ctb = cot_t[:, at]
        for j in range(FF // 256):
            hid = pl.ds(j * 256, 256)
            x = nn(wint[hid, :], two)
            da = nn(woutt[hid, :], ctb)
            sq = x * x
            t = jnp.tanh(x * (GELU_A + GELU_B * sq))
            s = 0.5 + 0.5 * t
            act = (x * s).astype(BF)
            slope = s + (x * (s - s * s)) * (2.0 * GELU_A + 6.0 * GELU_B * sq)
            dh = (slope * da).astype(BF)
            active[hid, at] = act
            d_hidden[hid, at] = dh
        d_two = nn(wml[0], d_hidden[:, at])
        mixed[at, :] = (middle + nn(wml[1], active[:, at])).T.astype(BF)
        gs = d_two * unit
        gain_two[...] += gs[:, 0:128] + gs[:, 128:256]
        du = d_two * gain_b
        m1 = jnp.mean(du, axis=0, keepdims=True)
        m2 = jnp.mean(du * unit, axis=0, keepdims=True)
        dm = ctb.astype(F32) + scale * (du - m1 - unit * m2)
        d_mid[:, at] = dm
        db = dm.astype(BF)
        d_branch[:, at] = db
        d_spread[:, at] = nn(wat[2], db).astype(BF)
        return carry

    lax.fori_loop(0, BATCH, spread_item, 0, unroll=8)
    gat[1].to_core()
    lax.fori_loop(0, 2, mlp_tile, 0, unroll=2)
    lax.fori_loop(2, 4, mlp_tile, 0, unroll=2)
    sums(red[2], 0, d_spread, 0)
    gat[1].done()
    lax.fori_loop(BATCH, ITEMS, spread_item, 0, unroll=8)
    red[2].chips()
    lax.fori_loop(4, 6, mlp_tile, 0, unroll=2)
    lax.fori_loop(6, 8, mlp_tile, 0, unroll=2)
    sums(red[3], 1, d_spread, 0)
    stores = [pltpu.make_async_copy(mixed, mixed_hbm, load_sem.at[2])]
    stores[0].start()
    attend_back(0)
    red[3].chips()

    def put(f, p, lo, value):
        src_big[f % 2, (f // 2) * 2 + p % 2, p // 2, lo : lo + value.shape[0], :] = value

    def grad_mlp(which, left, right):
        for j in range(FF // 256):
            grad = nt(left[...], right[j * 256 : j * 256 + 256, :]).astype(BF)
            for f in range(4):
                for i in range(2):
                    put(f, 2 * j + i, which * 64, grad[f * 64 : f * 64 + 64, i * 128 : i * 128 + 128])

    grad_mlp(0, norm_two, d_hidden)
    grad_mlp(1, cot_t, active)
    grad = nt(spread[...], d_branch[...]).astype(BF)
    for f in range(4):
        for p in range(8):
            lo = f * 64 + (p % 4) * 16
            put(f, p, 128, grad[lo : lo + 16, (p // 4) * 128 : (p // 4) * 128 + 128])
    for k in (1, 2, 3, 0):
        red_big.core(k)
    gat[2].to_core()
    attend_back(1)
    for k in (1, 2, 3):
        red_big.square(k)
    gat[2].done()
    block = iota((1, 2 * T), 1)
    block = jnp.where(block < T, block // DH % 2, jnp.where(block == T, 0, jnp.where(block == T + 16, 1, 2)))
    even, odd = [(block == i).astype(F32).astype(BF) for i in range(2)]
    ones_rows = jnp.ones((T, T), BF)
    blank = jnp.zeros((T - 32, T), BF)

    def back_item(b, carry):
        at = tile_of(b, T)
        batch = b // BATCH
        core = (b % BATCH) // 4
        for q in range(2):
            outs = [slice_out[batch, core, b % 4, 2 * q + i] for i in range(2)]
            ds = [d_slice[batch, core, b % 4, 2 * q + i] for i in range(2)]
            parts = outs + [d[0:DH] for d in ds] + [d[DH:UN] for d in ds] + [blank]
            turn = jnp.concatenate(parts, axis=0).T
            for one in range(2):
                rows_of = [4 * q + one, 4 * q + 2 + one]
                left = turn[one * G : one * G + G]
                left = jnp.concatenate([left * even, left * odd], axis=0)
                fields = [d_spread[h * DH : h * DH + DH, at] for h in rows_of]
                fields += [mid[C + h * DH : C + h * DH + DH, at] for h in rows_of]
                dp = nn(left, jnp.concatenate(fields + [ones_rows], axis=0)).reshape(2, G, T)
                pf = jnp.stack([probs[h * G : h * G + G, at] for h in rows_of]).astype(F32)
                back = pf * (dp - jnp.sum(pf * dp, axis=1, keepdims=True))
                for i, h in enumerate(rows_of):
                    d_logits[h * G : h * G + G, at] = back[i].astype(BF)
            for i in range(2):
                k = 2 * q + i
                part = nn(spread_unit(ds[i][0:DH]), probs[k * 128 : k * 128 + 128, at])
                d_both[C + k * 64 : C + k * 64 + 64, at] = part.astype(BF)
        return carry

    def back_tile(i, carry):
        at = tile_of(i)
        d_norm = nn(wat[0], d_both[0:C, at]) + nn(wat[1], d_both[C : 2 * C, at])
        sf = surf[:, at]
        unit, scale = norm_stats(xt[:, at].astype(F32) + embed2 * sf)
        gs = d_norm * unit
        gain_one[...] += gs[:, 0:128] + gs[:, 128:256]
        du = d_norm * wide(gain_a)
        m1 = jnp.mean(du, axis=0, keepdims=True)
        m2 = jnp.mean(du * unit, axis=0, keepdims=True)
        pg = d_mid[:, at] + scale * (du - m1 - unit * m2)
        es = pg * sf
        embed_acc[...] += es[:, 0:128] + es[:, 128:256]
        points_grad[at, :] = pg.T
        return carry

    def mid_tile(i, carry):
        at = tile_of(i)
        d_both[0:C, at] = nn(slicet[...], d_logits[:, at]).astype(BF)
        return carry

    lax.fori_loop(0, BATCH, back_item, 0, unroll=4)
    red_big.line()
    gat[3].to_core()
    lax.fori_loop(0, 4, mid_tile, 0, unroll=4)
    lax.fori_loop(0, 4, back_tile, 0, unroll=4)
    half_rows = [pl.ds(0, rows // 2), pl.ds(rows // 2, rows // 2)]

    def store_half(i):
        c = pltpu.make_async_copy(points_grad.at[half_rows[i], :], grad_hbm.at[half_rows[i], :], load_sem.at[3 + i])
        c.start()
        stores.append(c)

    store_half(0)
    whole = red_big.result().astype(BF)
    big[g.zown, g.y] = whole

    def copies(ref, base):
        part = ref.at[g.zown, g.y]
        cz = []
        for k in range(1, zs):
            c = rcopy(part, part, big_sem.at[base, k], big_sem.at[base + 1, k], g.zl(k)[1])
            g.owned(g.z, c.start)
            cz.append(c)
        return cz

    def to_y(ref, sem):
        cy = []
        for z in range(ZO):
            r = ref.at[z, g.y]
            c = rcopy(r, r, sem.at[0, z], sem.at[1, z], g.ypeer)
            c.start()
            cy.append(c)
        return cy

    big_z = copies(big, 0)
    gat[3].done()
    lax.fori_loop(BATCH, ITEMS, back_item, 0, unroll=4)
    lax.fori_loop(4, 8, mid_tile, 0, unroll=4)

    grads = [nt(normed[...], d_both[i * C : i * C + C, :]).astype(BF) for i in range(2)]
    for f in range(4):
        for p in range(8):
            lo, col = f * 64 + (p % 4) * 16, (p // 4) * 128
            both = [v[lo : lo + 16, col : col + 128] for v in grads]
            src_late[f % 2, (f // 2) * 2 + p % 2, p // 2] = jnp.concatenate(both, axis=0)
    for k in (1, 2, 3, 0):
        red_late.core(k)
    fold = jnp.zeros((DH, 128), F32)
    for i in range(4):
        part = nt(mid[i * 64 : i * 64 + 64, :], d_logits[i * 128 : i * 128 + 128, :])
        fold = fold + jnp.where(iota((DH, 128), 1) < G, part[0:DH], part[DH : 2 * DH])
    fold = jnp.where(iota((32, 128), 1) < G, fold + pltpu.roll(fold, G, 1), 0.0)
    for k in (1, 2, 3):
        red_late.square(k)
    for k in range(1, zs):
        g.owned((g.z - k + zs) % zs, big_z[k - 1].wait_recv)
    big_y = to_y(big, y_sem.at[0])
    lax.fori_loop(4, 8, back_tile, 0, unroll=4)
    store_half(1)

    ones = jnp.ones((8, 128), F32)
    line = [nt(ones, r[...], HIGH) for r in (gain_one, gain_two, embed_acc)]
    pick = iota((8, 256), 0)
    vec = jnp.where(pick == 0, line[0], jnp.where(pick == 1, line[1], jnp.where(pick == 2, line[2], 0.0)))
    small_src[0:32] = (fold + maps_acc[:, 0:128]).astype(BF)
    small_src[32:64] = maps_acc[:, 128:256].astype(BF)
    small_src[64:80] = jnp.concatenate([vec[:, 0:128], vec[:, 128:256]], axis=0).astype(BF)
    cs = [rcopy(small_src, sr1, sem.at[0, 0], sem.at[1, 0], g.core)]
    cs[0].start()

    acc = red_late.pair(0)
    for k in (1, 2, 3):
        red_late.c2[k - 1].wait_recv()
        acc = acc + red_late.r2[k - 1].astype(F32)
    line_late[g.z] = acc.astype(BF)
    line_copies = []
    for k in range(1, zs):
        c = rcopy(line_late.at[g.z], line_late.at[g.z], sem.at[4, k], sem.at[5, k], g.zl(k)[1])
        c.start()
        line_copies.append(c)
    cs[0].wait_recv()
    sr2[g.m] = (small_src[...].astype(F32) + sr1[...].astype(F32)).astype(BF)
    for k in (1, 2, 3):
        c = rcopy(sr2.at[g.m], sr2.at[g.m], sem.at[0, k], sem.at[1, k], g.xy(k)[1])
        c.start()
        cs.append(c)
    bigs = big[:, g.y].astype(F32).reshape(ZO * CB // 8, 8, 128)
    squares = jnp.sum(bigs * bigs, axis=0)
    for c in line_copies:
        c.wait_recv()
    acc = line_late[0].astype(F32)
    for z in range(1, zs):
        acc = acc + line_late[z].astype(F32)
    acc = acc.astype(BF)
    late[:, g.y] = acc
    mine = acc.astype(F32).reshape(ZO * CL // 8, 8, 128)
    here = g.a * 4 + g.m
    sqb[here] = squares + jnp.sum(mine * mine, axis=0)
    sq_copies = []
    for k in range(1, 8):
        dev = g.core if k == 4 else g.xy(k)[1] if k < 4 else g.xy_other(k - 4)[1]
        c = rcopy(sqb.at[here], sqb.at[here], sem.at[10, k], sem.at[11, k], dev)
        c.start()
        sq_copies.append(c)
    late_y = to_y(late, y_sem.at[1])
    for c in cs[1:4]:
        c.wait_recv()
    total = sr2[0].astype(F32)
    for m in range(1, 4):
        total = total + sr2[m].astype(F32)
    sr3[g.z] = total.astype(BF)
    for k in range(1, zs):
        c = rcopy(sr3.at[g.z], sr3.at[g.z], sem.at[2, k], sem.at[3, k], g.zl(k)[1])
        c.start()
        cs.append(c)
    for c in big_y + late_y + cs[4:]:
        c.wait_recv()
    total = sr3[0].astype(F32)
    for z in range(1, zs):
        total = total + sr3[z].astype(F32)
    small_sum[...] = total
    for c in sq_copies:
        c.wait_recv()
    sq = sqb[0]
    for i in range(1, 8):
        sq = sq + sqb[i]
    norm_out[0, 0] = jnp.sqrt(jnp.sum(sq) + jnp.sum(total * total))

    for c in cs + line_copies + sq_copies + big_y + late_y + [a_x, a_c, a_f, o_x, o_c, o_f, m_x, m_c, m_f]:
        c.wait_send()
    for c in stores:
        c.wait()
    for c in big_z:
        g.owned(g.z, c.wait_send)
    for c in red_late.c1.values():
        c.wait_send()
    for c in red_late.c2:
        c.wait_send()
    for r in red + [red_big] + gat:
        r.finish()


def adamw(state, new, sl, grad, factor, rate):
    weight, first, second, average = [r[sl] for r in state]
    clipped = grad * factor
    first_new = BETA_ONE * first + (1.0 - BETA_ONE) * clipped
    second_new = BETA_TWO * second + (1.0 - BETA_TWO) * clipped * clipped
    first_hat = first_new / (1.0 - BETA_ONE**STEP)
    second_hat = second_new / (1.0 - BETA_TWO**STEP)
    new_weight = weight - rate * (first_hat / (jnp.sqrt(second_hat) + ADAM_EPS) + DECAY * weight)
    average_new = EMA_RATE * average + (1.0 - EMA_RATE) * new_weight
    for r, v in zip(new, (new_weight, first_new, second_new, average_new, new_weight.astype(BF))):
        r[sl] = v


def last_kernel(surface, volume, norm, mixed_p, grad_p, big, late, small_sum, *refs):
    hbm_states, hbm_outs = refs[0:16], refs[16:38]
    states, news = refs[38:54], refs[54:74]
    rows_in, mixed_rows, mixed_low, grad_rows, in_sem, out_sem = refs[74:]
    rows = mixed_low.shape[0]
    ins = [pltpu.make_async_copy(h, v, in_sem.at[i]) for i, (h, v) in enumerate(zip(hbm_states, states))]
    gp = pltpu.make_async_copy(grad_p, rows_in, in_sem.at[16])
    gp.start()
    for c in ins:
        c.start()
    starts, _, sizes, total = counts(surface, volume)

    row = iota((T + 8, 1), 0)

    def place(source, out):
        blank = jnp.zeros((8, C), F32)

        def moved(b, base):
            first = pl.multiple_of(lax.div(base, jnp.int32(8)) * 8, 8)
            tile = jnp.concatenate([source[b * T : b * T + T, :].astype(F32), blank], axis=0)
            return first, base - first, pltpu.roll(tile, base - first, 0)

        for b in range(ITEMS):
            first, off, tile = moved(b, starts[b])
            head = pl.ds(first, 8)
            out[head, :] = jnp.where(row[0:8] >= off, tile[0:8], out[head, :])
            out[pl.ds(pl.multiple_of(first + 8, 8), T), :] = tile[8:]
        for b in range(ITEMS):
            first, off, tile = moved(b, total + b * T - starts[b] - sizes[b])
            here = pl.ds(first, T + 8)
            out[here, :] = jnp.where(row >= sizes[b] + off, tile, out[here, :])

    gp.wait()
    place(rows_in, grad_rows)
    outs = [pltpu.make_async_copy(grad_rows.at[pl.ds(0, rows), :], hbm_outs[1], out_sem.at[1])]
    outs[0].start()
    place(mixed_p, mixed_rows)
    mixed_low[...] = mixed_rows[0:rows, :].astype(BF)
    outs.append(pltpu.make_async_copy(mixed_low, hbm_outs[0], out_sem.at[0]))
    outs[1].start()

    attn, mlp, small_s, vector_s = [states[4 * i : 4 * i + 4] for i in range(4)]
    attn_new, mlp_new, small_new, vector_new = [news[5 * i : 5 * i + 5] for i in range(4)]
    factor = jnp.minimum(1.0, CLIP / norm[0, 0])
    everything = slice(None)
    both = (everything, everything)
    for c in ins:
        c.wait()
    for z in range(ZO):
        for y in range(2):
            p = z * 2 + y
            for i in range(2):
                grad = big[z, y, i * 64 : i * 64 + 64, :].astype(F32)
                adamw(mlp, mlp_new, (i, everything, slice(p * 128, p * 128 + 128)), grad, factor, RATE_MLP)

    def send(first, count):
        for i in range(first, first + count):
            c = pltpu.make_async_copy(news[i], hbm_outs[2 + i], out_sem.at[2 + i])
            c.start()
            outs.append(c)

    send(5, 5)
    for z in range(ZO):
        for y in range(2):
            p = z * 2 + y
            lo, col = (p % 4) * 16, (p // 4) * 128
            at = (slice(lo, lo + 16), slice(col, col + 128))
            grad = big[z, y, 128:144, :].astype(F32)
            adamw(attn, attn_new, (2,) + at, grad, factor, RATE_ATTN)
            for i in range(2):
                grad = late[z, y, i * 16 : i * 16 + 16, :].astype(F32)
                adamw(attn, attn_new, (i,) + at, grad, factor, RATE_ATTN)
    send(0, 5)
    gsmall = jnp.concatenate([small_sum[0:32, :], small_sum[32:64, :]], axis=1)[:, 0:160]
    adamw(small_s, small_new, both, gsmall, factor, RATE_SMALL)
    gvec = jnp.concatenate([small_sum[64:72, :], small_sum[72:80, :]], axis=1)[0:3, :]
    adamw(vector_s, vector_new, both, gvec, factor, RATE_VECTOR)
    send(10, 10)
    for c in outs:
        c.wait()


def body(zs, points, cotangent, surface_count, volume_count, *state):
    attn, mlp, small, vector = [state[4 * i : 4 * i + 4] for i in range(4)]
    rows = points.shape[0]
    vmem = pl.BlockSpec(memory_space=pltpu.VMEM)
    smem = pl.BlockSpec(memory_space=pltpu.SMEM)
    hbm = pl.BlockSpec(memory_space=pl.ANY)
    sd = jax.ShapeDtypeStruct

    def tall(features, dtype=BF):
        return pltpu.VMEM((features, rows), dtype)

    def units(n, depth):
        return pltpu.VMEM((n, 2, 4, ZO, depth, 128), BF)

    line = max(zs, 8)
    scratch = [
        pltpu.VMEM((rows // T, T, C), BF), pltpu.VMEM((rows // T, T, C), BF), pltpu.VMEM((rows, C), BF),
        pltpu.VMEM((rows, C), F32), pltpu.SemaphoreType.DMA((5,)),
        pltpu.SMEM((5, ITEMS), jnp.int32), tall(1, F32), tall(1, F32),
        tall(C), tall(C), tall(C), tall(2 * C), tall(H * G), tall(C), tall(C), tall(FF), tall(FF), tall(C), tall(C),
        tall(C, F32), tall(2 * C), tall(H * G),
        pltpu.VMEM((3, C, C), BF), pltpu.VMEM((2, C, FF), BF), pltpu.VMEM((2 * C, C), BF),
        pltpu.VMEM((H * G, C), BF), pltpu.VMEM((C, H * G), BF), pltpu.VMEM((C, C), BF),
        pltpu.VMEM((FF, C), BF), pltpu.VMEM((FF, C), BF),
        pltpu.VMEM((C, 128), F32), pltpu.VMEM((C, 128), F32), pltpu.VMEM((C, 128), F32),
        units(4, UN), pltpu.VMEM((2, 4, ZO, CB, 128), BF), pltpu.VMEM((2, 4, ZO, CL, 128), BF),
        units(2, DH), units(2, UN), pltpu.VMEM((2, 168, 128), F32), pltpu.VMEM((2, 128, 128), F32),
        pltpu.VMEM((DH, 256), F32),
        pltpu.VMEM((SM, 128), BF), pltpu.VMEM((SM, 128), BF), pltpu.VMEM((4, SM, 128), BF), pltpu.VMEM((zs, SM, 128), BF),
        pltpu.VMEM((zs, ZO, CL, 128), BF), pltpu.VMEM((8, 8, 128), F32),
        pltpu.SemaphoreType.DMA((2, 9)), pltpu.SemaphoreType.DMA((2, line)), pltpu.SemaphoreType.DMA((2, 2, ZO)),
        pltpu.SemaphoreType.DMA((12, line)),
    ]
    for _ in range(4):
        scratch += Direct.scratch(UN, zs)
    for depth in (CB, CL):
        scratch += Reduce.scratch(depth, zs)
    for _ in range(4):
        scratch += Gather.scratch(zs)
    mixed_p, grad_p, big, late, small_sum, norm = pl.pallas_call(
        functools.partial(main_kernel, zs),
        out_shape=[
            sd((rows, C), BF), sd((rows, C), F32), sd((ZO, 2, CB, 128), BF), sd((ZO, 2, CL, 128), BF),
            sd((SM, 128), F32), sd((1, 1), F32),
        ],
        in_specs=[smem, smem, hbm, hbm] + [vmem] * 4,
        out_specs=[hbm, hbm] + [vmem] * 3 + [smem],
        scratch_shapes=scratch,
        compiler_params=pltpu.CompilerParams(collective_id=0, has_side_effects=True, vmem_limit_bytes=60 << 20),
        name="main",
    )(surface_count, volume_count, points.reshape(-1, T, C), cotangent.reshape(-1, T, C), attn[0], mlp[0], small[0], vector[0])

    def news(leaves):
        return [sd(leaves[0].shape, F32)] * 4 + [sd(leaves[0].shape, BF)]

    everything = news(attn) + news(mlp) + news(small) + news(vector)
    outs = pl.pallas_call(
        last_kernel,
        out_shape=[sd((rows, C), BF), sd((rows, C), F32)] + everything,
        in_specs=[smem, smem, smem, vmem, hbm, vmem, vmem, vmem] + [hbm] * 16,
        out_specs=[hbm] * 22,
        scratch_shapes=[pltpu.VMEM(v.shape, v.dtype) for v in state]
        + [pltpu.VMEM(v.shape, v.dtype) for v in everything]
        + [
            pltpu.VMEM((rows, C), F32), pltpu.VMEM((rows + T, C), F32), pltpu.VMEM((rows, C), BF),
            pltpu.VMEM((rows + T, C), F32), pltpu.SemaphoreType.DMA((17,)), pltpu.SemaphoreType.DMA((22,)),
        ],
        compiler_params=pltpu.CompilerParams(vmem_limit_bytes=60 << 20),
        name="last",
    )(surface_count, volume_count, norm, mixed_p, grad_p, big, late, small_sum, *state)
    return tuple(outs[0:2]) + (norm.reshape(()),) + tuple(outs[2:])


def solution(mesh):
    rows = P(("pts", "fsdp"), None)
    split = P(None, "fsdp", None)
    in_specs = (rows,) * 4 + (split,) * 8 + (P(),) * 8
    out_specs = (rows, rows, P()) + (split,) * 10 + (P(),) * 10
    return jax.shard_map(
        functools.partial(body, mesh.shape["pts"] // 2),
        mesh=mesh, in_specs=in_specs, out_specs=out_specs, check_vma=False,
    )
```

```python
import functools
import math

import jax
import jax.numpy as jnp
from jax import lax
from jax.experimental import pallas as pl
from jax.experimental.pallas import tpu as pltpu
from jax.sharding import PartitionSpec as P

C = 256
H = 8
DH = 32
G = 64
FF = 1024
ITEMS = 16
STEP = 5
W = 256
T = 128
BATCH = 8
NORM_EPS = 1e-05
SLICE_EPS = 1e-05
CLIP = 1.0
BETA_ONE = 0.5
BETA_TWO = 0.5
ADAM_EPS = 1e-08
DECAY = 0.01
EMA_RATE = 0.6
RATE_ATTN = 0.04
RATE_MLP = 0.03
RATE_SMALL = 0.4
RATE_VECTOR = 0.3
ZO = 4
UN = 48
CB = 144
CL = 32
SM = 80
MESH = pl.DeviceIdType.MESH
HIGH = lax.Precision.HIGHEST
F32 = jnp.float32
BF = jnp.bfloat16
GELU_A = math.sqrt(2.0 / math.pi)
GELU_B = GELU_A * 0.044715


def nn(a, b, precision=None):
    return lax.dot_general(a, b, (((1,), (0,)), ((), ())), precision=precision, preferred_element_type=F32)


def nt(a, b, precision=None):
    return lax.dot_general(a, b, (((1,), (1,)), ((), ())), precision=precision, preferred_element_type=F32)


def tn(a, b, precision=None):
    return lax.dot_general(a, b, (((0,), (0,)), ((), ())), precision=precision, preferred_element_type=F32)


def iota(shape, dim):
    return lax.broadcasted_iota(jnp.int32, shape, dim)


def tile_of(i, width=W):
    return pl.ds(pl.multiple_of(i * width, width), width)


class Place:
    def __init__(self, zs):
        self.p = lax.axis_index("pts")
        self.f = lax.axis_index("fsdp")
        self.a = self.f % 2
        self.x = self.f // 2
        self.y = self.p % 2
        self.z = self.p // 2
        self.m = self.x * 2 + self.y
        self.zs = zs
        self.core = (self.p, self.f + 1 - 2 * self.a)
        self.xpeer = (self.p, (1 - self.x) * 2 + self.a)
        self.ypeer = (self.z * 2 + 1 - self.y, self.f)
        self.zown = self.z if zs == ZO else jnp.minimum(self.z, ZO - 1)

    def xy(self, k):
        mm = (self.m + k) % 4
        return mm, (self.z * 2 + mm % 2, (mm // 2) * 2 + self.a)

    def xy_other(self, k):
        mm = (self.m + k) % 4
        return mm, (self.z * 2 + mm % 2, (mm // 2) * 2 + 1 - self.a)

    def chips(self):
        return [(k, j) for j in range(self.zs - 1, -1, -1) for k in (3, 2, 1, 0) if k or j]

    def chip(self, k, j):
        mm, zz = (self.m + k) % 4, (self.z + j) % self.zs
        return mm, zz, (zz * 2 + mm % 2, (mm // 2) * 2 + self.a)

    def zl(self, k):
        zz = (self.z + k) % self.zs
        return zz, (zz * 2 + self.y, self.f)

    def barrier(self):
        b = pltpu.get_barrier_semaphore()
        peers = [self.core] + [self.chip(k, j)[2] for k, j in self.chips()]
        peers += [self.xy_other(k)[1] for k in (1, 2, 3)]
        for d in peers:
            pl.semaphore_signal(b, inc=1, device_id=d, device_id_type=MESH)
        pl.semaphore_wait(b, len(peers))

    def owned(self, z, fn):
        if self.zs == ZO:
            fn()
        else:
            pl.when(z < ZO)(fn)


def rcopy(src, dst, ss, rs, dev):
    return pltpu.make_async_remote_copy(
        src_ref=src, dst_ref=dst, send_sem=ss, recv_sem=rs, device_id=dev, device_id_type=MESH
    )


class Reduce:
    def __init__(self, g, src, bufs):
        self.g, self.src = g, src
        self.r1, self.s2, self.r2, self.s3, self.r3, self.sem = bufs
        self.c1, self.c2, self.c3 = {}, [], []

    @staticmethod
    def scratch(rows, zs):
        return [
            pltpu.VMEM((4, ZO, rows, 128), BF),
            pltpu.VMEM((3, ZO, rows, 128), BF),
            pltpu.VMEM((3, ZO, rows, 128), BF),
            pltpu.VMEM((ZO, rows, 128), BF),
            pltpu.VMEM((zs - 1, rows, 128), BF),
            pltpu.SemaphoreType.DMA((6, max(zs, 4))),
        ]

    def core(self, k):
        g = self.g
        mm = (g.m + k) % 4
        c = rcopy(self.src.at[1 - g.a, mm], self.r1.at[mm], self.sem.at[0, k], self.sem.at[1, k], g.core)
        c.start()
        self.c1[k] = c

    def pair(self, k):
        g = self.g
        self.c1[k].wait_recv()
        mm = (g.m + k) % 4
        return self.src[g.a, mm].astype(F32) + self.r1[mm].astype(F32)

    def square(self, k):
        g = self.g
        dev = g.xy(k)[1]
        self.s2[k - 1] = self.pair(k).astype(BF)
        c = rcopy(self.s2.at[k - 1], self.r2.at[k - 1], self.sem.at[2, k - 1], self.sem.at[3, k - 1], dev)
        c.start()
        self.c2.append(c)

    def line(self):
        g = self.g
        acc = self.pair(0)
        for k in (1, 2, 3):
            self.c2[k - 1].wait_recv()
            acc = acc + self.r2[k - 1].astype(F32)
        self.s3[...] = acc.astype(BF)
        for k in range(1, g.zs):
            zz, dev = g.zl(k)
            at = zz if g.zs == ZO else jnp.minimum(zz, ZO - 1)
            c = rcopy(self.s3.at[at], self.r3.at[k - 1], self.sem.at[4, k - 1], self.sem.at[5, k - 1], dev)
            g.owned(zz, c.start)
            self.c3.append(c)

    def result(self):
        g = self.g
        out = self.s3[g.zown].astype(F32)
        for k in range(1, g.zs):
            g.owned(g.z, self.c3[k - 1].wait_recv)
            out = out + self.r3[k - 1].astype(F32)
        return out

    def finish(self):
        g = self.g
        for c in self.c1.values():
            c.wait_send()
        for c in self.c2:
            c.wait_send()
        for k in range(1, g.zs):
            g.owned(g.zl(k)[0], self.c3[k - 1].wait_send)


class Direct:
    def __init__(self, g, src, bufs):
        self.g, self.src = g, src
        self.r1, self.s2, self.r2, self.core_sem, self.chip_sem = bufs
        self.c1, self.c2 = {}, {}

    @staticmethod
    def scratch(rows, zs):
        return [
            pltpu.VMEM((4, ZO, rows, 128), BF),
            pltpu.VMEM((4, ZO, rows, 128), BF),
            pltpu.VMEM((4, zs, rows, 128), BF),
            pltpu.SemaphoreType.DMA((2, 4)),
            pltpu.SemaphoreType.DMA((2, 4, zs)),
        ]

    def core(self, k):
        g = self.g
        mm = (g.m + k) % 4
        c = rcopy(self.src.at[1 - g.a, mm], self.r1.at[mm], self.core_sem.at[0, k], self.core_sem.at[1, k], g.core)
        c.start()
        self.c1[k] = c

    def chips(self):
        g = self.g
        for k in (3, 2, 1, 0):
            self.c1[k].wait_recv()
            mm = (g.m + k) % 4
            self.s2[k] = (self.src[g.a, mm].astype(F32) + self.r1[mm].astype(F32)).astype(BF)
        for k, j in g.chips():
            _, zz, dev = g.chip(k, j)
            at = zz if g.zs == ZO else jnp.minimum(zz, ZO - 1)
            c = rcopy(self.s2.at[k, at], self.r2.at[k, j], self.chip_sem.at[0, k, j], self.chip_sem.at[1, k, j], dev)
            g.owned(zz, c.start)
            self.c2[k, j] = (zz, c)

    def result(self):
        g = self.g
        out = self.s2[0, g.zown].astype(F32)
        for k, j in reversed(g.chips()):
            g.owned(g.z, self.c2[k, j][1].wait_recv)
            out = out + self.r2[k, j].astype(F32)
        return out

    def finish(self):
        for c in self.c1.values():
            c.wait_send()
        for zz, c in self.c2.values():
            self.g.owned(zz, c.wait_send)


class Gather:
    def __init__(self, g, out, bufs):
        self.g, self.out = g, out
        self.chip_sem, self.core_sem = bufs
        self.cz, self.cc = {}, []

    @staticmethod
    def scratch(zs):
        return [pltpu.SemaphoreType.DMA((2, 4, zs)), pltpu.SemaphoreType.DMA((2, 4))]

    def start(self):
        g = self.g
        own = self.out.at[g.a, g.m, g.zown]
        for k, j in g.chips():
            c = rcopy(own, own, self.chip_sem.at[0, k, j], self.chip_sem.at[1, k, j], g.chip(k, j)[2])
            g.owned(g.z, c.start)
            self.cz[k, j] = c

    def to_core(self):
        g = self.g
        for k in range(4):
            for j in range(g.zs):
                if k or j:
                    g.owned((g.z - j + g.zs) % g.zs, self.cz[k, j].wait_recv)
            r = self.out.at[g.a, (g.m - k + 4) % 4]
            c = rcopy(r, r, self.core_sem.at[0, k], self.core_sem.at[1, k], g.core)
            c.start()
            self.cc.append(c)

    def done(self):
        for c in self.cc:
            c.wait_recv()

    def finish(self):
        g = self.g
        for c in self.cz.values():
            g.owned(g.z, c.wait_send)
        for c in self.cc:
            c.wait_send()


def counts(surface, volume):
    at = surface[0, 0] * 0
    starts, surfs, sizes = [], [], []
    for b in range(ITEMS):
        starts.append(at)
        surfs.append(surface[0, b])
        sizes.append(surface[0, b] + volume[0, b])
        at = at + sizes[b]
    return starts, surfs, sizes, at


def column(row):
    return jnp.broadcast_to(row, (128, row.shape[1])).T


def wide(col):
    return jnp.concatenate([col, col], axis=1)


def norm_stats(v):
    mean = jnp.mean(v, axis=0, keepdims=True)
    centred = v - mean
    var = jnp.mean(centred * centred, axis=0, keepdims=True)
    scale = lax.rsqrt(var + NORM_EPS)
    return centred * scale, scale


def halves():
    lane = iota((1, 128), 1)
    return (lane < G).astype(F32).astype(BF), (lane >= G).astype(F32).astype(BF)


def spread_unit(unit):
    low, high = halves()
    return jnp.concatenate([unit * low, unit * high], axis=0)


def take_units(full):
    low = iota((DH, 128), 1) < G
    one = jnp.where(low, full[0:DH, 0:128], full[DH : 2 * DH, 0:128])
    two = jnp.where(low, full[2 * DH : 3 * DH, 128:256], full[3 * DH : 4 * DH, 128:256])
    return one, two


def item_units(fields, probs):
    left = jnp.concatenate([fields, jnp.ones((16, T), BF)], axis=0)
    full = nt(left, probs)
    one, two = take_units(full)
    one = jnp.concatenate([one, full[128:144, 0:128]], axis=0)
    two = jnp.concatenate([two, full[128:144, 128:256]], axis=0)
    return one.astype(BF), two.astype(BF)


def slice_columns(small):
    low = small[:, 0:128].astype(BF)
    pick = (iota((H * G, 128), 0) % G == iota((H * G, 128), 1)).astype(F32).astype(BF)
    rows = nt(pick, low).astype(BF)
    place = (iota((DH, C), 1) % DH == iota((DH, C), 0)).astype(F32).astype(BF)
    full = nn(rows, place)
    keep = iota((H * G, C), 0) // G == iota((H * G, C), 1) // DH
    return jnp.where(keep, full, 0.0).astype(BF)


def same_head():
    return iota((2 * G, 2 * G), 0) // G == iota((2 * G, 2 * G), 1) // G


def main_kernel(
    zs, surface, volume, points_hbm, cot_hbm, attn_w, mlp_w, small, vector,
    mixed_hbm, grad_hbm, big, late, small_sum, norm_out, points, cotangent, mixed, points_grad, load_sem,
    bounds, surf, keep, xt, cot_t, normed, mid, probs, spread, norm_two, active, d_hidden, d_branch, d_spread, d_mid,
    d_both, d_logits, wat, wml, wxf, slicew, slicet, wot, wint, woutt, gain_one, gain_two, embed_acc,
    src, src_big, src_late, slice_out, d_slice, saved, attention, maps_acc,
    small_src, sr1, sr2, sr3, line_late, sqb, weight_sem, big_sem, y_sem, sem, sq_sem, *sems,
):
    g = Place(zs)
    rows = ITEMS * T
    red = [Direct(g, src.at[i], sems[3 * i : 3 * i + 3] + sems[12 + 2 * (i % 2) : 14 + 2 * (i % 2)]) for i in range(4)]
    red_big = Reduce(g, src_big, sems[16:22])
    red_late = Reduce(g, src_late, sems[22:28])
    gat = [Gather(g, slice_out.at[i], sems[28 + 2 * i : 30 + 2 * i]) for i in range(2)]
    gat += [Gather(g, d_slice.at[i], sems[28 + 2 * i : 30 + 2 * i]) for i in range(2)]

    own = pl.ds(pl.multiple_of(g.f * 64, 64), 64)
    other = pl.ds(pl.multiple_of(((1 - g.x) * 2 + g.a) * 64, 64), 64)
    wat[:, own, :] = attn_w[...].astype(BF)
    load_points = pltpu.make_async_copy(points_hbm, points, load_sem.at[0])
    load_cot = pltpu.make_async_copy(cot_hbm, cotangent, load_sem.at[1])
    load_points.start()
    g.barrier()

    def weight(ref, lead, at, i, dev):
        r = ref.at[lead, at, :]
        return rcopy(r, r, weight_sem.at[0, i], weight_sem.at[1, i], dev)

    two, three, all_mlp = pl.ds(0, 2), pl.ds(2, 1), pl.ds(0, 2)
    a_x, a_c, a_f = weight(wat, two, own, 0, g.xpeer), weight(wat, two, own, 1, g.core), weight(wat, two, other, 2, g.core)
    o_x, o_c, o_f = weight(wat, three, own, 3, g.xpeer), weight(wat, three, own, 4, g.core), weight(wat, three, other, 5, g.core)
    m_x, m_c, m_f = weight(wml, all_mlp, own, 6, g.xpeer), weight(wml, all_mlp, own, 7, g.core), weight(wml, all_mlp, other, 8, g.core)
    a_x.start()
    a_c.start()
    load_cot.start()
    wml[:, own, :] = mlp_w[...].astype(BF)
    load_points.wait()

    starts, surfs, sizes, total = counts(surface, volume)
    lane = iota((1, T), 1)
    for b in range(ITEMS):
        shift = total + b * T - starts[b] - sizes[b]
        bounds[0, b] = starts[b]
        bounds[1, b] = sizes[b]
        bounds[2, b] = shift
        bounds[3, b] = jnp.minimum(lax.div(starts[b], jnp.int32(T)), ITEMS - 2)
        bounds[4, b] = jnp.minimum(lax.div(shift, jnp.int32(T)), ITEMS - 2)
        surf[:, b * T : b * T + T] = (lane < surfs[b]).astype(F32)
        keep[:, b * T : b * T + T] = (lane < sizes[b]).astype(F32)
    gain_a = column(vector[0:1, :])
    gain_b = wide(column(vector[1:2, :]))
    embed = column(vector[2:3, :])
    embed2 = wide(embed)

    def packed(ref, b):
        t, u, size = bounds[3, b], bounds[4, b], bounds[1, b]
        to, row = iota((T, 2 * T), 0), iota((T, 2 * T), 1)
        one = (row + t * T == to + bounds[0, b]) & (to < size)
        two = (row + u * T == to + bounds[2, b]) & (to >= size)
        pick = jnp.concatenate([one.astype(F32).astype(BF), two.astype(F32).astype(BF)], axis=1)
        return nn(pick, jnp.concatenate([ref[i] for i in (t, t + 1, u, u + 1)], axis=0)).T

    def pack_item(b, carry):
        at = tile_of(b, T)
        field = packed(points, b)
        xt[:, at] = field.astype(BF)
        unit, _ = norm_stats(field + embed * surf[:, at])
        normed[:, at] = (unit * gain_a).astype(BF)
        return carry

    def pack_cot(b, carry):
        cot_t[:, tile_of(b, T)] = packed(cotangent, b).astype(BF)
        return carry

    lax.fori_loop(0, ITEMS, pack_item, 0, unroll=8)
    a_x.wait_recv()
    a_f.start()
    for c in (m_x, o_x, m_c, o_c):
        c.start()
    slicew[...] = slice_columns(small)
    for r in (gain_one, gain_two, embed_acc, maps_acc):
        r[...] = jnp.zeros_like(r)

    def turned(v):
        return v.astype(F32).T.astype(BF)

    a_c.wait_recv()
    a_f.wait_recv()
    wxf[0:C, :] = turned(wat[0])
    wxf[C : 2 * C, :] = turned(wat[1])

    def soft_tile(i, carry):
        at = tile_of(i)
        both = nn(wxf[...], normed[:, at]).astype(BF)
        mid[:, at] = both
        logits = nn(slicew[...], both[0:C]).reshape(H, G, W)
        top = jnp.max(logits, axis=1, keepdims=True)
        e = jnp.exp(logits - top)
        scale = keep[:, at] / jnp.sum(e, axis=1, keepdims=True)
        probs[:, at] = (e * scale).reshape(H * G, W).astype(BF)
        return carry

    def sums(r, batch, fields, off):
        for half in range(2):
            for k in (1, 2, 3, 0):
                mm = (g.m + k) % 4
                core = (1 - g.a) if half == 0 else g.a
                at = tile_of(batch * BATCH + core * 4 + mm, T)
                for q in range(2):
                    both = item_units(fields[off + q * 128 : off + q * 128 + 128, at], probs[q * 256 : q * 256 + 256, at])
                    for i in range(2):
                        r.src[core, mm, 2 * q + i] = both[i]
                if half == 0:
                    r.core(k)

    def attend(batch):
        unit = red[batch].result()
        raw, scale = unit[0:DH], unit[DH : DH + 8] + SLICE_EPS
        token = raw / scale[0:1]
        qkv = tn(small[...], token, HIGH)
        query, key, value = qkv[64:96], qkv[96:128], qkv[128:160]
        scores = tn(key, query, HIGH) / math.sqrt(DH)
        scores = jnp.where(same_head(), scores, -jnp.inf)
        top = jnp.max(scores, axis=0, keepdims=True)
        e = jnp.exp(scores - top)
        weights = e / jnp.sum(e, axis=0, keepdims=True)
        slice_out[batch, g.a, g.m, g.zown] = nn(value.astype(BF), weights.astype(BF)).astype(BF)
        gat[batch].start()
        saved[batch, 0:32] = token
        saved[batch, 32:128] = qkv[64:160]
        saved[batch, 128:160] = raw
        saved[batch, 160:168] = scale
        attention[batch] = weights

    def attend_back(batch):
        unit = red[2 + batch].result()
        d_out = unit[0:DH]
        s = saved.at[batch]
        token, query, key, value = s[0:32], s[32:64], s[64:96], s[96:128]
        raw, scale = s[128:160], s[160:161]
        weights = attention[batch]
        low = weights.astype(BF)
        d_low, query, key, value = [v.astype(BF) for v in (d_out, query, key, value)]
        d_value = nt(d_low, low)
        d_weights = tn(value, d_low)
        d_scores = weights * (d_weights - jnp.sum(weights * d_weights, axis=0, keepdims=True))
        d_scores = (d_scores / math.sqrt(DH)).astype(BF)
        d_query = nn(key, d_scores)
        d_key = nt(query, d_scores)
        d_maps = jnp.concatenate([jnp.zeros((64, T), F32), d_query, d_key, d_value], axis=0).astype(BF)
        d_token = nn(small[...].astype(BF), d_maps)
        d_total = -jnp.sum(d_token * raw, axis=0, keepdims=True) / (scale * scale)
        tot = jnp.broadcast_to(d_total, (16, T))
        d_slice[batch, g.a, g.m, g.zown] = jnp.concatenate([d_token / scale, tot], axis=0).astype(BF)
        gat[2 + batch].start()
        part = nt(token.astype(BF), jnp.concatenate([d_maps, jnp.zeros((96, T), BF)], axis=0))
        if zs != ZO:
            part = jnp.where(g.z < ZO, part, 0.0)
        maps_acc[...] += part

    lax.fori_loop(0, 4, soft_tile, 0, unroll=2)
    sums(red[0], 0, mid, C)
    lax.fori_loop(4, 6, soft_tile, 0, unroll=2)
    red[0].chips()
    lax.fori_loop(6, 8, soft_tile, 0, unroll=2)
    sums(red[1], 1, mid, C)
    red[1].chips()
    m_x.wait_recv()
    m_f.start()
    o_x.wait_recv()
    o_f.start()
    load_cot.wait()
    slicet[...] = turned(slicew[...])
    attend(0)
    for c in (m_c, o_c, m_f, o_f):
        c.wait_recv()
    wot[...] = turned(wat[2])
    for j in range(FF // 256):
        wint[j * 256 : j * 256 + 256, :] = turned(wml[0, :, j * 256 : j * 256 + 256])
    attend(1)
    for j in range(FF // 256):
        woutt[j * 256 : j * 256 + 256, :] = turned(wml[1, :, j * 256 : j * 256 + 256])
    gat[0].to_core()
    lax.fori_loop(0, ITEMS, pack_cot, 0, unroll=4)
    gat[0].done()

    def spread_item(b, carry):
        at = tile_of(b, T)
        batch = b // BATCH
        core = (b % BATCH) // 4
        for i in range(4):
            part = nn(spread_unit(slice_out[batch, core, b % 4, i]), probs[i * 128 : i * 128 + 128, at])
            spread[i * 64 : i * 64 + 64, at] = part.astype(BF)
        return carry

    def mlp_tile(i, carry):
        at = tile_of(i)
        middle = xt[:, at].astype(F32) + embed2 * surf[:, at] + nn(wot[...], spread[:, at])
        unit, scale = norm_stats(middle)
        two = (unit * gain_b).astype(BF)
        norm_two[:, at] = two
        ctb = cot_t[:, at]
        for j in range(FF // 256):
            hid = pl.ds(j * 256, 256)
            x = nn(wint[hid, :], two)
            da = nn(woutt[hid, :], ctb)
            sq = x * x
            t = jnp.tanh(x * (GELU_A + GELU_B * sq))
            s = 0.5 + 0.5 * t
            act = (x * s).astype(BF)
            slope = s + (x * (s - s * s)) * (2.0 * GELU_A + 6.0 * GELU_B * sq)
            dh = (slope * da).astype(BF)
            active[hid, at] = act
            d_hidden[hid, at] = dh
        d_two = nn(wml[0], d_hidden[:, at])
        mixed[at, :] = (middle + nn(wml[1], active[:, at])).T.astype(BF)
        gs = d_two * unit
        gain_two[...] += gs[:, 0:128] + gs[:, 128:256]
        du = d_two * gain_b
        m1 = jnp.mean(du, axis=0, keepdims=True)
        m2 = jnp.mean(du * unit, axis=0, keepdims=True)
        dm = ctb.astype(F32) + scale * (du - m1 - unit * m2)
        d_mid[:, at] = dm
        db = dm.astype(BF)
        d_branch[:, at] = db
        d_spread[:, at] = nn(wat[2], db).astype(BF)
        return carry

    lax.fori_loop(0, BATCH, spread_item, 0, unroll=8)
    gat[1].to_core()
    lax.fori_loop(0, 2, mlp_tile, 0, unroll=2)
    lax.fori_loop(2, 4, mlp_tile, 0, unroll=2)
    red[0].finish()
    sums(red[2], 0, d_spread, 0)
    gat[1].done()
    red[1].finish()
    lax.fori_loop(BATCH, ITEMS, spread_item, 0, unroll=8)
    red[2].chips()
    lax.fori_loop(4, 6, mlp_tile, 0, unroll=2)
    lax.fori_loop(6, 8, mlp_tile, 0, unroll=2)
    gat[0].finish()
    gat[1].finish()
    attend_back(0)
    sums(red[3], 1, d_spread, 0)
    stores = [pltpu.make_async_copy(mixed, mixed_hbm, load_sem.at[2])]
    stores[0].start()

    def put(f, p, lo, value):
        src_big[f % 2, (f // 2) * 2 + p % 2, p // 2, lo : lo + value.shape[0], :] = value

    def grad_mlp(which, left, right):
        for j in range(FF // 256):
            grad = nt(left[...], right[j * 256 : j * 256 + 256, :]).astype(BF)
            for f in range(4):
                for i in range(2):
                    put(f, 2 * j + i, which * 64, grad[f * 64 : f * 64 + 64, i * 128 : i * 128 + 128])

    grad_mlp(0, norm_two, d_hidden)
    red[3].chips()
    grad_mlp(1, cot_t, active)
    gat[2].to_core()
    grad = nt(spread[...], d_branch[...]).astype(BF)
    for f in range(4):
        for p in range(8):
            lo = f * 64 + (p % 4) * 16
            put(f, p, 128, grad[lo : lo + 16, (p // 4) * 128 : (p // 4) * 128 + 128])
    gat[2].done()
    block = iota((1, 2 * T), 1)
    block = jnp.where(block < T, block // DH % 2, jnp.where(block == T, 0, jnp.where(block == T + 16, 1, 2)))
    even, odd = [(block == i).astype(F32).astype(BF) for i in range(2)]
    ones_rows = jnp.ones((T, T), BF)
    blank = jnp.zeros((T - 32, T), BF)

    def back_item(b, carry):
        at = tile_of(b, T)
        batch = b // BATCH
        core = (b % BATCH) // 4
        for q in range(2):
            outs = [slice_out[batch, core, b % 4, 2 * q + i] for i in range(2)]
            ds = [d_slice[batch, core, b % 4, 2 * q + i] for i in range(2)]
            parts = outs + [d[0:DH] for d in ds] + [d[DH:UN] for d in ds] + [blank]
            turn = jnp.concatenate(parts, axis=0).T
            for one in range(2):
                rows_of = [4 * q + one, 4 * q + 2 + one]
                left = turn[one * G : one * G + G]
                left = jnp.concatenate([left * even, left * odd], axis=0)
                fields = [d_spread[h * DH : h * DH + DH, at] for h in rows_of]
                fields += [mid[C + h * DH : C + h * DH + DH, at] for h in rows_of]
                dp = nn(left, jnp.concatenate(fields + [ones_rows], axis=0)).reshape(2, G, T)
                pf = jnp.stack([probs[h * G : h * G + G, at] for h in rows_of]).astype(F32)
                back = pf * (dp - jnp.sum(pf * dp, axis=1, keepdims=True))
                for i, h in enumerate(rows_of):
                    d_logits[h * G : h * G + G, at] = back[i].astype(BF)
            for i in range(2):
                k = 2 * q + i
                part = nn(spread_unit(ds[i][0:DH]), probs[k * 128 : k * 128 + 128, at])
                d_both[C + k * 64 : C + k * 64 + 64, at] = part.astype(BF)
        return carry

    def back_tile(i, carry):
        at = tile_of(i)
        d_norm = nn(wat[0], d_both[0:C, at]) + nn(wat[1], d_both[C : 2 * C, at])
        sf = surf[:, at]
        unit, scale = norm_stats(xt[:, at].astype(F32) + embed2 * sf)
        gs = d_norm * unit
        gain_one[...] += gs[:, 0:128] + gs[:, 128:256]
        du = d_norm * wide(gain_a)
        m1 = jnp.mean(du, axis=0, keepdims=True)
        m2 = jnp.mean(du * unit, axis=0, keepdims=True)
        pg = d_mid[:, at] + scale * (du - m1 - unit * m2)
        es = pg * sf
        embed_acc[...] += es[:, 0:128] + es[:, 128:256]
        points_grad[at, :] = pg.T
        return carry

    def mid_tile(i, carry):
        at = tile_of(i)
        d_both[0:C, at] = nn(slicet[...], d_logits[:, at]).astype(BF)
        return carry

    lax.fori_loop(0, 4, back_item, 0, unroll=4)
    attend_back(1)
    for k in (1, 2, 3, 0):
        red_big.core(k)
    lax.fori_loop(4, BATCH, back_item, 0, unroll=4)
    for k in (1, 2, 3):
        red_big.square(k)
    lax.fori_loop(0, 4, mid_tile, 0, unroll=4)
    lax.fori_loop(0, 4, back_tile, 0, unroll=4)
    gat[3].to_core()
    half_rows = [pl.ds(0, rows // 2), pl.ds(rows // 2, rows // 2)]

    def store_half(i):
        c = pltpu.make_async_copy(points_grad.at[half_rows[i], :], grad_hbm.at[half_rows[i], :], load_sem.at[3 + i])
        c.start()
        stores.append(c)

    store_half(0)
    def copies(ref, base):
        part = ref.at[g.zown, g.y]
        cz = []
        for k in range(1, zs):
            c = rcopy(part, part, big_sem.at[base, k], big_sem.at[base + 1, k], g.zl(k)[1])
            g.owned(g.z, c.start)
            cz.append(c)
        return cz

    def to_y(ref, sem):
        cy = []
        for z in range(ZO):
            r = ref.at[z, g.y]
            c = rcopy(r, r, sem.at[0, z], sem.at[1, z], g.ypeer)
            c.start()
            cy.append(c)
        return cy

    gat[3].done()
    lax.fori_loop(BATCH, BATCH + 4, back_item, 0, unroll=4)
    red_big.line()
    lax.fori_loop(BATCH + 4, ITEMS, back_item, 0, unroll=4)
    lax.fori_loop(4, 8, mid_tile, 0, unroll=4)

    grads = [nt(normed[...], d_both[i * C : i * C + C, :]).astype(BF) for i in range(2)]
    for f in range(4):
        for p in range(8):
            lo, col = f * 64 + (p % 4) * 16, (p // 4) * 128
            both = [v[lo : lo + 16, col : col + 128] for v in grads]
            src_late[f % 2, (f // 2) * 2 + p % 2, p // 2] = jnp.concatenate(both, axis=0)
    for k in (1, 2, 3, 0):
        red_late.core(k)
    fold = jnp.zeros((DH, 128), F32)
    for i in range(4):
        part = nt(mid[i * 64 : i * 64 + 64, :], d_logits[i * 128 : i * 128 + 128, :])
        fold = fold + jnp.where(iota((DH, 128), 1) < G, part[0:DH], part[DH : 2 * DH])
    fold = jnp.where(iota((32, 128), 1) < G, fold + pltpu.roll(fold, G, 1), 0.0)
    big[g.zown, g.y] = red_big.result().astype(BF)
    big_z = copies(big, 0)
    for k in (1, 2, 3):
        red_late.square(k)
    lax.fori_loop(4, 8, back_tile, 0, unroll=4)
    for k in range(1, zs):
        g.owned((g.z - k + zs) % zs, big_z[k - 1].wait_recv)
    big_y = to_y(big, y_sem.at[0])
    store_half(1)

    ones = jnp.ones((8, 128), F32)
    line = [nt(ones, r[...], HIGH) for r in (gain_one, gain_two, embed_acc)]
    pick = iota((8, 256), 0)
    vec = jnp.where(pick == 0, line[0], jnp.where(pick == 1, line[1], jnp.where(pick == 2, line[2], 0.0)))
    small_src[0:32] = (fold + maps_acc[:, 0:128]).astype(BF)
    small_src[32:64] = maps_acc[:, 128:256].astype(BF)
    small_src[64:80] = jnp.concatenate([vec[:, 0:128], vec[:, 128:256]], axis=0).astype(BF)
    cs = [rcopy(small_src, sr1, sem.at[0, 0], sem.at[1, 0], g.core)]
    cs[0].start()

    acc = red_late.pair(0)
    for k in (1, 2, 3):
        red_late.c2[k - 1].wait_recv()
        acc = acc + red_late.r2[k - 1].astype(F32)
    line_late[g.z] = acc.astype(BF)
    line_copies = []
    for k in range(1, zs):
        c = rcopy(line_late.at[g.z], line_late.at[g.z], sem.at[4, k], sem.at[5, k], g.zl(k)[1])
        c.start()
        line_copies.append(c)
    cs[0].wait_recv()
    sr2[g.m] = (small_src[...].astype(F32) + sr1[...].astype(F32)).astype(BF)
    for k in (1, 2, 3):
        c = rcopy(sr2.at[g.m], sr2.at[g.m], sem.at[0, k], sem.at[1, k], g.xy(k)[1])
        c.start()
        cs.append(c)
    bigs = big[:, g.y].astype(F32).reshape(ZO * CB // 8, 8, 128)
    squares = jnp.sum(bigs * bigs, axis=0)
    for c in line_copies:
        c.wait_recv()
    acc = line_late[0].astype(F32)
    for z in range(1, zs):
        acc = acc + line_late[z].astype(F32)
    acc = acc.astype(BF)
    late[:, g.y] = acc
    mine = acc.astype(F32).reshape(ZO * CL // 8, 8, 128)
    here = g.a * 4 + g.m
    sqb[here] = squares + jnp.sum(mine * mine, axis=0)
    sq_copies = []
    for k in range(1, 8):
        dev = g.core if k == 4 else g.xy(k)[1] if k < 4 else g.xy_other(k - 4)[1]
        c = rcopy(sqb.at[here], sqb.at[here], sq_sem.at[0, k], sq_sem.at[1, k], dev)
        c.start()
        sq_copies.append(c)
    late_y = to_y(late, y_sem.at[1])
    for c in cs[1:4]:
        c.wait_recv()
    total = sr2[0].astype(F32)
    for m in range(1, 4):
        total = total + sr2[m].astype(F32)
    sr3[g.z] = total.astype(BF)
    for k in range(1, zs):
        c = rcopy(sr3.at[g.z], sr3.at[g.z], sem.at[2, k], sem.at[3, k], g.zl(k)[1])
        c.start()
        cs.append(c)
    for c in big_y + late_y + cs[4:]:
        c.wait_recv()
    total = sr3[0].astype(F32)
    for z in range(1, zs):
        total = total + sr3[z].astype(F32)
    small_sum[...] = total
    for c in sq_copies:
        c.wait_recv()
    sq = sqb[0]
    for i in range(1, 8):
        sq = sq + sqb[i]
    norm_out[0, 0] = jnp.sqrt(jnp.sum(sq) + jnp.sum(total * total))

    for c in cs + line_copies + sq_copies + big_y + late_y + [a_x, a_c, a_f, o_x, o_c, o_f, m_x, m_c, m_f]:
        c.wait_send()
    for c in stores:
        c.wait()
    for c in big_z:
        g.owned(g.z, c.wait_send)
    for c in red_late.c1.values():
        c.wait_send()
    for c in red_late.c2:
        c.wait_send()
    for r in red[2:] + [red_big] + gat[2:]:
        r.finish()


def adamw(state, new, sl, grad, factor, rate):
    weight, first, second, average = [r[sl] for r in state]
    clipped = grad * factor
    first_new = BETA_ONE * first + (1.0 - BETA_ONE) * clipped
    second_new = BETA_TWO * second + (1.0 - BETA_TWO) * clipped * clipped
    first_hat = first_new / (1.0 - BETA_ONE**STEP)
    second_hat = second_new / (1.0 - BETA_TWO**STEP)
    new_weight = weight - rate * (first_hat / (jnp.sqrt(second_hat) + ADAM_EPS) + DECAY * weight)
    average_new = EMA_RATE * average + (1.0 - EMA_RATE) * new_weight
    for r, v in zip(new, (new_weight, first_new, second_new, average_new, new_weight.astype(BF))):
        r[sl] = v


def last_kernel(surface, volume, norm, mixed_p, grad_p, big, late, small_sum, *refs):
    hbm_states, hbm_outs = refs[0:16], refs[16:38]
    states, news = refs[38:54], refs[54:74]
    rows_in, mixed_in, mixed_rows, mixed_low, grad_rows, in_sem, out_sem = refs[74:]
    rows = mixed_low.shape[0]
    ins = [pltpu.make_async_copy(h, v, in_sem.at[i]) for i, (h, v) in enumerate(zip(hbm_states, states))]
    gp = pltpu.make_async_copy(grad_p, rows_in, in_sem.at[16])
    mp = pltpu.make_async_copy(mixed_p, mixed_in, in_sem.at[17])
    for c in ins[4:8] + ins[0:4] + ins[8:] + [gp, mp]:
        c.start()
    starts, _, sizes, total = counts(surface, volume)

    row = iota((T + 8, 1), 0)
    sub = iota((1, 8, 1), 1)

    def place(source, out):
        def moved(b, base):
            first = pl.multiple_of(lax.div(base, jnp.int32(8)) * 8, 8)
            off = base - first
            turn = pltpu.roll(source[b * T : b * T + T, :].astype(F32).reshape(T // 8, 8, C), off, 1)
            later = jnp.where(sub >= off, turn[1:], turn[:-1])
            return first, off, jnp.concatenate([turn[0:1], later, turn[-1:]], axis=0).reshape(T + 8, C)

        for b in range(ITEMS):
            first, off, tile = moved(b, starts[b])
            head = pl.ds(first, 8)
            out[head, :] = jnp.where(row[0:8] >= off, tile[0:8], out[head, :])
            out[pl.ds(pl.multiple_of(first + 8, 8), T), :] = tile[8:]
        for b in range(ITEMS):
            first, off, tile = moved(b, total + b * T - starts[b] - sizes[b])
            here = pl.ds(first, T + 8)
            out[here, :] = jnp.where(row >= sizes[b] + off, tile, out[here, :])

    outs = []
    attn, mlp, small_s, vector_s = [states[4 * i : 4 * i + 4] for i in range(4)]
    attn_new, mlp_new, small_new, vector_new = [news[5 * i : 5 * i + 5] for i in range(4)]
    factor = jnp.minimum(1.0, CLIP / norm[0, 0])
    everything = slice(None)
    both = (everything, everything)
    for c in ins[4:8]:
        c.wait()
    for z in range(ZO):
        for y in range(2):
            p = z * 2 + y
            for i in range(2):
                grad = big[z, y, i * 64 : i * 64 + 64, :].astype(F32)
                adamw(mlp, mlp_new, (i, everything, slice(p * 128, p * 128 + 128)), grad, factor, RATE_MLP)

    def send(first, count):
        for i in range(first, first + count):
            c = pltpu.make_async_copy(news[i], hbm_outs[2 + i], out_sem.at[2 + i])
            c.start()
            outs.append(c)

    send(5, 5)
    for c in ins[0:4] + ins[8:]:
        c.wait()
    for z in range(ZO):
        for y in range(2):
            p = z * 2 + y
            lo, col = (p % 4) * 16, (p // 4) * 128
            at = (slice(lo, lo + 16), slice(col, col + 128))
            grad = big[z, y, 128:144, :].astype(F32)
            adamw(attn, attn_new, (2,) + at, grad, factor, RATE_ATTN)
            for i in range(2):
                grad = late[z, y, i * 16 : i * 16 + 16, :].astype(F32)
                adamw(attn, attn_new, (i,) + at, grad, factor, RATE_ATTN)
    send(0, 5)
    gsmall = jnp.concatenate([small_sum[0:32, :], small_sum[32:64, :]], axis=1)[:, 0:160]
    adamw(small_s, small_new, both, gsmall, factor, RATE_SMALL)
    gvec = jnp.concatenate([small_sum[64:72, :], small_sum[72:80, :]], axis=1)[0:3, :]
    adamw(vector_s, vector_new, both, gvec, factor, RATE_VECTOR)
    send(10, 10)
    gp.wait()
    place(rows_in, grad_rows)
    outs.append(pltpu.make_async_copy(grad_rows.at[pl.ds(0, rows), :], hbm_outs[1], out_sem.at[1]))
    outs[-1].start()
    mp.wait()
    place(mixed_in, mixed_rows)
    mixed_low[...] = mixed_rows[0:rows, :].astype(BF)
    outs.append(pltpu.make_async_copy(mixed_low, hbm_outs[0], out_sem.at[0]))
    outs[-1].start()
    for c in outs:
        c.wait()


def body(zs, points, cotangent, surface_count, volume_count, *state):
    attn, mlp, small, vector = [state[4 * i : 4 * i + 4] for i in range(4)]
    rows = points.shape[0]
    vmem = pl.BlockSpec(memory_space=pltpu.VMEM)
    smem = pl.BlockSpec(memory_space=pltpu.SMEM)
    hbm = pl.BlockSpec(memory_space=pl.ANY)
    sd = jax.ShapeDtypeStruct

    def tall(features, dtype=BF):
        return pltpu.VMEM((features, rows), dtype)

    def units(n, depth):
        return pltpu.VMEM((n, 2, 4, ZO, depth, 128), BF)

    scratch = [
        pltpu.VMEM((rows // T, T, C), BF), pltpu.VMEM((rows // T, T, C), BF), pltpu.VMEM((rows, C), BF),
        pltpu.VMEM((rows, C), F32), pltpu.SemaphoreType.DMA((5,)),
        pltpu.SMEM((5, ITEMS), jnp.int32), tall(1, F32), tall(1, F32),
        tall(C), tall(C), tall(C), tall(2 * C), tall(H * G), tall(C), tall(C), tall(FF), tall(FF), tall(C), tall(C),
        tall(C, F32), tall(2 * C), tall(H * G),
        pltpu.VMEM((3, C, C), BF), pltpu.VMEM((2, C, FF), BF), pltpu.VMEM((2 * C, C), BF),
        pltpu.VMEM((H * G, C), BF), pltpu.VMEM((C, H * G), BF), pltpu.VMEM((C, C), BF),
        pltpu.VMEM((FF, C), BF), pltpu.VMEM((FF, C), BF),
        pltpu.VMEM((C, 128), F32), pltpu.VMEM((C, 128), F32), pltpu.VMEM((C, 128), F32),
        units(4, UN), pltpu.VMEM((2, 4, ZO, CB, 128), BF), pltpu.VMEM((2, 4, ZO, CL, 128), BF),
        units(2, DH), units(2, UN), pltpu.VMEM((2, 168, 128), F32), pltpu.VMEM((2, 128, 128), F32),
        pltpu.VMEM((DH, 256), F32),
        pltpu.VMEM((SM, 128), BF), pltpu.VMEM((SM, 128), BF), pltpu.VMEM((4, SM, 128), BF), pltpu.VMEM((zs, SM, 128), BF),
        pltpu.VMEM((zs, ZO, CL, 128), BF), pltpu.VMEM((8, 8, 128), F32),
        pltpu.SemaphoreType.DMA((2, 9)), pltpu.SemaphoreType.DMA((2, max(zs, 4))), pltpu.SemaphoreType.DMA((2, 2, ZO)),
        pltpu.SemaphoreType.DMA((6, max(zs, 4))), pltpu.SemaphoreType.DMA((2, 8)),
    ]
    for _ in range(4):
        scratch += Direct.scratch(UN, zs)[0:3]
    for _ in range(2):
        scratch += Direct.scratch(UN, zs)[3:5]
    for depth in (CB, CL):
        scratch += Reduce.scratch(depth, zs)
    for _ in range(2):
        scratch += Gather.scratch(zs)
    mixed_p, grad_p, big, late, small_sum, norm = pl.pallas_call(
        functools.partial(main_kernel, zs),
        out_shape=[
            sd((rows, C), BF), sd((rows, C), F32), sd((ZO, 2, CB, 128), BF), sd((ZO, 2, CL, 128), BF),
            sd((SM, 128), F32), sd((1, 1), F32),
        ],
        in_specs=[smem, smem, hbm, hbm] + [vmem] * 4,
        out_specs=[hbm, hbm] + [vmem] * 3 + [smem],
        scratch_shapes=scratch,
        compiler_params=pltpu.CompilerParams(collective_id=0, has_side_effects=True, vmem_limit_bytes=60 << 20),
        name="main",
    )(surface_count, volume_count, points.reshape(-1, T, C), cotangent.reshape(-1, T, C), attn[0], mlp[0], small[0], vector[0])

    def news(leaves):
        return [sd(leaves[0].shape, F32)] * 4 + [sd(leaves[0].shape, BF)]

    everything = news(attn) + news(mlp) + news(small) + news(vector)
    outs = pl.pallas_call(
        last_kernel,
        out_shape=[sd((rows, C), BF), sd((rows, C), F32)] + everything,
        in_specs=[smem, smem, smem, hbm, hbm, vmem, vmem, vmem] + [hbm] * 16,
        out_specs=[hbm] * 22,
        scratch_shapes=[pltpu.VMEM(v.shape, v.dtype) for v in state]
        + [pltpu.VMEM(v.shape, v.dtype) for v in everything]
        + [
            pltpu.VMEM((rows, C), F32), pltpu.VMEM((rows, C), BF), pltpu.VMEM((rows + T, C), F32), pltpu.VMEM((rows, C), BF),
            pltpu.VMEM((rows + T, C), F32), pltpu.SemaphoreType.DMA((18,)), pltpu.SemaphoreType.DMA((22,)),
        ],
        compiler_params=pltpu.CompilerParams(vmem_limit_bytes=60 << 20),
        name="last",
    )(surface_count, volume_count, norm, mixed_p, grad_p, big, late, small_sum, *state)
    return tuple(outs[0:2]) + (norm.reshape(()),) + tuple(outs[2:])


def solution(mesh):
    rows = P(("pts", "fsdp"), None)
    split = P(None, "fsdp", None)
    in_specs = (rows,) * 4 + (split,) * 8 + (P(),) * 8
    out_specs = (rows, rows, P()) + (split,) * 10 + (P(),) * 10
    return jax.shard_map(
        functools.partial(body, mesh.shape["pts"] // 2),
        mesh=mesh, in_specs=in_specs, out_specs=out_specs, check_vma=False,
    )
```

```python
import functools
import math

import jax
import jax.numpy as jnp
from jax import lax
from jax.experimental import pallas as pl
from jax.experimental.pallas import tpu as pltpu
from jax.sharding import PartitionSpec as P

C = 256
H = 8
DH = 32
G = 64
FF = 1024
ITEMS = 16
STEP = 5
W = 256
T = 128
BATCH = 8
NORM_EPS = 1e-05
SLICE_EPS = 1e-05
CLIP = 1.0
BETA_ONE = 0.5
BETA_TWO = 0.5
ADAM_EPS = 1e-08
DECAY = 0.01
EMA_RATE = 0.6
RATE_ATTN = 0.04
RATE_MLP = 0.03
RATE_SMALL = 0.4
RATE_VECTOR = 0.3
ZO = 4
UN = 48
CB = 144
CL = 32
SM = 80
MESH = pl.DeviceIdType.MESH
HIGH = lax.Precision.HIGHEST
F32 = jnp.float32
BF = jnp.bfloat16
GELU_A = math.sqrt(2.0 / math.pi)
GELU_B = GELU_A * 0.044715


def nn(a, b, precision=None):
    return lax.dot_general(a, b, (((1,), (0,)), ((), ())), precision=precision, preferred_element_type=F32)


def nt(a, b, precision=None):
    return lax.dot_general(a, b, (((1,), (1,)), ((), ())), precision=precision, preferred_element_type=F32)


def tn(a, b, precision=None):
    return lax.dot_general(a, b, (((0,), (0,)), ((), ())), precision=precision, preferred_element_type=F32)


def iota(shape, dim):
    return lax.broadcasted_iota(jnp.int32, shape, dim)


def tile_of(i, width=W):
    return pl.ds(pl.multiple_of(i * width, width), width)


class Place:
    def __init__(self, zs):
        self.p = lax.axis_index("pts")
        self.f = lax.axis_index("fsdp")
        self.a = self.f % 2
        self.x = self.f // 2
        self.y = self.p % 2
        self.z = self.p // 2
        self.m = self.x * 2 + self.y
        self.zs = zs
        self.core = (self.p, self.f + 1 - 2 * self.a)
        self.xpeer = (self.p, (1 - self.x) * 2 + self.a)
        self.ypeer = (self.z * 2 + 1 - self.y, self.f)
        self.zown = self.z if zs == ZO else jnp.minimum(self.z, ZO - 1)

    def xy(self, k):
        mm = (self.m + k) % 4
        return mm, (self.z * 2 + mm % 2, (mm // 2) * 2 + self.a)

    def xy_other(self, k):
        mm = (self.m + k) % 4
        return mm, (self.z * 2 + mm % 2, (mm // 2) * 2 + 1 - self.a)

    def chips(self):
        return [(k, j) for j in range(self.zs - 1, -1, -1) for k in (3, 2, 1, 0) if k or j]

    def chip(self, k, j):
        mm, zz = (self.m + k) % 4, (self.z + j) % self.zs
        return mm, zz, (zz * 2 + mm % 2, (mm // 2) * 2 + self.a)

    def zl(self, k):
        zz = (self.z + k) % self.zs
        return zz, (zz * 2 + self.y, self.f)

    def barrier(self):
        b = pltpu.get_barrier_semaphore()
        peers = [self.core] + [self.chip(k, j)[2] for k, j in self.chips()]
        peers += [self.xy_other(k)[1] for k in (1, 2, 3)]
        for d in peers:
            pl.semaphore_signal(b, inc=1, device_id=d, device_id_type=MESH)
        pl.semaphore_wait(b, len(peers))

    def owned(self, z, fn):
        if self.zs == ZO:
            fn()
        else:
            pl.when(z < ZO)(fn)


def rcopy(src, dst, ss, rs, dev):
    return pltpu.make_async_remote_copy(
        src_ref=src, dst_ref=dst, send_sem=ss, recv_sem=rs, device_id=dev, device_id_type=MESH
    )


class Reduce:
    def __init__(self, g, src, bufs):
        self.g, self.src = g, src
        self.r1, self.s2, self.r2, self.s3, self.r3, self.sem = bufs
        self.c1, self.c2, self.c3 = {}, [], []

    @staticmethod
    def scratch(rows, zs):
        return [
            pltpu.VMEM((4, ZO, rows, 128), BF),
            pltpu.VMEM((3, ZO, rows, 128), BF),
            pltpu.VMEM((3, ZO, rows, 128), BF),
            pltpu.VMEM((ZO, rows, 128), BF),
            pltpu.VMEM((zs - 1, rows, 128), BF),
            pltpu.SemaphoreType.DMA((6, max(zs, 4))),
        ]

    def core(self, k):
        g = self.g
        mm = (g.m + k) % 4
        c = rcopy(self.src.at[1 - g.a, mm], self.r1.at[mm], self.sem.at[0, k], self.sem.at[1, k], g.core)
        c.start()
        self.c1[k] = c

    def pair(self, k):
        g = self.g
        self.c1[k].wait_recv()
        mm = (g.m + k) % 4
        return self.src[g.a, mm].astype(F32) + self.r1[mm].astype(F32)

    def square(self, k):
        g = self.g
        dev = g.xy(k)[1]
        self.s2[k - 1] = self.pair(k).astype(BF)
        c = rcopy(self.s2.at[k - 1], self.r2.at[k - 1], self.sem.at[2, k - 1], self.sem.at[3, k - 1], dev)
        c.start()
        self.c2.append(c)

    def line(self):
        g = self.g
        acc = self.pair(0)
        for k in (1, 2, 3):
            self.c2[k - 1].wait_recv()
            acc = acc + self.r2[k - 1].astype(F32)
        self.s3[...] = acc.astype(BF)
        for k in range(1, g.zs):
            zz, dev = g.zl(k)
            at = zz if g.zs == ZO else jnp.minimum(zz, ZO - 1)
            c = rcopy(self.s3.at[at], self.r3.at[k - 1], self.sem.at[4, k - 1], self.sem.at[5, k - 1], dev)
            g.owned(zz, c.start)
            self.c3.append(c)

    def result(self):
        g = self.g
        out = self.s3[g.zown].astype(F32)
        for k in range(1, g.zs):
            g.owned(g.z, self.c3[k - 1].wait_recv)
            out = out + self.r3[k - 1].astype(F32)
        return out

    def finish(self):
        g = self.g
        for c in self.c1.values():
            c.wait_send()
        for c in self.c2:
            c.wait_send()
        for k in range(1, g.zs):
            g.owned(g.zl(k)[0], self.c3[k - 1].wait_send)


class Direct:
    def __init__(self, g, src, bufs):
        self.g, self.src = g, src
        self.r1, self.s2, self.r2, self.core_sem, self.chip_sem = bufs
        self.c1, self.c2 = {}, {}

    @staticmethod
    def scratch(rows, zs):
        return [
            pltpu.VMEM((4, ZO, rows, 128), BF),
            pltpu.VMEM((4, ZO, rows, 128), BF),
            pltpu.VMEM((4, zs, rows, 128), BF),
            pltpu.SemaphoreType.DMA((2, 4)),
            pltpu.SemaphoreType.DMA((2, 4, zs)),
        ]

    def core(self, k):
        g = self.g
        mm = (g.m + k) % 4
        c = rcopy(self.src.at[1 - g.a, mm], self.r1.at[mm], self.core_sem.at[0, k], self.core_sem.at[1, k], g.core)
        c.start()
        self.c1[k] = c

    def chips(self):
        g = self.g
        for k in (3, 2, 1, 0):
            self.c1[k].wait_recv()
            mm = (g.m + k) % 4
            self.s2[k] = (self.src[g.a, mm].astype(F32) + self.r1[mm].astype(F32)).astype(BF)
        for k, j in g.chips():
            _, zz, dev = g.chip(k, j)
            at = zz if g.zs == ZO else jnp.minimum(zz, ZO - 1)
            c = rcopy(self.s2.at[k, at], self.r2.at[k, j], self.chip_sem.at[0, k, j], self.chip_sem.at[1, k, j], dev)
            g.owned(zz, c.start)
            self.c2[k, j] = (zz, c)

    def result(self):
        g = self.g
        out = self.s2[0, g.zown].astype(F32)
        for k, j in reversed(g.chips()):
            g.owned(g.z, self.c2[k, j][1].wait_recv)
            out = out + self.r2[k, j].astype(F32)
        return out

    def finish(self):
        for c in self.c1.values():
            c.wait_send()
        for zz, c in self.c2.values():
            self.g.owned(zz, c.wait_send)


class Gather:
    def __init__(self, g, out, bufs):
        self.g, self.out = g, out
        self.chip_sem, self.core_sem = bufs
        self.cz, self.cc = {}, []

    @staticmethod
    def scratch(zs):
        return [pltpu.SemaphoreType.DMA((2, 4, zs)), pltpu.SemaphoreType.DMA((2, 4))]

    def start(self):
        g = self.g
        own = self.out.at[g.a, g.m, g.zown]
        for k, j in g.chips():
            c = rcopy(own, own, self.chip_sem.at[0, k, j], self.chip_sem.at[1, k, j], g.chip(k, j)[2])
            g.owned(g.z, c.start)
            self.cz[k, j] = c

    def to_core(self):
        g = self.g
        for k in range(4):
            for j in range(g.zs):
                if k or j:
                    g.owned((g.z - j + g.zs) % g.zs, self.cz[k, j].wait_recv)
            r = self.out.at[g.a, (g.m - k + 4) % 4]
            c = rcopy(r, r, self.core_sem.at[0, k], self.core_sem.at[1, k], g.core)
            c.start()
            self.cc.append(c)

    def done(self):
        for c in self.cc:
            c.wait_recv()

    def finish(self):
        g = self.g
        for c in self.cz.values():
            g.owned(g.z, c.wait_send)
        for c in self.cc:
            c.wait_send()


def counts(surface, volume):
    at = surface[0, 0] * 0
    starts, surfs, sizes = [], [], []
    for b in range(ITEMS):
        starts.append(at)
        surfs.append(surface[0, b])
        sizes.append(surface[0, b] + volume[0, b])
        at = at + sizes[b]
    return starts, surfs, sizes, at


def column(row):
    return jnp.broadcast_to(row, (128, row.shape[1])).T


def wide(col):
    return jnp.concatenate([col, col], axis=1)


def norm_stats(v):
    mean = jnp.mean(v, axis=0, keepdims=True)
    centred = v - mean
    var = jnp.mean(centred * centred, axis=0, keepdims=True)
    scale = lax.rsqrt(var + NORM_EPS)
    return centred * scale, scale


def halves():
    lane = iota((1, 128), 1)
    return (lane < G).astype(F32).astype(BF), (lane >= G).astype(F32).astype(BF)


def spread_unit(unit):
    low, high = halves()
    return jnp.concatenate([unit * low, unit * high], axis=0)


def take_units(full):
    low = iota((DH, 128), 1) < G
    one = jnp.where(low, full[0:DH, 0:128], full[DH : 2 * DH, 0:128])
    two = jnp.where(low, full[2 * DH : 3 * DH, 128:256], full[3 * DH : 4 * DH, 128:256])
    return one, two


def item_units(fields, probs):
    left = jnp.concatenate([fields, jnp.ones((16, T), BF)], axis=0)
    full = nt(left, probs)
    one, two = take_units(full)
    one = jnp.concatenate([one, full[128:144, 0:128]], axis=0)
    two = jnp.concatenate([two, full[128:144, 128:256]], axis=0)
    return one.astype(BF), two.astype(BF)


def slice_columns(small):
    low = small[:, 0:128].astype(BF)
    pick = (iota((H * G, 128), 0) % G == iota((H * G, 128), 1)).astype(F32).astype(BF)
    rows = nt(pick, low).astype(BF)
    place = (iota((DH, C), 1) % DH == iota((DH, C), 0)).astype(F32).astype(BF)
    full = nn(rows, place)
    keep = iota((H * G, C), 0) // G == iota((H * G, C), 1) // DH
    return jnp.where(keep, full, 0.0).astype(BF)


def same_head():
    return iota((2 * G, 2 * G), 0) // G == iota((2 * G, 2 * G), 1) // G


def main_kernel(
    zs, surface, volume, points_hbm, cot_hbm, attn_w, mlp_w, small, vector,
    mixed_hbm, grad_hbm, big, late, small_sum, norm_out, points, cotangent, mixed, points_grad, load_sem,
    bounds, surf, keep, xt, cot_t, normed, mid, probs, spread, norm_two, active, d_hidden, d_branch, d_spread, d_mid,
    d_both, d_logits, wat, wml, wxf, slicew, slicet, wot, wint, woutt, gain_one, gain_two, embed_acc,
    src, src_big, src_late, slice_out, d_slice, saved, attention, maps_acc,
    small_src, sr1, sr2, sr3, line_late, sqb, weight_sem, big_sem, y_sem, sem, sq_sem, *sems,
):
    g = Place(zs)
    rows = ITEMS * T
    red = [Direct(g, src.at[i], sems[3 * i : 3 * i + 3] + sems[12 + 2 * (i % 2) : 14 + 2 * (i % 2)]) for i in range(4)]
    red_big = Reduce(g, src_big, sems[16:22])
    red_late = Reduce(g, src_late, sems[22:28])
    gat = [Gather(g, slice_out.at[i], sems[28 + 2 * i : 30 + 2 * i]) for i in range(2)]
    gat += [Gather(g, d_slice.at[i], sems[28 + 2 * i : 30 + 2 * i]) for i in range(2)]

    own = pl.ds(pl.multiple_of(g.f * 64, 64), 64)
    other = pl.ds(pl.multiple_of(((1 - g.x) * 2 + g.a) * 64, 64), 64)
    wat[:, own, :] = attn_w[...].astype(BF)
    load_points = pltpu.make_async_copy(points_hbm, points, load_sem.at[0])
    load_cot = pltpu.make_async_copy(cot_hbm, cotangent, load_sem.at[1])
    load_points.start()
    g.barrier()

    def weight(ref, lead, at, i, dev):
        r = ref.at[lead, at, :]
        return rcopy(r, r, weight_sem.at[0, i], weight_sem.at[1, i], dev)

    two, three, all_mlp = pl.ds(0, 2), pl.ds(2, 1), pl.ds(0, 2)
    a_x, a_c, a_f = weight(wat, two, own, 0, g.xpeer), weight(wat, two, own, 1, g.core), weight(wat, two, other, 2, g.core)
    o_x, o_c, o_f = weight(wat, three, own, 3, g.xpeer), weight(wat, three, own, 4, g.core), weight(wat, three, other, 5, g.core)
    m_x, m_c, m_f = weight(wml, all_mlp, own, 6, g.xpeer), weight(wml, all_mlp, own, 7, g.core), weight(wml, all_mlp, other, 8, g.core)
    a_x.start()
    a_c.start()
    load_cot.start()
    wml[:, own, :] = mlp_w[...].astype(BF)
    load_points.wait()

    starts, surfs, sizes, total = counts(surface, volume)
    lane = iota((1, T), 1)
    for b in range(ITEMS):
        shift = total + b * T - starts[b] - sizes[b]
        bounds[0, b] = starts[b]
        bounds[1, b] = sizes[b]
        bounds[2, b] = shift
        bounds[3, b] = jnp.minimum(lax.div(starts[b], jnp.int32(T)), ITEMS - 2)
        bounds[4, b] = jnp.minimum(lax.div(shift, jnp.int32(T)), ITEMS - 2)
        surf[:, b * T : b * T + T] = (lane < surfs[b]).astype(F32)
        keep[:, b * T : b * T + T] = (lane < sizes[b]).astype(F32)
    gain_a = column(vector[0:1, :])
    gain_b = wide(column(vector[1:2, :]))
    embed = column(vector[2:3, :])
    embed2 = wide(embed)

    def packed(ref, b):
        t, u, size = bounds[3, b], bounds[4, b], bounds[1, b]
        to, row = iota((T, 2 * T), 0), iota((T, 2 * T), 1)
        one = (row + t * T == to + bounds[0, b]) & (to < size)
        two = (row + u * T == to + bounds[2, b]) & (to >= size)
        pick = jnp.concatenate([one.astype(F32).astype(BF), two.astype(F32).astype(BF)], axis=1)
        return nn(pick, jnp.concatenate([ref[i] for i in (t, t + 1, u, u + 1)], axis=0)).T

    def pack_item(b, carry):
        at = tile_of(b, T)
        field = packed(points, b)
        xt[:, at] = field.astype(BF)
        unit, _ = norm_stats(field + embed * surf[:, at])
        normed[:, at] = (unit * gain_a).astype(BF)
        return carry

    def pack_cot(b, carry):
        cot_t[:, tile_of(b, T)] = packed(cotangent, b).astype(BF)
        return carry

    lax.fori_loop(0, ITEMS, pack_item, 0, unroll=8)
    a_x.wait_recv()
    a_f.start()
    for c in (m_x, o_x, m_c, o_c):
        c.start()
    slicew[...] = slice_columns(small)
    for r in (gain_one, gain_two, embed_acc, maps_acc):
        r[...] = jnp.zeros_like(r)

    def turned(v):
        return v.astype(F32).T.astype(BF)

    a_c.wait_recv()
    a_f.wait_recv()
    wxf[0:C, :] = turned(wat[0])
    wxf[C : 2 * C, :] = turned(wat[1])

    def soft_tile(i, carry):
        at = tile_of(i)
        both = nn(wxf[...], normed[:, at]).astype(BF)
        mid[:, at] = both
        logits = nn(slicew[...], both[0:C]).reshape(H, G, W)
        top = jnp.max(logits, axis=1, keepdims=True)
        e = jnp.exp(logits - top)
        scale = keep[:, at] / jnp.sum(e, axis=1, keepdims=True)
        probs[:, at] = (e * scale).reshape(H * G, W).astype(BF)
        return carry

    def sums(r, batch, fields, off):
        for half in range(2):
            for k in (1, 2, 3, 0):
                mm = (g.m + k) % 4
                core = (1 - g.a) if half == 0 else g.a
                at = tile_of(batch * BATCH + core * 4 + mm, T)
                for q in range(2):
                    both = item_units(fields[off + q * 128 : off + q * 128 + 128, at], probs[q * 256 : q * 256 + 256, at])
                    for i in range(2):
                        r.src[core, mm, 2 * q + i] = both[i]
                if half == 0:
                    r.core(k)

    def attend(batch):
        unit = red[batch].result()
        raw, scale = unit[0:DH], unit[DH : DH + 8] + SLICE_EPS
        token = raw / scale[0:1]
        qkv = tn(small[...], token, HIGH)
        query, key, value = qkv[64:96], qkv[96:128], qkv[128:160]
        scores = tn(key, query, HIGH) / math.sqrt(DH)
        scores = jnp.where(same_head(), scores, -jnp.inf)
        top = jnp.max(scores, axis=0, keepdims=True)
        e = jnp.exp(scores - top)
        weights = e / jnp.sum(e, axis=0, keepdims=True)
        slice_out[batch, g.a, g.m, g.zown] = nn(value.astype(BF), weights.astype(BF)).astype(BF)
        gat[batch].start()
        saved[batch, 0:32] = token
        saved[batch, 32:128] = qkv[64:160]
        saved[batch, 128:160] = raw
        saved[batch, 160:168] = scale
        attention[batch] = weights

    def attend_back(batch):
        unit = red[2 + batch].result()
        d_out = unit[0:DH]
        s = saved.at[batch]
        token, query, key, value = s[0:32], s[32:64], s[64:96], s[96:128]
        raw, scale = s[128:160], s[160:161]
        weights = attention[batch]
        low = weights.astype(BF)
        d_low, query, key, value = [v.astype(BF) for v in (d_out, query, key, value)]
        d_value = nt(d_low, low)
        d_weights = tn(value, d_low)
        d_scores = weights * (d_weights - jnp.sum(weights * d_weights, axis=0, keepdims=True))
        d_scores = (d_scores / math.sqrt(DH)).astype(BF)
        d_query = nn(key, d_scores)
        d_key = nt(query, d_scores)
        d_maps = jnp.concatenate([jnp.zeros((64, T), F32), d_query, d_key, d_value], axis=0).astype(BF)
        d_token = nn(small[...].astype(BF), d_maps)
        d_total = -jnp.sum(d_token * raw, axis=0, keepdims=True) / (scale * scale)
        tot = jnp.broadcast_to(d_total, (16, T))
        d_slice[batch, g.a, g.m, g.zown] = jnp.concatenate([d_token / scale, tot], axis=0).astype(BF)
        gat[2 + batch].start()
        part = nt(token.astype(BF), jnp.concatenate([d_maps, jnp.zeros((96, T), BF)], axis=0))
        if zs != ZO:
            part = jnp.where(g.z < ZO, part, 0.0)
        maps_acc[...] += part

    lax.fori_loop(0, 4, soft_tile, 0, unroll=2)
    sums(red[0], 0, mid, C)
    lax.fori_loop(4, 6, soft_tile, 0, unroll=2)
    red[0].chips()
    lax.fori_loop(6, 8, soft_tile, 0, unroll=2)
    sums(red[1], 1, mid, C)
    red[1].chips()
    m_x.wait_recv()
    m_f.start()
    o_x.wait_recv()
    o_f.start()
    load_cot.wait()
    slicet[...] = turned(slicew[...])
    attend(0)
    for c in (m_c, o_c, m_f, o_f):
        c.wait_recv()
    wot[...] = turned(wat[2])
    for j in range(FF // 256):
        wint[j * 256 : j * 256 + 256, :] = turned(wml[0, :, j * 256 : j * 256 + 256])
    attend(1)
    for j in range(FF // 256):
        woutt[j * 256 : j * 256 + 256, :] = turned(wml[1, :, j * 256 : j * 256 + 256])
    gat[0].to_core()
    lax.fori_loop(0, ITEMS, pack_cot, 0, unroll=4)
    gat[0].done()

    def spread_item(b, carry):
        at = tile_of(b, T)
        batch = b // BATCH
        core = (b % BATCH) // 4
        for i in range(4):
            part = nn(spread_unit(slice_out[batch, core, b % 4, i]), probs[i * 128 : i * 128 + 128, at])
            spread[i * 64 : i * 64 + 64, at] = part.astype(BF)
        return carry

    def mlp_tile(i, carry):
        at = tile_of(i)
        middle = xt[:, at].astype(F32) + embed2 * surf[:, at] + nn(wot[...], spread[:, at])
        unit, scale = norm_stats(middle)
        two = (unit * gain_b).astype(BF)
        norm_two[:, at] = two
        ctb = cot_t[:, at]
        for j in range(FF // 256):
            hid = pl.ds(j * 256, 256)
            x = nn(wint[hid, :], two)
            da = nn(woutt[hid, :], ctb)
            sq = x * x
            t = jnp.tanh(x * (GELU_A + GELU_B * sq))
            s = 0.5 + 0.5 * t
            act = (x * s).astype(BF)
            slope = s + (x * (s - s * s)) * (2.0 * GELU_A + 6.0 * GELU_B * sq)
            dh = (slope * da).astype(BF)
            active[hid, at] = act
            d_hidden[hid, at] = dh
        d_two = nn(wml[0], d_hidden[:, at])
        mixed[at, :] = (middle + nn(wml[1], active[:, at])).T.astype(BF)
        gs = d_two * unit
        gain_two[...] += gs[:, 0:128] + gs[:, 128:256]
        du = d_two * gain_b
        m1 = jnp.mean(du, axis=0, keepdims=True)
        m2 = jnp.mean(du * unit, axis=0, keepdims=True)
        dm = ctb.astype(F32) + scale * (du - m1 - unit * m2)
        d_mid[:, at] = dm
        db = dm.astype(BF)
        d_branch[:, at] = db
        d_spread[:, at] = nn(wat[2], db).astype(BF)
        return carry

    lax.fori_loop(0, BATCH, spread_item, 0, unroll=8)
    gat[1].to_core()
    lax.fori_loop(0, 2, mlp_tile, 0, unroll=2)
    lax.fori_loop(2, 4, mlp_tile, 0, unroll=2)
    red[0].finish()
    sums(red[2], 0, d_spread, 0)
    gat[1].done()
    red[1].finish()
    lax.fori_loop(BATCH, ITEMS, spread_item, 0, unroll=8)
    red[2].chips()
    lax.fori_loop(4, 6, mlp_tile, 0, unroll=2)
    lax.fori_loop(6, 8, mlp_tile, 0, unroll=2)
    gat[0].finish()
    gat[1].finish()
    attend_back(0)
    sums(red[3], 1, d_spread, 0)
    stores = [pltpu.make_async_copy(mixed, mixed_hbm, load_sem.at[2])]
    stores[0].start()

    def put(f, p, lo, value):
        src_big[f % 2, (f // 2) * 2 + p % 2, p // 2, lo : lo + value.shape[0], :] = value

    def grad_mlp(which, left, right):
        for j in range(FF // 256):
            grad = nt(left[...], right[j * 256 : j * 256 + 256, :]).astype(BF)
            for f in range(4):
                for i in range(2):
                    put(f, 2 * j + i, which * 64, grad[f * 64 : f * 64 + 64, i * 128 : i * 128 + 128])

    grad_mlp(0, norm_two, d_hidden)
    red[3].chips()
    grad_mlp(1, cot_t, active)
    gat[2].to_core()
    grad = nt(spread[...], d_branch[...]).astype(BF)
    for f in range(4):
        for p in range(8):
            lo = f * 64 + (p % 4) * 16
            put(f, p, 128, grad[lo : lo + 16, (p // 4) * 128 : (p // 4) * 128 + 128])
    for k in (1, 2, 3, 0):
        red_big.core(k)
    gat[2].done()
    block = iota((1, 2 * T), 1)
    block = jnp.where(block < T, block // DH % 2, jnp.where(block == T, 0, jnp.where(block == T + 16, 1, 2)))
    even, odd = [(block == i).astype(F32).astype(BF) for i in range(2)]
    ones_rows = jnp.ones((T, T), BF)
    blank = jnp.zeros((T - 32, T), BF)

    def back_item(b, carry):
        at = tile_of(b, T)
        batch = b // BATCH
        core = (b % BATCH) // 4
        for q in range(2):
            outs = [slice_out[batch, core, b % 4, 2 * q + i] for i in range(2)]
            ds = [d_slice[batch, core, b % 4, 2 * q + i] for i in range(2)]
            parts = outs + [d[0:DH] for d in ds] + [d[DH:UN] for d in ds] + [blank]
            turn = jnp.concatenate(parts, axis=0).T
            for one in range(2):
                rows_of = [4 * q + one, 4 * q + 2 + one]
                left = turn[one * G : one * G + G]
                left = jnp.concatenate([left * even, left * odd], axis=0)
                fields = [d_spread[h * DH : h * DH + DH, at] for h in rows_of]
                fields += [mid[C + h * DH : C + h * DH + DH, at] for h in rows_of]
                dp = nn(left, jnp.concatenate(fields + [ones_rows], axis=0)).reshape(2, G, T)
                pf = jnp.stack([probs[h * G : h * G + G, at] for h in rows_of]).astype(F32)
                back = pf * (dp - jnp.sum(pf * dp, axis=1, keepdims=True))
                for i, h in enumerate(rows_of):
                    d_logits[h * G : h * G + G, at] = back[i].astype(BF)
            for i in range(2):
                k = 2 * q + i
                part = nn(spread_unit(ds[i][0:DH]), probs[k * 128 : k * 128 + 128, at])
                d_both[C + k * 64 : C + k * 64 + 64, at] = part.astype(BF)
        return carry

    def back_tile(i, carry):
        at = tile_of(i)
        d_norm = nn(wat[0], d_both[0:C, at]) + nn(wat[1], d_both[C : 2 * C, at])
        sf = surf[:, at]
        unit, scale = norm_stats(xt[:, at].astype(F32) + embed2 * sf)
        gs = d_norm * unit
        gain_one[...] += gs[:, 0:128] + gs[:, 128:256]
        du = d_norm * wide(gain_a)
        m1 = jnp.mean(du, axis=0, keepdims=True)
        m2 = jnp.mean(du * unit, axis=0, keepdims=True)
        pg = d_mid[:, at] + scale * (du - m1 - unit * m2)
        es = pg * sf
        embed_acc[...] += es[:, 0:128] + es[:, 128:256]
        points_grad[at, :] = pg.T
        return carry

    def mid_tile(i, carry):
        at = tile_of(i)
        d_both[0:C, at] = nn(slicet[...], d_logits[:, at]).astype(BF)
        return carry

    lax.fori_loop(0, 4, back_item, 0, unroll=4)
    attend_back(1)
    lax.fori_loop(4, BATCH, back_item, 0, unroll=4)
    for k in (1, 2, 3):
        red_big.square(k)
    lax.fori_loop(0, 4, mid_tile, 0, unroll=4)
    lax.fori_loop(0, 4, back_tile, 0, unroll=4)
    gat[3].to_core()
    half_rows = [pl.ds(0, rows // 2), pl.ds(rows // 2, rows // 2)]

    def store_half(i):
        c = pltpu.make_async_copy(points_grad.at[half_rows[i], :], grad_hbm.at[half_rows[i], :], load_sem.at[3 + i])
        c.start()
        stores.append(c)

    store_half(0)
    def copies(ref):
        part = ref.at[g.zown, g.y]
        out = []
        for j in range(zs - 1, -1, -1):
            zz = (g.z + j) % zs
            for i in range(2):
                if i or j:
                    dev = (zz * 2 + (1 - g.y if i else g.y), g.f)
                    c = rcopy(part, part, big_sem.at[0, i, j], big_sem.at[1, i, j], dev)
                    g.owned(g.z, c.start)
                    out.append(((g.z - j + zs) % zs, c))
        return out

    def to_y(ref, sem):
        cy = []
        for z in range(ZO):
            r = ref.at[z, g.y]
            c = rcopy(r, r, sem.at[0, z], sem.at[1, z], g.ypeer)
            c.start()
            cy.append(c)
        return cy

    gat[3].done()
    lax.fori_loop(BATCH, BATCH + 4, back_item, 0, unroll=4)
    red_big.line()
    lax.fori_loop(BATCH + 4, ITEMS, back_item, 0, unroll=4)
    lax.fori_loop(4, 8, mid_tile, 0, unroll=4)

    grads = [nt(normed[...], d_both[i * C : i * C + C, :]).astype(BF) for i in range(2)]
    for f in range(4):
        for p in range(8):
            lo, col = f * 64 + (p % 4) * 16, (p // 4) * 128
            both = [v[lo : lo + 16, col : col + 128] for v in grads]
            src_late[f % 2, (f // 2) * 2 + p % 2, p // 2] = jnp.concatenate(both, axis=0)
    for k in (1, 2, 3, 0):
        red_late.core(k)
    fold = jnp.zeros((DH, 128), F32)
    for i in range(4):
        part = nt(mid[i * 64 : i * 64 + 64, :], d_logits[i * 128 : i * 128 + 128, :])
        fold = fold + jnp.where(iota((DH, 128), 1) < G, part[0:DH], part[DH : 2 * DH])
    fold = jnp.where(iota((32, 128), 1) < G, fold + pltpu.roll(fold, G, 1), 0.0)
    big[g.zown, g.y] = red_big.result().astype(BF)
    big_c = copies(big)
    for k in (1, 2, 3):
        red_late.square(k)
    lax.fori_loop(4, 8, back_tile, 0, unroll=4)
    store_half(1)

    ones = jnp.ones((8, 128), F32)
    line = [nt(ones, r[...], HIGH) for r in (gain_one, gain_two, embed_acc)]
    pick = iota((8, 256), 0)
    vec = jnp.where(pick == 0, line[0], jnp.where(pick == 1, line[1], jnp.where(pick == 2, line[2], 0.0)))
    small_src[0:32] = (fold + maps_acc[:, 0:128]).astype(BF)
    small_src[32:64] = maps_acc[:, 128:256].astype(BF)
    small_src[64:80] = jnp.concatenate([vec[:, 0:128], vec[:, 128:256]], axis=0).astype(BF)
    cs = [rcopy(small_src, sr1, sem.at[0, 0], sem.at[1, 0], g.core)]
    cs[0].start()

    acc = red_late.pair(0)
    for k in (1, 2, 3):
        red_late.c2[k - 1].wait_recv()
        acc = acc + red_late.r2[k - 1].astype(F32)
    line_late[g.z] = acc.astype(BF)
    line_copies = []
    for k in range(1, zs):
        c = rcopy(line_late.at[g.z], line_late.at[g.z], sem.at[4, k], sem.at[5, k], g.zl(k)[1])
        c.start()
        line_copies.append(c)
    cs[0].wait_recv()
    sr2[g.m] = (small_src[...].astype(F32) + sr1[...].astype(F32)).astype(BF)
    for k in (1, 2, 3):
        c = rcopy(sr2.at[g.m], sr2.at[g.m], sem.at[0, k], sem.at[1, k], g.xy(k)[1])
        c.start()
        cs.append(c)
    for z, c in big_c:
        g.owned(z, c.wait_recv)
    bigs = big[:, g.y].astype(F32).reshape(ZO * CB // 8, 8, 128)
    squares = jnp.sum(bigs * bigs, axis=0)
    for c in line_copies:
        c.wait_recv()
    acc = line_late[0].astype(F32)
    for z in range(1, zs):
        acc = acc + line_late[z].astype(F32)
    acc = acc.astype(BF)
    late[:, g.y] = acc
    mine = acc.astype(F32).reshape(ZO * CL // 8, 8, 128)
    here = g.a * 4 + g.m
    sqb[here] = squares + jnp.sum(mine * mine, axis=0)
    sq_copies = []
    for k in range(1, 8):
        dev = g.core if k == 4 else g.xy(k)[1] if k < 4 else g.xy_other(k - 4)[1]
        c = rcopy(sqb.at[here], sqb.at[here], sq_sem.at[0, k], sq_sem.at[1, k], dev)
        c.start()
        sq_copies.append(c)
    late_y = to_y(late, y_sem)
    for c in cs[1:4]:
        c.wait_recv()
    total = sr2[0].astype(F32)
    for m in range(1, 4):
        total = total + sr2[m].astype(F32)
    sr3[g.z] = total.astype(BF)
    for k in range(1, zs):
        c = rcopy(sr3.at[g.z], sr3.at[g.z], sem.at[2, k], sem.at[3, k], g.zl(k)[1])
        c.start()
        cs.append(c)
    for c in late_y + cs[4:]:
        c.wait_recv()
    total = sr3[0].astype(F32)
    for z in range(1, zs):
        total = total + sr3[z].astype(F32)
    small_sum[...] = total
    for c in sq_copies:
        c.wait_recv()
    sq = sqb[0]
    for i in range(1, 8):
        sq = sq + sqb[i]
    norm_out[0, 0] = jnp.sqrt(jnp.sum(sq) + jnp.sum(total * total))

    for c in cs + line_copies + sq_copies + late_y + [a_x, a_c, a_f, o_x, o_c, o_f, m_x, m_c, m_f]:
        c.wait_send()
    for c in stores:
        c.wait()
    for _, c in big_c:
        g.owned(g.z, c.wait_send)
    for c in red_late.c1.values():
        c.wait_send()
    for c in red_late.c2:
        c.wait_send()
    for r in red[2:] + [red_big] + gat[2:]:
        r.finish()


def adamw(state, new, sl, grad, factor, rate):
    weight, first, second, average = [r[sl] for r in state]
    clipped = grad * factor
    first_new = BETA_ONE * first + (1.0 - BETA_ONE) * clipped
    second_new = BETA_TWO * second + (1.0 - BETA_TWO) * clipped * clipped
    first_hat = first_new / (1.0 - BETA_ONE**STEP)
    second_hat = second_new / (1.0 - BETA_TWO**STEP)
    new_weight = weight - rate * (first_hat / (jnp.sqrt(second_hat) + ADAM_EPS) + DECAY * weight)
    average_new = EMA_RATE * average + (1.0 - EMA_RATE) * new_weight
    for r, v in zip(new, (new_weight, first_new, second_new, average_new, new_weight.astype(BF))):
        r[sl] = v


def last_kernel(surface, volume, norm, mixed_p, grad_p, big, late, small_sum, *refs):
    hbm_states, hbm_outs = refs[0:16], refs[16:38]
    states, news = refs[38:54], refs[54:74]
    rows_in, mixed_in, mixed_rows, mixed_low, grad_rows, in_sem, out_sem = refs[74:]
    rows = mixed_low.shape[0]
    ins = [pltpu.make_async_copy(h, v, in_sem.at[i]) for i, (h, v) in enumerate(zip(hbm_states, states))]
    gp = pltpu.make_async_copy(grad_p, rows_in, in_sem.at[16])
    mp = pltpu.make_async_copy(mixed_p, mixed_in, in_sem.at[17])
    for c in ins[4:8] + ins[0:4] + ins[8:] + [gp, mp]:
        c.start()
    starts, _, sizes, total = counts(surface, volume)

    row = iota((T + 8, 1), 0)
    sub = iota((1, 8, 1), 1)

    def place(source, out):
        def moved(b, base):
            first = pl.multiple_of(lax.div(base, jnp.int32(8)) * 8, 8)
            off = base - first
            turn = pltpu.roll(source[b * T : b * T + T, :].astype(F32).reshape(T // 8, 8, C), off, 1)
            later = jnp.where(sub >= off, turn[1:], turn[:-1])
            return first, off, jnp.concatenate([turn[0:1], later, turn[-1:]], axis=0).reshape(T + 8, C)

        for b in range(ITEMS):
            first, off, tile = moved(b, starts[b])
            head = pl.ds(first, 8)
            out[head, :] = jnp.where(row[0:8] >= off, tile[0:8], out[head, :])
            out[pl.ds(pl.multiple_of(first + 8, 8), T), :] = tile[8:]
        for b in range(ITEMS):
            first, off, tile = moved(b, total + b * T - starts[b] - sizes[b])
            here = pl.ds(first, T + 8)
            out[here, :] = jnp.where(row >= sizes[b] + off, tile, out[here, :])

    outs = []
    attn, mlp, small_s, vector_s = [states[4 * i : 4 * i + 4] for i in range(4)]
    attn_new, mlp_new, small_new, vector_new = [news[5 * i : 5 * i + 5] for i in range(4)]
    factor = jnp.minimum(1.0, CLIP / norm[0, 0])
    everything = slice(None)
    both = (everything, everything)
    for c in ins[4:8]:
        c.wait()
    for z in range(ZO):
        for y in range(2):
            p = z * 2 + y
            for i in range(2):
                grad = big[z, y, i * 64 : i * 64 + 64, :].astype(F32)
                adamw(mlp, mlp_new, (i, everything, slice(p * 128, p * 128 + 128)), grad, factor, RATE_MLP)

    def send(first, count):
        for i in range(first, first + count):
            c = pltpu.make_async_copy(news[i], hbm_outs[2 + i], out_sem.at[2 + i])
            c.start()
            outs.append(c)

    send(5, 5)
    for c in ins[0:4] + ins[8:]:
        c.wait()
    for z in range(ZO):
        for y in range(2):
            p = z * 2 + y
            lo, col = (p % 4) * 16, (p // 4) * 128
            at = (slice(lo, lo + 16), slice(col, col + 128))
            grad = big[z, y, 128:144, :].astype(F32)
            adamw(attn, attn_new, (2,) + at, grad, factor, RATE_ATTN)
            for i in range(2):
                grad = late[z, y, i * 16 : i * 16 + 16, :].astype(F32)
                adamw(attn, attn_new, (i,) + at, grad, factor, RATE_ATTN)
    send(0, 5)
    gsmall = jnp.concatenate([small_sum[0:32, :], small_sum[32:64, :]], axis=1)[:, 0:160]
    adamw(small_s, small_new, both, gsmall, factor, RATE_SMALL)
    gvec = jnp.concatenate([small_sum[64:72, :], small_sum[72:80, :]], axis=1)[0:3, :]
    adamw(vector_s, vector_new, both, gvec, factor, RATE_VECTOR)
    send(10, 10)
    gp.wait()
    place(rows_in, grad_rows)
    outs.append(pltpu.make_async_copy(grad_rows.at[pl.ds(0, rows), :], hbm_outs[1], out_sem.at[1]))
    outs[-1].start()
    mp.wait()
    place(mixed_in, mixed_rows)
    mixed_low[...] = mixed_rows[0:rows, :].astype(BF)
    outs.append(pltpu.make_async_copy(mixed_low, hbm_outs[0], out_sem.at[0]))
    outs[-1].start()
    for c in outs:
        c.wait()


def body(zs, points, cotangent, surface_count, volume_count, *state):
    attn, mlp, small, vector = [state[4 * i : 4 * i + 4] for i in range(4)]
    rows = points.shape[0]
    vmem = pl.BlockSpec(memory_space=pltpu.VMEM)
    smem = pl.BlockSpec(memory_space=pltpu.SMEM)
    hbm = pl.BlockSpec(memory_space=pl.ANY)
    sd = jax.ShapeDtypeStruct

    def tall(features, dtype=BF):
        return pltpu.VMEM((features, rows), dtype)

    def units(n, depth):
        return pltpu.VMEM((n, 2, 4, ZO, depth, 128), BF)

    scratch = [
        pltpu.VMEM((rows // T, T, C), BF), pltpu.VMEM((rows // T, T, C), BF), pltpu.VMEM((rows, C), BF),
        pltpu.VMEM((rows, C), F32), pltpu.SemaphoreType.DMA((5,)),
        pltpu.SMEM((5, ITEMS), jnp.int32), tall(1, F32), tall(1, F32),
        tall(C), tall(C), tall(C), tall(2 * C), tall(H * G), tall(C), tall(C), tall(FF), tall(FF), tall(C), tall(C),
        tall(C, F32), tall(2 * C), tall(H * G),
        pltpu.VMEM((3, C, C), BF), pltpu.VMEM((2, C, FF), BF), pltpu.VMEM((2 * C, C), BF),
        pltpu.VMEM((H * G, C), BF), pltpu.VMEM((C, H * G), BF), pltpu.VMEM((C, C), BF),
        pltpu.VMEM((FF, C), BF), pltpu.VMEM((FF, C), BF),
        pltpu.VMEM((C, 128), F32), pltpu.VMEM((C, 128), F32), pltpu.VMEM((C, 128), F32),
        units(4, UN), pltpu.VMEM((2, 4, ZO, CB, 128), BF), pltpu.VMEM((2, 4, ZO, CL, 128), BF),
        units(2, DH), units(2, UN), pltpu.VMEM((2, 168, 128), F32), pltpu.VMEM((2, 128, 128), F32),
        pltpu.VMEM((DH, 256), F32),
        pltpu.VMEM((SM, 128), BF), pltpu.VMEM((SM, 128), BF), pltpu.VMEM((4, SM, 128), BF), pltpu.VMEM((zs, SM, 128), BF),
        pltpu.VMEM((zs, ZO, CL, 128), BF), pltpu.VMEM((8, 8, 128), F32),
        pltpu.SemaphoreType.DMA((2, 9)), pltpu.SemaphoreType.DMA((2, 2, zs)), pltpu.SemaphoreType.DMA((2, ZO)),
        pltpu.SemaphoreType.DMA((6, max(zs, 4))), pltpu.SemaphoreType.DMA((2, 8)),
    ]
    for _ in range(4):
        scratch += Direct.scratch(UN, zs)[0:3]
    for _ in range(2):
        scratch += Direct.scratch(UN, zs)[3:5]
    for depth in (CB, CL):
        scratch += Reduce.scratch(depth, zs)
    for _ in range(2):
        scratch += Gather.scratch(zs)
    mixed_p, grad_p, big, late, small_sum, norm = pl.pallas_call(
        functools.partial(main_kernel, zs),
        out_shape=[
            sd((rows, C), BF), sd((rows, C), F32), sd((ZO, 2, CB, 128), BF), sd((ZO, 2, CL, 128), BF),
            sd((SM, 128), F32), sd((1, 1), F32),
        ],
        in_specs=[smem, smem, hbm, hbm] + [vmem] * 4,
        out_specs=[hbm, hbm] + [vmem] * 3 + [smem],
        scratch_shapes=scratch,
        compiler_params=pltpu.CompilerParams(collective_id=0, has_side_effects=True, vmem_limit_bytes=60 << 20),
        name="main",
    )(surface_count, volume_count, points.reshape(-1, T, C), cotangent.reshape(-1, T, C), attn[0], mlp[0], small[0], vector[0])

    def news(leaves):
        return [sd(leaves[0].shape, F32)] * 4 + [sd(leaves[0].shape, BF)]

    everything = news(attn) + news(mlp) + news(small) + news(vector)
    outs = pl.pallas_call(
        last_kernel,
        out_shape=[sd((rows, C), BF), sd((rows, C), F32)] + everything,
        in_specs=[smem, smem, smem, hbm, hbm, vmem, vmem, vmem] + [hbm] * 16,
        out_specs=[hbm] * 22,
        scratch_shapes=[pltpu.VMEM(v.shape, v.dtype) for v in state]
        + [pltpu.VMEM(v.shape, v.dtype) for v in everything]
        + [
            pltpu.VMEM((rows, C), F32), pltpu.VMEM((rows, C), BF), pltpu.VMEM((rows + T, C), F32), pltpu.VMEM((rows, C), BF),
            pltpu.VMEM((rows + T, C), F32), pltpu.SemaphoreType.DMA((18,)), pltpu.SemaphoreType.DMA((22,)),
        ],
        compiler_params=pltpu.CompilerParams(vmem_limit_bytes=60 << 20),
        name="last",
    )(surface_count, volume_count, norm, mixed_p, grad_p, big, late, small_sum, *state)
    return tuple(outs[0:2]) + (norm.reshape(()),) + tuple(outs[2:])


def solution(mesh):
    rows = P(("pts", "fsdp"), None)
    split = P(None, "fsdp", None)
    in_specs = (rows,) * 4 + (split,) * 8 + (P(),) * 8
    out_specs = (rows, rows, P()) + (split,) * 10 + (P(),) * 10
    return jax.shard_map(
        functools.partial(body, mesh.shape["pts"] // 2),
        mesh=mesh, in_specs=in_specs, out_specs=out_specs, check_vma=False,
    )
```
